256 devices in a mesh: grp: 64 (over y, x, z_lo), tp: 4 (over z_hi, core).
Axes of the slice: x: 4, y: 4, z: 8 (z_hi: 2, z_lo: 4; z = z_hi * 4 + z_lo), core: 2. Of those that a mesh axis runs over, the one named last changes fastest.
Arguments:
- x_rows: bfloat16 [1024, 7168], P('grp'), may hold values from -6 to 6
- route_ids: int32 [1024, 2], P('grp'), may hold values from 0 to 7, all different within a row; in each aligned block of 16 rows (0 to 15, 16 to 31, ...) at most 5 rows name the same one
- router: float32 [7168, 8], replicated, may hold values from -0.0625 to 0.0625
- w_gate: bfloat16 [7168, 40960], P(None, ('grp', 'tp')), may hold values from -0.0625 to 0.0625
- w_up: bfloat16 [7168, 40960], P(None, ('grp', 'tp')), may hold values from -0.0625 to 0.0625
- w_down: bfloat16 [40960, 7168], P(('grp', 'tp')), may hold values from -0.078125 to 0.078125
- queries: bfloat16 [1024, 16384], P(('grp', 'tp')), may hold values from -90 to 90
- cache: bfloat16 [1024, 1024, 512], P(('grp', 'tp')), may hold values from -5 to 5
- lengths: int32 [1024], P(('grp', 'tp')), may hold values from 2 to 1024, as said below
Outputs:
- moe_out: bfloat16 [1024, 7168], P('grp', 'tp')
- attn_out: bfloat16 [1024, 16384], P(('grp', 'tp'))
The draws below stay inside these ranges and needn't reach their ends.
Inputs may be any that keep to these rules, and one draw needn't show every extreme that they name: `route_ids`: in each aligned block of 16 rows (the rows of one index of grp) no expert is named by more than 5 rows, and some block has an expert named by exactly 5 rows; the ids of a row differ. `lengths`: some request has all 1024 positions live.
All inputs are finite; a program needn't handle non-finite values.
Results may differ from the reference program's by a relative error of at most 0.005.
Values may be sent and summed in bfloat16 or wider, within the bound.
No kernel may reach another device: no remote copies, remote signals or barrier semaphores. Data moves between devices by JAX's collectives and lax.ppermute only.
A program may use at most 128 MiB of HBM per device.

```python
import math
import jax
import jax.numpy as jnp
import numpy as np
from jax import lax

D = 7168
FF = 5120
HEADS = 64
HEAD_DIM = 256
EXPERTS = 8
TOPK = 2
CACHE_LEN = 1024
ROWS_DEV = 16
CAP = 5
ROWS = 1024
ATT_ROWS = 1024
N_GRP = 64


def shared_parts(key):
    first = jnp.clip(jax.random.normal(jax.random.fold_in(key, 11), (ATT_ROWS, HEAD_DIM), jnp.float32), -4.5, 4.5)
    return first


def draw_cache(key, part):
    first = shared_parts(key)
    key = jax.random.fold_in(key, 3)
    base = jnp.clip(jax.random.normal(key, (ATT_ROWS, CACHE_LEN, 2 * HEAD_DIM), jnp.float32), -4.5, 4.5)
    base = base.at[:, 0, :HEAD_DIM].set(first)
    return base.astype(jnp.bfloat16)


def draw_queries(key, part):
    key = jax.random.fold_in(key, 5)
    drawn = jnp.clip(jax.random.normal(key, (ATT_ROWS, HEADS, HEAD_DIM), jnp.float32), -4.5, 4.5)
    drawn = jnp.clip(drawn, -90.0, 90.0)
    return drawn.reshape(ATT_ROWS, HEADS * HEAD_DIM).astype(jnp.bfloat16)


def draw_lengths(key, part):
    key = jax.random.fold_in(key, 7)
    first_try = jax.random.randint(jax.random.fold_in(key, 1), (ATT_ROWS,), 2, CACHE_LEN + 1)
    second_try = jax.random.randint(jax.random.fold_in(key, 2), (ATT_ROWS,), 2, CACHE_LEN + 1)
    chosen = jnp.minimum(first_try, second_try)
    longest = jax.random.randint(jax.random.fold_in(key, 3), (), 0, ATT_ROWS)
    chosen = jnp.where(jnp.arange(ATT_ROWS) == longest, CACHE_LEN, chosen)
    return chosen.astype(jnp.int32)


def block_levels(key, shape, split, least, top_value):
    level = 1.0
    for dim, blocks in split:
        heights = jax.random.uniform(jax.random.fold_in(jax.random.fold_in(key, 6), dim), (blocks,), jnp.float32, least / len(split), top_value / len(split))
        level = level * jnp.repeat(jnp.exp(heights), shape[dim] // blocks).reshape((-1,) + (1,) * (len(shape) - 1 - dim))
    return level


def assign_block(rng, own, number, rows, amount, top, limit, lean):
    ranking = jax.random.permutation(rng, amount)
    crowded, common = load_shares(amount, rows * top, limit, lean, True), load_shares(amount, rows * top, limit, lean, False)
    places = jnp.arange(amount)

    def named(tallies, offset_by):
        used = int((tallies > 0).sum())
        fixed = max(1, used // 4)
        passed = fixed + (places - fixed + offset_by * (used - fixed)) % max(1, amount - fixed)
        return jnp.zeros((amount,), jnp.int32).at[ranking[jnp.where(places < fixed, places, passed)]].set(jnp.asarray(tallies, jnp.int32))

    tallies = jnp.where(number % 4 == 0, named(crowded, number // 4), named(common, number - number // 4 - 1))
    mixed = jax.random.permutation(jax.random.fold_in(own, 3), amount)
    donor, sink = mixed[0:amount // 2 * 2:2], mixed[1:amount // 2 * 2:2]
    room = jnp.minimum(tallies[donor] - 1, limit - tallies[sink]) // 2
    room = jnp.where((donor == ranking[0]) | (sink == ranking[0]) | (tallies[sink] == 0), 0, jnp.maximum(room, 0))
    passed = jax.random.randint(jax.random.fold_in(own, 4), (amount // 2,), 0, 1 << 20) % (room + 1)
    tallies = tallies.at[donor].add(-passed).at[sink].add(passed)
    items = jnp.searchsorted(jnp.cumsum(tallies), jnp.arange(rows * top), side="right").astype(jnp.int32)
    grid = items.reshape(top, rows).T
    grid = grid[jax.random.permutation(jax.random.fold_in(own, 1), rows)]
    offset_by = jax.random.randint(jax.random.fold_in(own, 2), (rows, 1), 0, top)
    return jnp.take_along_axis(grid, (jnp.arange(top)[None, :] + offset_by) % top, axis=1)


def load_shares(count, total, limit, lean, full):
    weights = [(1 << 20) // math.isqrt(standing ** lean) + 1 for standing in range(1, count + 1)]
    largest = limit if full else min(limit, max(-(-total // count), total * weights[0] // sum(weights)))
    least = 1 if total - largest >= count - 1 else 0
    given, rest = [largest] + [least] * (count - 1), total - largest - least * (count - 1)
    while rest > 0:
        movable = [i for i in range(1, count) if given[i] < largest] or [i for i in range(1, count) if given[i] < limit]
        mass, budget = sum([weights[i] for i in movable]), rest
        for i in movable:
            addition = min(limit - given[i], max(1, budget * weights[i] // mass), rest)
            given[i] = given[i] + addition
            rest = rest - addition
    return np.array(given)


def noise(stream_key, extent, deviation, most, shards=(), held_as=jnp.bfloat16):
    factor_of = block_levels(stream_key, extent, shards, -0.22, 0.18) if shards else 1.0
    entries = jax.random.normal(stream_key, extent, jnp.float32) * deviation * factor_of
    return jnp.minimum(jnp.maximum(entries, -most), most).astype(held_as)


def setup_inputs(seed: int = 0) -> dict:
    streams_of = jax.random.split(jax.random.key(seed), 10)
    x_rows = noise(streams_of[0], (ROWS, D), 1.0, 6.0, ((0, 64),))
    route_ids_keys = jax.random.split(jax.random.fold_in(streams_of[1], 1), ROWS // ROWS_DEV)
    route_ids_turns = jax.random.permutation(jax.random.fold_in(streams_of[1], 3), ROWS // ROWS_DEV)
    route_ids = jax.vmap(lambda own, number: assign_block(jax.random.fold_in(streams_of[1], 2), own, number, ROWS_DEV, EXPERTS, TOPK, CAP, 2))(route_ids_keys, route_ids_turns).reshape((ROWS, TOPK))
    router = noise(streams_of[2], (D, EXPERTS), D ** -0.5, 0.0625, (), jnp.float32)
    w_gate = noise(streams_of[3], (D, EXPERTS * FF), D ** -0.5, 0.0625, ((1, 256),))
    w_up = noise(streams_of[4], (D, EXPERTS * FF), D ** -0.5, 0.0625, ((1, 256),))
    w_down = noise(streams_of[5], (EXPERTS * FF, D), FF ** -0.5, 0.078125, ((0, 256),))
    queries = draw_queries(jax.random.fold_in(streams_of[9], 71), 0)
    cache = draw_cache(jax.random.fold_in(streams_of[9], 71), 0)
    lengths = draw_lengths(jax.random.fold_in(streams_of[9], 71), 0)
    return dict(x_rows=x_rows, route_ids=route_ids, router=router, w_gate=w_gate, w_up=w_up, w_down=w_down, queries=queries, cache=cache, lengths=lengths)


def mixture(x_rows, route_ids, router, w_gate, w_up, w_down):
    logits = jnp.dot(x_rows.astype(jnp.float32), router, precision=lax.Precision.HIGHEST)
    chosen = jnp.take_along_axis(logits, route_ids, axis=1)
    squashed = jax.nn.sigmoid(chosen)
    gate_share = squashed / lax.optimization_barrier(jnp.sum(squashed, axis=1, keepdims=True))
    bound = N_GRP * CAP
    slot_range = jnp.arange(bound)

    def add_expert(running, expert):
        matched = route_ids == expert
        weight_row = lax.optimization_barrier(jnp.sum(jnp.where(matched, gate_share, 0.0), axis=1))
        used = jnp.any(matched, axis=1)
        picked = jnp.nonzero(used, size=bound, fill_value=0)[0]
        count = jnp.sum(used.astype(jnp.int32))
        rows_in = x_rows[picked]
        start = (expert * FF).astype(jnp.int32)
        gate_cols = lax.dynamic_slice_in_dim(w_gate, start, FF, 1)
        up_cols = lax.dynamic_slice_in_dim(w_up, start, FF, 1)
        down_rows = lax.dynamic_slice_in_dim(w_down, start, FF, 0)
        gate_part = jnp.dot(rows_in, gate_cols, preferred_element_type=jnp.float32)
        up_part = jnp.dot(rows_in, up_cols, preferred_element_type=jnp.float32)
        hidden = (jax.nn.silu(gate_part) * up_part).astype(jnp.bfloat16)
        result = jnp.dot(hidden, down_rows, preferred_element_type=jnp.float32)
        keeper = jnp.where(slot_range < count, weight_row[picked], 0.0)
        running = running.at[picked].add(result * keeper[:, None])
        return (running, None)
    start_sum = jnp.zeros((x_rows.shape[0], x_rows.shape[1]), jnp.float32)
    running, unused = lax.scan(add_expert, start_sum, jnp.arange(EXPERTS, dtype=jnp.int32))
    return running.astype(jnp.bfloat16)

def attend_one(item):
    query_row, block, length = item
    query_heads = query_row.reshape(HEADS, HEAD_DIM)
    key_block = block[:, :HEAD_DIM]
    value_block = block[:, HEAD_DIM:]
    scores = jnp.dot(query_heads, key_block.T, preferred_element_type=jnp.float32) / math.sqrt(HEAD_DIM)
    live = jnp.arange(CACHE_LEN) < length
    scores = jnp.where(live[None, :], scores, -1e+30)
    largest = lax.optimization_barrier(jnp.max(scores, axis=1, keepdims=True))
    weights = jnp.where(live[None, :], jnp.exp(scores - largest), 0.0)
    denominator = lax.optimization_barrier(jnp.sum(weights, axis=1, keepdims=True))
    mixed = jnp.dot(weights.astype(jnp.bfloat16), value_block, preferred_element_type=jnp.float32)
    return (mixed / denominator).astype(jnp.bfloat16).reshape(HEADS * HEAD_DIM)

def reference(x_rows, route_ids, router, w_gate, w_up, w_down, queries, cache, lengths):
    moe_out = mixture(x_rows, route_ids, router, w_gate, w_up, w_down)
    attn_out = lax.map(attend_one, (queries, cache, lengths))
    return (moe_out, attn_out)
```

```python
import math

import jax
import jax.numpy as jnp
from jax import lax
from jax.sharding import Mesh
from jax.sharding import PartitionSpec as P

CAP = 5
SLOT = 8
ZLO = 4
ZALL = 8


def attention_block(queries, cache, lengths):
    head_dim = cache.shape[2] // 2
    head_count = queries.shape[1] // head_dim
    requests = queries.shape[0]
    position_count = cache.shape[1]
    query_heads = queries.reshape(requests, head_count, head_dim)
    key_block = cache[:, :, :head_dim]
    value_block = cache[:, :, head_dim:]
    scores = jnp.einsum(
        "bhd,bpd->bhp", query_heads, key_block, preferred_element_type=jnp.float32
    ) / math.sqrt(head_dim)
    live = jnp.arange(position_count)[None, :] < lengths[:, None]
    scores = jnp.where(live[:, None, :], scores, -1e30)
    largest = jnp.max(scores, axis=2, keepdims=True)
    weights = jnp.where(live[:, None, :], jnp.exp(scores - largest), 0.0)
    denominator = jnp.sum(weights, axis=2, keepdims=True)
    mixed = jnp.einsum(
        "bhp,bpd->bhd",
        weights.astype(jnp.bfloat16),
        value_block,
        preferred_element_type=jnp.float32,
    )
    return (mixed / denominator).astype(jnp.bfloat16).reshape(requests, head_count * head_dim)


def place(z):
    return (z % ZLO) * 2 + z // ZLO


UP = [(place(z), place((z + 1) % ZALL)) for z in range(ZALL)]
DOWN = [(place(z), place((z - 1) % ZALL)) for z in range(ZALL)]
SWAP = [(0, 1), (1, 0)]


def to_next(value):
    return lax.ppermute(value, ("zl", "zh"), UP)


def to_last(value):
    return lax.ppermute(value, ("zl", "zh"), DOWN)


def shards(x_rows, route_ids, router, w_gate, w_up, w_down, queries, cache, lengths):
    local_rows, model_width = x_rows.shape
    expert_count = router.shape[1]
    picks = route_ids.shape[1]
    quarter = model_width // 4
    half = model_width // 2
    piece = quarter // 2
    bf16, f32 = jnp.bfloat16, jnp.float32
    x_pos, z_lo, z_hi, core = (lax.axis_index(a) for a in ("xl", "zl", "zh", "c"))
    z_pos = z_hi * ZLO + z_lo

    flat_ids = route_ids.reshape(-1)
    onehot = (flat_ids[:, None] == jnp.arange(expert_count)[None, :]).astype(jnp.int32)
    before = jnp.cumsum(onehot, axis=0) - onehot
    slot_of = jnp.sum(before * onehot, axis=1)
    placed = onehot[:, :, None] * (
        slot_of[:, None, None] == jnp.arange(SLOT)[None, None, :]
    ).astype(jnp.int32)
    placed = placed.reshape(local_rows, picks, expert_count * SLOT)
    selector = jnp.sum(placed, axis=1).astype(bf16)

    x_quarter = lax.dynamic_slice_in_dim(x_rows, (z_hi * 2 + core) * quarter, quarter, 1)
    packed = jnp.einsum("rs,rd->sd", selector, x_quarter, preferred_element_type=f32).astype(bf16)
    arrived = lax.all_to_all(
        packed.reshape(expert_count, SLOT, quarter), ("y", "xh"), 0, 0, tiled=True
    )
    mine = arrived[:, :CAP].reshape(expert_count * CAP, quarter)
    theirs = lax.ppermute(mine, "xl", SWAP)
    first = x_pos == 0
    own = jnp.concatenate(
        [jnp.where(first, mine, theirs), jnp.where(first, theirs, mine)], axis=0
    )
    rows = own.shape[0]

    held = [None] * ZALL
    held[0] = own
    held[1], held[7] = to_last(own), to_next(own)
    held[2], held[6] = to_last(held[1]), to_next(held[7])
    held[3], held[5] = to_last(held[2]), to_next(held[6])
    held[4] = jnp.concatenate(
        [to_last(held[3][:, :piece]), to_next(held[5][:, piece:])], axis=1
    )
    other = [lax.ppermute(block, "c", SWAP) for block in held]
    is_zero = core == 0
    low_first = [(z_pos + k) % ZALL < ZLO for k in range(ZLO)]
    lines = []
    for k in range(ZLO):
        parts = []
        for at in (
            jnp.where(low_first[k], 0, 1),
            jnp.where(low_first[k], 1, 0),
        ):
            a = jnp.where(at == 0, held[k], held[k + ZLO])
            b = jnp.where(at == 0, other[k], other[k + ZLO])
            parts += [jnp.where(is_zero, a, b), jnp.where(is_zero, b, a)]
        lines.append(jnp.concatenate(parts, axis=1))
    rows_in = jnp.concatenate(lines, axis=0)

    gate_part = jnp.dot(rows_in, w_gate, preferred_element_type=f32)
    up_part = jnp.dot(rows_in, w_up, preferred_element_type=f32)
    hidden = (jax.nn.silu(gate_part) * up_part).astype(bf16)

    def columns(which):
        return jnp.concatenate(
            [
                lax.dynamic_slice_in_dim(w_down, which * quarter, quarter, 1),
                lax.dynamic_slice_in_dim(w_down, half + which * quarter, quarter, 1),
            ],
            axis=1,
        )

    away = jnp.dot(hidden, columns(1 - core), preferred_element_type=f32).astype(bf16)
    got = lax.ppermute(away, "c", SWAP)
    kept = jnp.dot(hidden, columns(core), preferred_element_type=f32) + got.astype(f32)

    def share(k):
        side = (z_pos + k) % ZALL // ZLO
        return lax.dynamic_slice(kept, ((k % ZLO) * rows, side * quarter), (rows, quarter))

    far = share(4).astype(bf16)
    from_last = to_next(far[:, :piece]).astype(f32)
    from_next = to_last(far[:, piece:]).astype(f32)
    from_last = jnp.pad(from_last, ((0, 0), (0, piece)))
    from_next = jnp.pad(from_next, ((0, 0), (piece, 0)))
    for k in (3, 2, 1):
        from_last = to_next((share(k) + from_last).astype(bf16)).astype(f32)
        from_next = to_last((share(ZALL - k) + from_next).astype(bf16)).astype(f32)
    total = share(0) + from_last + from_next
    top, bottom = total[: rows // 2], total[rows // 2 :]
    sent = jnp.where(first, bottom, top).astype(bf16)
    final = jnp.where(first, top, bottom) + lax.ppermute(sent, "xl", SWAP).astype(f32)
    final = jnp.pad(
        final.reshape(expert_count, CAP, quarter), ((0, 0), (0, SLOT - CAP), (0, 0))
    )
    returned = lax.all_to_all(final, ("y", "xh"), 0, 0, tiled=True)

    logits = jnp.dot(x_rows.astype(f32), router, precision=lax.Precision.HIGHEST)
    chosen = jnp.sum(
        onehot.reshape(local_rows, picks, expert_count).astype(f32) * logits[:, None, :], axis=2
    )
    squashed = jax.nn.sigmoid(chosen)
    gate_share = squashed / jnp.sum(squashed, axis=1, keepdims=True)
    weighting = jnp.sum(placed.astype(f32) * gate_share[:, :, None], axis=1)
    moe_out = jnp.dot(
        weighting, returned.reshape(expert_count * SLOT, quarter), precision=lax.Precision.HIGHEST
    )
    attn_out = attention_block(queries, cache, lengths)
    return (moe_out.astype(bf16), attn_out)


def solution(mesh):
    fine = Mesh(mesh.devices.reshape(4, 2, 2, 4, 2, 2), ("y", "xh", "xl", "zl", "zh", "c"))
    grp, tp = ("y", "xh", "xl", "zl"), ("zh", "c")
    every = grp + tp
    return jax.shard_map(
        shards,
        mesh=fine,
        in_specs=(
            P(grp, None),
            P(grp, None),
            P(),
            P(None, every),
            P(None, every),
            P(every, None),
            P(every, None),
            P(every, None, None),
            P(every),
        ),
        out_specs=(P(grp, tp), P(every, None)),
        check_vma=False,
    )
```

```python
import functools
import math

import jax
import jax.numpy as jnp
import numpy as np
from jax import lax
from jax.experimental import pallas as pl
from jax.experimental.pallas import tpu as pltpu
from jax.sharding import Mesh
from jax.sharding import PartitionSpec as P

CAP = 5
ZLO = 4
ZALL = 8
EXPERTS = 8
BLOCK = 16
PLANE = 16
LANES = 128
REACH = (0, 1, 2, -1)
BF16, F32 = jnp.bfloat16, jnp.float32
VMEM_BYTES = 40 * 1024 * 1024


def place(z):
    return (z % ZLO) * 2 + z // ZLO


def z_pairs(step):
    return [(place(z), place((z + step) % ZALL)) for z in range(ZALL)]


SWAP = [(0, 1), (1, 0)]


def z_send(value, step):
    return lax.ppermute(value, ("zl", "zh"), z_pairs(step))


def as_bf16(array):
    return jnp.asarray(np.asarray(array, np.float32), BF16)


def tables():
    lane = np.arange(LANES)
    lane_e = np.where(lane < EXPERTS * CAP, lane // CAP, -1)
    lane_s = lane % CAP
    e, u = np.divmod(np.arange(EXPERTS * BLOCK), BLOCK)
    k64 = np.arange(ZLO * BLOCK) // BLOCK
    pick_main = (lane_e[None] == e[:, None]) & (lane_s[None] == (u % CAP)[:, None])
    mask_main = (u // CAP)[:, None] == k64[None]
    g, s = np.divmod(u, 4)
    pick_rest = (lane_e[None] == e[:, None]) & (lane_s[None] == ((16 + s) % CAP)[:, None])
    g256 = np.arange(4 * 64) // 64
    k256 = np.tile(k64, 4)
    mask_rest = (g[:, None] == g256[None]) & (((16 + s) // CAP)[:, None] == k256[None])
    row = np.arange(PLANE * BLOCK)
    src, gs = np.divmod(row, BLOCK)
    spot = (gs // 4) * 64 + src * 4 + gs % 4
    shuffle = np.zeros((PLANE * BLOCK, PLANE * BLOCK))
    shuffle[spot, row] = 1
    e2, u2 = row // (2 * BLOCK), row % BLOCK
    back_main = (lane_e[:, None] == e2[None]) & (lane_s[:, None] == (u2 % CAP)[None])
    back_mask = k64[:, None] == (u2 // CAP)[None]
    g2, s2 = np.divmod(u2, 4)
    back_rest = (lane_e[:, None] == e2[None]) & (lane_s[:, None] == ((16 + s2) % CAP)[None])
    back_rest_mask = np.stack(
        [(g2[None] == i) & (k64[:, None] == ((16 + s2) // CAP)[None]) for i in range(4)]
    )
    spread = lane[:, None] == e2[None]
    return dict(
        pack=[as_bf16(a) for a in (pick_main, mask_main, pick_rest, mask_rest)],
        shuffle=as_bf16(shuffle),
        unshuffle=as_bf16(shuffle.T),
        back=[as_bf16(a) for a in (back_main, back_mask, back_rest, back_rest_mask, spread)],
    )


def dot(a, b):
    return jnp.dot(a, b, preferred_element_type=F32)


def dot_t(a, b):
    return lax.dot_general(a, b, (((1,), (1,)), ((), ())), preferred_element_type=F32)


def call(kernel, out_shape, *args):
    at = [pl.BlockSpec(memory_space=pltpu.SMEM if a.dtype == jnp.int32 else pltpu.VMEM) for a in args]
    return pl.pallas_call(
        kernel,
        out_shape=out_shape,
        in_specs=at,
        out_specs=jax.tree.map(lambda _: pl.BlockSpec(memory_space=pltpu.VMEM), out_shape),
        compiler_params=pltpu.CompilerParams(vmem_limit_bytes=VMEM_BYTES),
    )(*args)


def pack_kernel(quarter, *refs):
    blocks, (pick_main, mask_main, pick_rest, mask_rest), (out, marks) = refs[:4], refs[4:8], refs[8:]
    half = 2 * quarter
    eighth = quarter // 2
    rows = jnp.concatenate([b[:, :half] for b in blocks], axis=0)
    chosen = jnp.concatenate([b[:, half:] for b in blocks], axis=0)
    marks[...] = chosen
    select = (dot_t(pick_main[...], chosen) * mask_main[...].astype(F32)).astype(BF16)
    main = dot(select, rows).astype(BF16).reshape(EXPERTS, BLOCK, half)
    chosen4 = jnp.concatenate([chosen] * 4, axis=0)
    rows4 = jnp.concatenate([rows[:, i * eighth : (i + 1) * eighth] for i in range(4)], axis=0)
    select = (dot_t(pick_rest[...], chosen4) * mask_rest[...].astype(F32)).astype(BF16)
    rest = dot(select, rows4).astype(BF16).reshape(EXPERTS, BLOCK, eighth)
    for x in range(2):
        out[:, x, :, :half] = main
        out[:, x, :, half:] = rest


def experts_in(quarter, core, block, shuffle, w_gate, w_up):
    half, eighth = 2 * quarter, quarter // 2
    rest = dot(shuffle[...], block[:, half:]).astype(BF16)
    gate, up = 0.0, 0.0
    for f in range(2):
        top = block[:, f * quarter : (f + 1) * quarter]
        tail = jnp.concatenate(
            [rest[(2 * f + i) * 64 : (2 * f + i + 1) * 64] for i in range(2)], axis=1
        )
        rows = jnp.concatenate([top, tail], axis=0)
        at = pl.ds(pl.multiple_of(f * half + core * quarter, LANES), quarter)
        gate = gate + dot(rows, w_gate[at, :])
        up = up + dot(rows, w_up[at, :])
    return gate, up


def experts_out(quarter, core, hidden, w_down):
    half, eighth = 2 * quarter, quarter // 2
    mains, rests = [], []
    for f in range(2):
        at = pl.ds(pl.multiple_of(f * half + core * quarter, LANES), quarter)
        y = dot(hidden, w_down[:, at])
        mains.append(y[: PLANE * BLOCK])
        tail = y[PLANE * BLOCK :]
        rests += [tail[:, :eighth], tail[:, eighth:]]
    return mains, jnp.concatenate(rests, axis=0)


def own_kernel(quarter, core, block, shuffle, w_gate, w_up, gate_out, up_out):
    gate, up = experts_in(quarter, core[0], block, shuffle, w_gate, w_up)
    gate_out[...] = gate
    up_out[...] = up


def other_kernel(
    quarter, core, block, shuffle, unshuffle, w_gate, w_up, w_down, gate_in, up_in, hidden_out, away
):
    half = 2 * quarter
    there = 1 - core[0]
    gate, up = experts_in(quarter, there, block, shuffle, w_gate, w_up)
    gate, up = gate + gate_in[...], up + up_in[...]
    hidden = (gate * jax.nn.sigmoid(gate) * up).astype(BF16)
    hidden_out[...] = hidden
    mains, rest = experts_out(quarter, there, hidden, w_down)
    for f in range(2):
        away[:, f * quarter : (f + 1) * quarter] = mains[f].astype(BF16)
    away[:, half:] = dot(unshuffle[...], rest.astype(BF16)).astype(BF16)


def sum_kernel(quarter, core, hidden, unshuffle, w_down, got, out):
    half = 2 * quarter
    mains, rest = experts_out(quarter, core[0], hidden[...], w_down)
    for f in range(2):
        at = slice(f * quarter, (f + 1) * quarter)
        out[:, at] = (mains[f] + got[:, at].astype(F32)).astype(BF16)
    high = rest.astype(BF16)
    low = (rest - high.astype(F32)).astype(BF16)
    rest = dot(unshuffle[...], high) + dot(unshuffle[...], low)
    out[:, half:] = (rest + got[:, half:].astype(F32)).astype(BF16)


def combine_kernel(quarter, *refs):
    back, marks = refs[0], refs[1]
    shares = refs[2:6]
    back_main, back_mask, back_rest, back_rest_mask, spread = refs[6:11]
    outs = refs[11:]
    half, eighth = 2 * quarter, quarter // 2
    share = jnp.concatenate([s[...] for s in shares], axis=0)
    high = share.astype(BF16)
    low = (share - high.astype(F32)).astype(BF16)
    chosen = marks[...]
    main = dot(chosen, back_main[...]) * back_mask[...].astype(F32)
    rest = dot(chosen, back_rest[...])
    wide_high, wide_low = dot(high, spread[...]), dot(low, spread[...])
    total = dot((main * wide_high).astype(BF16), back[:, :half]) + dot(
        (main * wide_low).astype(BF16), back[:, :half]
    )
    tail = back[:, half:]
    pieces = []
    for i in range(4):
        mask = rest * back_rest_mask[i].astype(F32)
        pieces.append(
            dot((mask * wide_high).astype(BF16), tail) + dot((mask * wide_low).astype(BF16), tail)
        )
    total = total + jnp.concatenate(pieces, axis=1)
    outs[0][...] = total[:BLOCK]
    for k in range(1, ZLO):
        outs[k][...] = total[k * BLOCK : (k + 1) * BLOCK].astype(BF16)


def attention_block(queries, cache, lengths):
    head_dim = cache.shape[2] // 2
    head_count = queries.shape[1] // head_dim
    requests = queries.shape[0]
    position_count = cache.shape[1]
    query_heads = queries.reshape(requests, head_count, head_dim)
    key_block = cache[:, :, :head_dim]
    value_block = cache[:, :, head_dim:]
    scores = jnp.einsum(
        "bhd,bpd->bhp", query_heads, key_block, preferred_element_type=F32
    ) / math.sqrt(head_dim)
    live = jnp.arange(position_count)[None, :] < lengths[:, None]
    scores = jnp.where(live[:, None, :], scores, -1e30)
    largest = jnp.max(scores, axis=2, keepdims=True)
    weights = jnp.where(live[:, None, :], jnp.exp(scores - largest), 0.0)
    denominator = jnp.sum(weights, axis=2, keepdims=True)
    mixed = jnp.einsum("bhp,bpd->bhd", weights.astype(BF16), value_block, preferred_element_type=F32)
    return (mixed / denominator).astype(BF16).reshape(requests, head_count * head_dim)


def shards(x_rows, route_ids, router, w_gate, w_up, w_down, queries, cache, lengths):
    model_width = x_rows.shape[1]
    hidden_count = w_gate.shape[1]
    quarter = model_width // 4
    half, eighth = 2 * quarter, quarter // 2
    width = half + eighth
    table = tables()
    z_hi, core = lax.axis_index("zh"), lax.axis_index("c")
    core_ref = core.astype(jnp.int32).reshape(1)

    lane = jnp.arange(LANES)
    named = jnp.any(
        (route_ids[:, :, None] == (lane // CAP)[None, None, :]) & (lane < EXPERTS * CAP), axis=1
    )
    earlier = jnp.arange(BLOCK)[:, None] > jnp.arange(BLOCK)[None, :]
    rank = jnp.sum(jnp.where(earlier[:, :, None], named[None].astype(jnp.int32), 0), axis=1)
    marks = (named & (rank == (lane % CAP)[None, :])).astype(BF16)
    payload = jnp.concatenate(
        [
            lax.dynamic_slice_in_dim(x_rows, core * quarter, quarter, 1),
            lax.dynamic_slice_in_dim(x_rows, half + core * quarter, quarter, 1),
            marks,
        ],
        axis=1,
    )
    blocks = [payload] + [z_send(payload, -k) for k in REACH[1:]]

    packed, marks = call(
        functools.partial(pack_kernel, quarter),
        (
            jax.ShapeDtypeStruct((EXPERTS, 2, BLOCK, width), BF16),
            jax.ShapeDtypeStruct((ZLO * BLOCK, LANES), BF16),
        ),
        *blocks,
        *table["pack"],
    )
    arrived = lax.all_to_all(
        packed.reshape(PLANE, BLOCK, width), ("y", "xh", "xl"), 0, 0, tiled=True
    ).reshape(PLANE * BLOCK, width)
    beside = lax.ppermute(arrived, "c", SWAP)
    rows = PLANE * (BLOCK + ZLO)
    partial = jax.ShapeDtypeStruct((rows, hidden_count), F32)
    gate, up = call(
        functools.partial(own_kernel, quarter),
        (partial, partial),
        core_ref, arrived, table["shuffle"], w_gate, w_up,
    )
    pieces = jax.ShapeDtypeStruct((PLANE * BLOCK, width), BF16)
    hidden, away = call(
        functools.partial(other_kernel, quarter),
        (jax.ShapeDtypeStruct((rows, hidden_count), BF16), pieces),
        core_ref, beside, table["shuffle"], table["unshuffle"], w_gate, w_up, w_down, gate, up,
    )
    got = lax.ppermute(away, "c", SWAP)
    summed = call(
        functools.partial(sum_kernel, quarter),
        pieces,
        core_ref, hidden, table["unshuffle"], w_down, got,
    )
    returned = lax.all_to_all(
        summed.reshape(PLANE, BLOCK, width), ("y", "xh", "xl"), 0, 0, tiled=True
    ).reshape(PLANE * BLOCK, width)

    logits = jnp.dot(x_rows.astype(F32), router, precision=lax.Precision.HIGHEST)
    squashed = jax.nn.sigmoid(logits)
    picked = jnp.any(route_ids[:, :, None] == jnp.arange(EXPERTS)[None, None, :], axis=1)
    share = squashed / jnp.sum(jnp.where(picked, squashed, 0.0), axis=1, keepdims=True)
    share = jnp.pad(jnp.where(picked, share, 0.0), ((0, 0), (0, LANES - EXPERTS)))
    shares = [share] + [z_send(share, -k) for k in REACH[1:]]

    parts = call(
        functools.partial(combine_kernel, quarter),
        tuple(jax.ShapeDtypeStruct((BLOCK, half), F32 if k == 0 else BF16) for k in range(ZLO)),
        returned, marks, *shares, *table["back"],
    )
    total = parts[0]
    for k in range(1, ZLO):
        total = total + z_send(parts[k], REACH[k]).astype(F32)
    low, high = total[:, :quarter], total[:, quarter:]
    lower = z_hi == 0
    sent = jnp.where(lower, high, low).astype(BF16)
    moe_out = jnp.where(lower, low, high) + lax.ppermute(sent, "zh", SWAP).astype(F32)
    attn_out = attention_block(queries, cache, lengths)
    return (moe_out.astype(BF16), attn_out)


def solution(mesh):
    fine = Mesh(mesh.devices.reshape(4, 2, 2, 4, 2, 2), ("y", "xh", "xl", "zl", "zh", "c"))
    grp, tp = ("y", "xh", "xl", "zl"), ("zh", "c")
    every = grp + tp
    return jax.shard_map(
        shards,
        mesh=fine,
        in_specs=(
            P(grp, None),
            P(grp, None),
            P(),
            P(None, every),
            P(None, every),
            P(every, None),
            P(every, None),
            P(every, None, None),
            P(every),
        ),
        out_specs=(P(grp, tp), P(every, None)),
        check_vma=False,
    )
```

```python
import functools
import math

import jax
import jax.numpy as jnp
from jax import lax
from jax.experimental import pallas as pl
from jax.experimental.pallas import tpu as pltpu
from jax.sharding import Mesh
from jax.sharding import PartitionSpec as P

CAP = 5
ZLO = 4
ZALL = 8
EXPERTS = 8
BLOCK = 16
PLANE = 16
LANES = 128
REACH = (0, 1, 2, -1)
BF16, F32 = jnp.bfloat16, jnp.float32
VMEM_BYTES = 40 * 1024 * 1024


def place(z):
    return (z % ZLO) * 2 + z // ZLO


def z_pairs(step):
    return [(place(z), place((z + step) % ZALL)) for z in range(ZALL)]


SWAP = [(0, 1), (1, 0)]


def z_send(value, step):
    return lax.ppermute(value, ("zl", "zh"), z_pairs(step))


def grid(rows, columns):
    return (
        lax.broadcasted_iota(jnp.int32, (rows, columns), 0),
        lax.broadcasted_iota(jnp.int32, (rows, columns), 1),
    )


def fifth(value):
    return (value * 205) >> 10


def fifth_rest(value):
    return value - CAP * fifth(value)


def ones(condition):
    return jnp.where(condition, 1.0, 0.0)


def shuffle_table(back):
    new, old = grid(PLANE * BLOCK, PLANE * BLOCK)
    if back:
        new, old = old, new
    spot = ((old >> 2) & 3) * 64 + (old >> 4) * 4 + (old & 3)
    return ones(new == spot).astype(BF16)


def dot(a, b):
    return jnp.dot(a, b, preferred_element_type=F32)


def dot_t(a, b):
    return lax.dot_general(a, b, (((1,), (1,)), ((), ())), preferred_element_type=F32)


def call(kernel, out_shape, *args):
    at = [pl.BlockSpec(memory_space=pltpu.SMEM if a.dtype == jnp.int32 else pltpu.VMEM) for a in args]
    return pl.pallas_call(
        kernel,
        out_shape=out_shape,
        in_specs=at,
        out_specs=jax.tree.map(lambda _: pl.BlockSpec(memory_space=pltpu.VMEM), out_shape),
        compiler_params=pltpu.CompilerParams(vmem_limit_bytes=VMEM_BYTES),
    )(*args)


def pack_kernel(quarter, *refs):
    blocks, (out, marks) = refs[:4], refs[4:]
    half = 2 * quarter
    eighth = quarter // 2
    rows = jnp.concatenate([b[:, :half] for b in blocks], axis=0)
    chosen = jnp.concatenate([b[:, half:] for b in blocks], axis=0)
    marks[...] = chosen
    slot, lane = grid(EXPERTS * BLOCK, LANES)
    same = fifth(lane) == slot >> 4
    pick_main = ones(same & (fifth_rest(lane) == fifth_rest(slot & 15))).astype(BF16)
    pick_rest = ones(same & (fifth_rest(lane) == 1 + (slot & 3))).astype(BF16)
    slot, row = grid(EXPERTS * BLOCK, ZLO * BLOCK)
    mask = ones(fifth(slot & 15) == row >> 4)
    main = dot((dot_t(pick_main, chosen) * mask).astype(BF16), rows)
    main = main.astype(BF16).reshape(EXPERTS, BLOCK, half)
    chosen4 = jnp.concatenate([chosen] * 4, axis=0)
    rows4 = jnp.concatenate([rows[:, i * eighth : (i + 1) * eighth] for i in range(4)], axis=0)
    slot, row = grid(EXPERTS * BLOCK, 4 * ZLO * BLOCK)
    mask = ones(((slot >> 2) & 3 == row >> 6) & ((row >> 4) & 3 == 3))
    rest = dot((dot_t(pick_rest, chosen4) * mask).astype(BF16), rows4)
    rest = rest.astype(BF16).reshape(EXPERTS, BLOCK, eighth)
    for x in range(2):
        out[:, x, :, :half] = main
        out[:, x, :, half:] = rest


def experts_in(quarter, core, block, w_gate, w_up):
    half = 2 * quarter
    rest = dot(shuffle_table(False), block[:, half:]).astype(BF16)
    gate, up = 0.0, 0.0
    for f in range(2):
        top = block[:, f * quarter : (f + 1) * quarter]
        tail = jnp.concatenate(
            [rest[(2 * f + i) * 64 : (2 * f + i + 1) * 64] for i in range(2)], axis=1
        )
        rows = jnp.concatenate([top, tail], axis=0)
        at = pl.ds(pl.multiple_of(f * half + core * quarter, LANES), quarter)
        gate = gate + dot_t(rows, w_gate[:, at])
        up = up + dot_t(rows, w_up[:, at])
    return gate, up


def experts_out(quarter, core, hidden, w_down):
    half, eighth = 2 * quarter, quarter // 2
    mains, rests = [], []
    for f in range(2):
        at = pl.ds(pl.multiple_of(f * half + core * quarter, LANES), quarter)
        y = dot(hidden, w_down[:, at])
        mains.append(y[: PLANE * BLOCK])
        tail = y[PLANE * BLOCK :]
        rests += [tail[:, :eighth], tail[:, eighth:]]
    return mains, jnp.concatenate(rests, axis=0)


def own_kernel(quarter, core, block, w_gate, w_up, gate_out, up_out):
    gate, up = experts_in(quarter, core[0], block, w_gate, w_up)
    gate_out[...] = gate
    up_out[...] = up


def other_kernel(
    quarter, core, block, w_gate, w_up, w_down, gate_in, up_in, hidden_out, away
):
    half = 2 * quarter
    there = 1 - core[0]
    gate, up = experts_in(quarter, there, block, w_gate, w_up)
    gate, up = gate + gate_in[...], up + up_in[...]
    hidden = (gate * jax.nn.sigmoid(gate) * up).astype(BF16)
    hidden_out[...] = hidden
    mains, rest = experts_out(quarter, there, hidden, w_down)
    for f in range(2):
        away[:, f * quarter : (f + 1) * quarter] = mains[f].astype(BF16)
    away[:, half:] = dot(shuffle_table(True), rest.astype(BF16)).astype(BF16)


def sum_kernel(quarter, core, hidden, w_down, got, out):
    half = 2 * quarter
    mains, rest = experts_out(quarter, core[0], hidden[...], w_down)
    for f in range(2):
        at = slice(f * quarter, (f + 1) * quarter)
        out[:, at] = (mains[f] + got[:, at].astype(F32)).astype(BF16)
    high = rest.astype(BF16)
    low = (rest - high.astype(F32)).astype(BF16)
    unshuffle = shuffle_table(True)
    rest = dot(unshuffle, high) + dot(unshuffle, low)
    out[:, half:] = (rest + got[:, half:].astype(F32)).astype(BF16)


def combine_kernel(quarter, *refs):
    back, marks, shares, outs = refs[0], refs[1], refs[2:6], refs[6:]
    half = 2 * quarter
    share = jnp.concatenate([s[...] for s in shares], axis=0)
    high = share.astype(BF16)
    low = (share - high.astype(F32)).astype(BF16)
    chosen = marks[...]
    lane, slot = grid(LANES, PLANE * BLOCK)
    same = fifth(lane) == slot >> 5
    back_main = ones(same & (fifth_rest(lane) == fifth_rest(slot & 15))).astype(BF16)
    back_rest = ones(same & (fifth_rest(lane) == 1 + (slot & 3))).astype(BF16)
    spread = ones(lane == slot >> 5).astype(BF16)
    row, slot = grid(ZLO * BLOCK, PLANE * BLOCK)
    main = dot(chosen, back_main) * ones(fifth(slot & 15) == row >> 4)
    rest = dot(chosen, back_rest) * ones(row >> 4 == 3)
    wide_high, wide_low = dot(high, spread), dot(low, spread)
    total = dot((main * wide_high).astype(BF16), back[:, :half]) + dot(
        (main * wide_low).astype(BF16), back[:, :half]
    )
    tail = back[:, half:]
    pieces = []
    for i in range(4):
        mask = rest * ones((slot >> 2) & 3 == i)
        pieces.append(
            dot((mask * wide_high).astype(BF16), tail) + dot((mask * wide_low).astype(BF16), tail)
        )
    total = total + jnp.concatenate(pieces, axis=1)
    outs[0][...] = total[:BLOCK]
    for k in range(1, ZLO):
        outs[k][...] = total[k * BLOCK : (k + 1) * BLOCK].astype(BF16)


def attention_block(queries, cache, lengths):
    head_dim = cache.shape[2] // 2
    head_count = queries.shape[1] // head_dim
    requests = queries.shape[0]
    position_count = cache.shape[1]
    query_heads = queries.reshape(requests, head_count, head_dim)
    key_block = cache[:, :, :head_dim]
    value_block = cache[:, :, head_dim:]
    scores = jnp.einsum(
        "bhd,bpd->bhp", query_heads, key_block, preferred_element_type=F32
    ) / math.sqrt(head_dim)
    live = jnp.arange(position_count)[None, :] < lengths[:, None]
    scores = jnp.where(live[:, None, :], scores, -1e30)
    largest = jnp.max(scores, axis=2, keepdims=True)
    weights = jnp.where(live[:, None, :], jnp.exp(scores - largest), 0.0)
    denominator = jnp.sum(weights, axis=2, keepdims=True)
    mixed = jnp.einsum("bhp,bpd->bhd", weights.astype(BF16), value_block, preferred_element_type=F32)
    return (mixed / denominator).astype(BF16).reshape(requests, head_count * head_dim)


def shards(x_rows, route_ids, router, w_gate, w_up, w_down, queries, cache, lengths):
    model_width = x_rows.shape[1]
    hidden_count = w_gate.shape[1]
    w_gate, w_up = w_gate.T, w_up.T
    quarter = model_width // 4
    half, eighth = 2 * quarter, quarter // 2
    width = half + eighth
    z_hi, core = lax.axis_index("zh"), lax.axis_index("c")
    core_ref = core.astype(jnp.int32).reshape(1)

    lane = jnp.arange(LANES)
    named = jnp.any(
        (route_ids[:, :, None] == (lane // CAP)[None, None, :]) & (lane < EXPERTS * CAP), axis=1
    )
    earlier = jnp.arange(BLOCK)[:, None] > jnp.arange(BLOCK)[None, :]
    rank = jnp.sum(jnp.where(earlier[:, :, None], named[None].astype(jnp.int32), 0), axis=1)
    marks = (named & (rank == (lane % CAP)[None, :])).astype(BF16)
    payload = jnp.concatenate(
        [
            lax.dynamic_slice_in_dim(x_rows, core * quarter, quarter, 1),
            lax.dynamic_slice_in_dim(x_rows, half + core * quarter, quarter, 1),
            marks,
        ],
        axis=1,
    )
    blocks = [payload] + [z_send(payload, -k) for k in REACH[1:]]

    packed, marks = call(
        functools.partial(pack_kernel, quarter),
        (
            jax.ShapeDtypeStruct((EXPERTS, 2, BLOCK, width), BF16),
            jax.ShapeDtypeStruct((ZLO * BLOCK, LANES), BF16),
        ),
        *blocks,
    )
    arrived = lax.all_to_all(
        packed.reshape(PLANE, BLOCK, width), ("y", "xh", "xl"), 0, 0, tiled=True
    ).reshape(PLANE * BLOCK, width)
    beside = lax.ppermute(arrived, "c", SWAP)
    rows = PLANE * (BLOCK + ZLO)
    partial = jax.ShapeDtypeStruct((rows, hidden_count), F32)
    gate, up = call(
        functools.partial(own_kernel, quarter),
        (partial, partial),
        core_ref, arrived, w_gate, w_up,
    )
    pieces = jax.ShapeDtypeStruct((PLANE * BLOCK, width), BF16)
    hidden, away = call(
        functools.partial(other_kernel, quarter),
        (jax.ShapeDtypeStruct((rows, hidden_count), BF16), pieces),
        core_ref, beside, w_gate, w_up, w_down, gate, up,
    )
    got = lax.ppermute(away, "c", SWAP)
    summed = call(
        functools.partial(sum_kernel, quarter),
        pieces,
        core_ref, hidden, w_down, got,
    )
    summed, queries = lax.optimization_barrier((summed, queries))
    attn_out = attention_block(queries, cache, lengths)
    returned = lax.all_to_all(
        summed.reshape(PLANE, BLOCK, width), ("y", "xh", "xl"), 0, 0, tiled=True
    ).reshape(PLANE * BLOCK, width)

    logits = jnp.dot(x_rows.astype(F32), router, precision=lax.Precision.HIGHEST)
    squashed = jax.nn.sigmoid(logits)
    picked = jnp.any(route_ids[:, :, None] == jnp.arange(EXPERTS)[None, None, :], axis=1)
    share = squashed / jnp.sum(jnp.where(picked, squashed, 0.0), axis=1, keepdims=True)
    share = jnp.pad(jnp.where(picked, share, 0.0), ((0, 0), (0, LANES - EXPERTS)))
    shares = [share] + [z_send(share, -k) for k in REACH[1:]]

    returned, attn_out = lax.optimization_barrier((returned, attn_out))
    parts = call(
        functools.partial(combine_kernel, quarter),
        tuple(jax.ShapeDtypeStruct((BLOCK, half), F32 if k == 0 else BF16) for k in range(ZLO)),
        returned, marks, *shares,
    )
    total = parts[0]
    for k in range(1, ZLO):
        total = total + z_send(parts[k], REACH[k]).astype(F32)
    low, high = total[:, :quarter], total[:, quarter:]
    lower = z_hi == 0
    sent = jnp.where(lower, high, low).astype(BF16)
    moe_out = jnp.where(lower, low, high) + lax.ppermute(sent, "zh", SWAP).astype(F32)
    return (moe_out.astype(BF16), attn_out)


def solution(mesh):
    fine = Mesh(mesh.devices.reshape(4, 2, 2, 4, 2, 2), ("y", "xh", "xl", "zl", "zh", "c"))
    grp, tp = ("y", "xh", "xl", "zl"), ("zh", "c")
    every = grp + tp
    return jax.shard_map(
        shards,
        mesh=fine,
        in_specs=(
            P(grp, None),
            P(grp, None),
            P(),
            P(None, every),
            P(None, every),
            P(every, None),
            P(every, None),
            P(every, None, None),
            P(every),
        ),
        out_specs=(P(grp, tp), P(every, None)),
        check_vma=False,
    )
```

```python
import functools
import math

import jax
import jax.numpy as jnp
from jax import lax
from jax.experimental import pallas as pl
from jax.experimental.pallas import tpu as pltpu
from jax.sharding import Mesh
from jax.sharding import PartitionSpec as P

CAP = 5
ZLO = 4
ZALL = 8
EXPERTS = 8
BLOCK = 16
PLANE = 16
LANES = 128
REACH = (0, 1, 2, -1)
HIGH, LOW = 64, 72
BF16, F32 = jnp.bfloat16, jnp.float32
VMEM_BYTES = 40 * 1024 * 1024


def place(z):
    return (z % ZLO) * 2 + z // ZLO


def z_pairs(step):
    return [(place(z), place((z + step) % ZALL)) for z in range(ZALL)]


SWAP = [(0, 1), (1, 0)]


def z_send(value, step):
    return lax.ppermute(value, ("zl", "zh"), z_pairs(step))


def grid(rows, columns):
    return (
        lax.broadcasted_iota(jnp.int32, (rows, columns), 0),
        lax.broadcasted_iota(jnp.int32, (rows, columns), 1),
    )


def fifth(value):
    return (value * 205) >> 10


def fifth_rest(value):
    return value - CAP * fifth(value)


def ones(condition):
    return jnp.where(condition, 1.0, 0.0)


def shuffle_table(back):
    new, old = grid(PLANE * BLOCK, PLANE * BLOCK)
    if back:
        new, old = old, new
    spot = ((old >> 2) & 3) * 64 + (old >> 4) * 4 + (old & 3)
    return ones(new == spot).astype(BF16)


def dot(a, b):
    return jnp.dot(a, b, preferred_element_type=F32)


def dot_t(a, b):
    return lax.dot_general(a, b, (((1,), (1,)), ((), ())), preferred_element_type=F32)


def call(kernel, out_shape, *args):
    at = [pl.BlockSpec(memory_space=pltpu.SMEM if a.dtype == jnp.int32 else pltpu.VMEM) for a in args]
    return pl.pallas_call(
        kernel,
        out_shape=out_shape,
        in_specs=at,
        out_specs=jax.tree.map(lambda _: pl.BlockSpec(memory_space=pltpu.VMEM), out_shape),
        compiler_params=pltpu.CompilerParams(vmem_limit_bytes=VMEM_BYTES),
    )(*args)


def rows_kernel(quarter, where, x_rows, ids, router, out):
    half = 2 * quarter
    values = x_rows[...].astype(F32)
    first, second = ids[:, 0:1], ids[:, 1:2]
    row, lane = grid(BLOCK, LANES)
    squashed, total = [], 0.0
    for e in range(EXPERTS):
        logit = jnp.sum(values * router[e : e + 1, :], axis=1, keepdims=True)
        kept = jnp.where((first == e) | (second == e), jax.nn.sigmoid(logit), 0.0)
        squashed.append(kept)
        total = total + kept
    tail = jnp.zeros((BLOCK, LANES), F32)
    for e in range(EXPERTS):
        share = squashed[e] / total
        high = share.astype(BF16).astype(F32)
        low = (share - high).astype(BF16).astype(F32)
        tail = jnp.where(lane == HIGH + e, high, jnp.where(lane == LOW + e, low, tail))
    expert = fifth(lane)
    named = (first == expert) | (second == expert)
    row, column = grid(BLOCK, BLOCK)
    rank = dot(ones(row > column).astype(BF16), ones(named).astype(BF16))
    marks = ones(named & (rank == fifth_rest(lane).astype(F32)))
    tail = jnp.where(lane < EXPERTS * CAP, marks, tail)
    for f in range(2):
        at = pl.ds(pl.multiple_of(f * half + where[0] * quarter, LANES), quarter)
        out[:, f * quarter : (f + 1) * quarter] = x_rows[:, at]
    out[:, half:] = tail.astype(BF16)


def pack_kernel(quarter, *refs):
    blocks, (out, marks) = refs[:4], refs[4:]
    half = 2 * quarter
    eighth = quarter // 2
    rows = jnp.concatenate([b[:, :half] for b in blocks], axis=0)
    chosen = jnp.concatenate([b[:, half:] for b in blocks], axis=0)
    marks[...] = chosen
    lane = grid(ZLO * BLOCK, LANES)[1]
    chosen = jnp.where(lane < EXPERTS * CAP, chosen, jnp.zeros_like(chosen))
    slot, lane = grid(EXPERTS * BLOCK, LANES)
    same = fifth(lane) == slot >> 4
    pick_main = ones(same & (fifth_rest(lane) == fifth_rest(slot & 15))).astype(BF16)
    pick_rest = ones(same & (fifth_rest(lane) == 1 + (slot & 3))).astype(BF16)
    slot, row = grid(EXPERTS * BLOCK, ZLO * BLOCK)
    mask = ones(fifth(slot & 15) == row >> 4)
    main = dot((dot_t(pick_main, chosen) * mask).astype(BF16), rows)
    main = main.astype(BF16).reshape(EXPERTS, BLOCK, half)
    chosen4 = jnp.concatenate([chosen] * 4, axis=0)
    rows4 = jnp.concatenate([rows[:, i * eighth : (i + 1) * eighth] for i in range(4)], axis=0)
    slot, row = grid(EXPERTS * BLOCK, 4 * ZLO * BLOCK)
    mask = ones(((slot >> 2) & 3 == row >> 6) & ((row >> 4) & 3 == 3))
    rest = dot((dot_t(pick_rest, chosen4) * mask).astype(BF16), rows4)
    rest = rest.astype(BF16).reshape(EXPERTS, BLOCK, eighth)
    for x in range(2):
        out[:, x, :, :half] = main
        out[:, x, :, half:] = rest


def experts_in(quarter, core, block, w_gate, w_up):
    half = 2 * quarter
    rest = dot(shuffle_table(False), block[:, half:]).astype(BF16)
    gate, up = 0.0, 0.0
    for f in range(2):
        top = block[:, f * quarter : (f + 1) * quarter]
        tail = jnp.concatenate(
            [rest[(2 * f + i) * 64 : (2 * f + i + 1) * 64] for i in range(2)], axis=1
        )
        rows = jnp.concatenate([top, tail], axis=0)
        at = pl.ds(pl.multiple_of(f * half + core * quarter, LANES), quarter)
        gate = gate + dot_t(rows, w_gate[:, at])
        up = up + dot_t(rows, w_up[:, at])
    return gate, up


def experts_out(quarter, core, hidden, w_down):
    half, eighth = 2 * quarter, quarter // 2
    mains, rests = [], []
    for f in range(2):
        at = pl.ds(pl.multiple_of(f * half + core * quarter, LANES), quarter)
        y = dot(hidden, w_down[:, at])
        mains.append(y[: PLANE * BLOCK])
        tail = y[PLANE * BLOCK :]
        rests += [tail[:, :eighth], tail[:, eighth:]]
    return mains, jnp.concatenate(rests, axis=0)


def own_kernel(quarter, core, block, w_gate, w_up, gate_out, up_out):
    gate, up = experts_in(quarter, core[0], block, w_gate, w_up)
    gate_out[...] = gate
    up_out[...] = up


def other_kernel(
    quarter, core, block, w_gate, w_up, w_down, gate_in, up_in, hidden_out, away
):
    half = 2 * quarter
    there = 1 - core[0]
    gate, up = experts_in(quarter, there, block, w_gate, w_up)
    gate, up = gate + gate_in[...], up + up_in[...]
    hidden = (gate * jax.nn.sigmoid(gate) * up).astype(BF16)
    hidden_out[...] = hidden
    mains, rest = experts_out(quarter, there, hidden, w_down)
    for f in range(2):
        away[:, f * quarter : (f + 1) * quarter] = mains[f].astype(BF16)
    away[:, half:] = dot(shuffle_table(True), rest.astype(BF16)).astype(BF16)


def sum_kernel(quarter, core, hidden, w_down, got, out):
    half = 2 * quarter
    mains, rest = experts_out(quarter, core[0], hidden[...], w_down)
    for f in range(2):
        at = slice(f * quarter, (f + 1) * quarter)
        out[:, at] = (mains[f] + got[:, at].astype(F32)).astype(BF16)
    high = rest.astype(BF16)
    low = (rest - high.astype(F32)).astype(BF16)
    unshuffle = shuffle_table(True)
    rest = dot(unshuffle, high) + dot(unshuffle, low)
    out[:, half:] = (rest + got[:, half:].astype(F32)).astype(BF16)


def combine_kernel(quarter, where, back, marks, out):
    half = 2 * quarter
    chosen = marks[...]
    lane, slot = grid(LANES, PLANE * BLOCK)
    expert = slot >> 5
    same = fifth(lane) == expert
    back_main = ones(same & (fifth_rest(lane) == fifth_rest(slot & 15))).astype(BF16)
    back_rest = ones(same & (fifth_rest(lane) == 1 + (slot & 3))).astype(BF16)
    wide_high = dot(chosen, ones(lane == HIGH + expert).astype(BF16))
    wide_low = dot(chosen, ones(lane == LOW + expert).astype(BF16))
    row, slot = grid(ZLO * BLOCK, PLANE * BLOCK)
    main = dot(chosen, back_main) * ones(fifth(slot & 15) == row >> 4)
    rest = dot(chosen, back_rest) * ones(row >> 4 == 3)
    total = dot((main * wide_high).astype(BF16), back[:, :half]) + dot(
        (main * wide_low).astype(BF16), back[:, :half]
    )
    tail = back[:, half:]
    pieces = []
    for i in range(4):
        mask = rest * ones((slot >> 2) & 3 == i)
        pieces.append(
            dot((mask * wide_high).astype(BF16), tail) + dot((mask * wide_low).astype(BF16), tail)
        )
    total = total + jnp.concatenate(pieces, axis=1)
    for k in range(ZLO):
        owner = (where[1] + (REACH[k] % ZLO)) & (ZLO - 1)
        for f in range(2):
            piece = total[k * BLOCK : (k + 1) * BLOCK, f * quarter : (f + 1) * quarter]
            out[owner * 2 + f] = piece.astype(BF16)


def attention_block(queries, cache, lengths):
    head_dim = cache.shape[2] // 2
    head_count = queries.shape[1] // head_dim
    requests = queries.shape[0]
    position_count = cache.shape[1]
    query_heads = queries.reshape(requests, head_count, head_dim)
    key_block = cache[:, :, :head_dim]
    value_block = cache[:, :, head_dim:]
    scores = jnp.einsum(
        "bhd,bpd->bhp", query_heads, key_block, preferred_element_type=F32
    ) / math.sqrt(head_dim)
    live = jnp.arange(position_count)[None, :] < lengths[:, None]
    scores = jnp.where(live[:, None, :], scores, -1e30)
    largest = jnp.max(scores, axis=2, keepdims=True)
    weights = jnp.where(live[:, None, :], jnp.exp(scores - largest), 0.0)
    denominator = jnp.sum(weights, axis=2, keepdims=True)
    mixed = jnp.einsum("bhp,bpd->bhd", weights.astype(BF16), value_block, preferred_element_type=F32)
    return (mixed / denominator).astype(BF16).reshape(requests, head_count * head_dim)


def shards(x_rows, route_ids, router, w_gate, w_up, w_down, queries, cache, lengths):
    model_width = x_rows.shape[1]
    hidden_count = w_gate.shape[1]
    w_gate, w_up = w_gate.T, w_up.T
    quarter = model_width // 4
    half, eighth = 2 * quarter, quarter // 2
    width = half + eighth
    where = jnp.stack([lax.axis_index("c"), lax.axis_index("zl")]).astype(jnp.int32)
    payload = call(
        functools.partial(rows_kernel, quarter),
        jax.ShapeDtypeStruct((BLOCK, half + LANES), BF16),
        where, x_rows, route_ids.astype(F32), router.T,
    )
    blocks = [payload] + [z_send(payload, -k) for k in REACH[1:]]

    payload, queries = lax.optimization_barrier((payload, queries))
    attn_out = attention_block(queries, cache, lengths)
    blocks, attn_out = lax.optimization_barrier((blocks, attn_out))
    packed, marks = call(
        functools.partial(pack_kernel, quarter),
        (
            jax.ShapeDtypeStruct((EXPERTS, 2, BLOCK, width), BF16),
            jax.ShapeDtypeStruct((ZLO * BLOCK, LANES), BF16),
        ),
        *blocks,
    )
    arrived = lax.all_to_all(
        packed.reshape(PLANE, BLOCK, width), ("y", "xh", "xl"), 0, 0, tiled=True
    ).reshape(PLANE * BLOCK, width)
    beside = lax.ppermute(arrived, "c", SWAP)
    rows = PLANE * (BLOCK + ZLO)
    partial = jax.ShapeDtypeStruct((rows, hidden_count), F32)
    gate, up = call(
        functools.partial(own_kernel, quarter),
        (partial, partial),
        where, arrived, w_gate, w_up,
    )
    pieces = jax.ShapeDtypeStruct((PLANE * BLOCK, width), BF16)
    hidden, away = call(
        functools.partial(other_kernel, quarter),
        (jax.ShapeDtypeStruct((rows, hidden_count), BF16), pieces),
        where, beside, w_gate, w_up, w_down, gate, up,
    )
    got = lax.ppermute(away, "c", SWAP)
    summed = call(
        functools.partial(sum_kernel, quarter),
        pieces,
        where, hidden, w_down, got,
    )
    returned = lax.all_to_all(
        summed.reshape(PLANE, BLOCK, width), ("y", "xh", "xl"), 0, 0, tiled=True
    ).reshape(PLANE * BLOCK, width)

    parts = call(
        functools.partial(combine_kernel, quarter),
        jax.ShapeDtypeStruct((ZALL, BLOCK, quarter), BF16),
        where, returned, marks,
    )
    parts = lax.all_to_all(parts, ("zl", "zh"), 0, 0, tiled=True)
    moe_out = jnp.sum(parts.astype(F32), axis=0)
    return (moe_out.astype(BF16), attn_out)


def solution(mesh):
    fine = Mesh(mesh.devices.reshape(4, 2, 2, 4, 2, 2), ("y", "xh", "xl", "zl", "zh", "c"))
    grp, tp = ("y", "xh", "xl", "zl"), ("zh", "c")
    every = grp + tp
    return jax.shard_map(
        shards,
        mesh=fine,
        in_specs=(
            P(grp, None),
            P(grp, None),
            P(),
            P(None, every),
            P(None, every),
            P(every, None),
            P(every, None),
            P(every, None, None),
            P(every),
        ),
        out_specs=(P(grp, tp), P(every, None)),
        check_vma=False,
    )
```

```python
import functools
import math

import jax
import jax.numpy as jnp
from jax import lax
from jax.experimental import pallas as pl
from jax.experimental.pallas import tpu as pltpu
from jax.sharding import Mesh
from jax.sharding import PartitionSpec as P

CAP = 5
ZLO = 4
ZALL = 8
EXPERTS = 8
BLOCK = 16
PLANE = 16
LANES = 128
REACH = (0, 1, 2, -1)
HIGH, LOW = 64, 72
PLAIN, RING = 3, 2
BF16, F32 = jnp.bfloat16, jnp.float32
VMEM_BYTES = 40 * 1024 * 1024


def place(z):
    return (z % ZLO) * 2 + z // ZLO


def z_pairs(step):
    return [(place(z), place((z + step) % ZALL)) for z in range(ZALL)]


SWAP = [(0, 1), (1, 0)]


def z_send(value, step):
    return lax.ppermute(value, ("zl", "zh"), z_pairs(step))


def grid(rows, columns):
    return (
        lax.broadcasted_iota(jnp.int32, (rows, columns), 0),
        lax.broadcasted_iota(jnp.int32, (rows, columns), 1),
    )


def fifth(value):
    return (value * 205) >> 10


def fifth_rest(value):
    return value - CAP * fifth(value)


def third(value):
    return (value * 86) >> 8


def ones(condition):
    return jnp.where(condition, 1.0, 0.0)


def shuffle_table(back):
    new, old = grid(PLANE * BLOCK, PLANE * BLOCK)
    if back:
        new, old = old, new
    spot = ((old >> 2) & 3) * 64 + (old >> 4) * 4 + (old & 3)
    return ones(new == spot).astype(BF16)


def dot(a, b):
    return jnp.dot(a, b, preferred_element_type=F32)


def dot_t(a, b):
    return lax.dot_general(a, b, (((1,), (1,)), ((), ())), preferred_element_type=F32)


def call(kernel, out_shape, *args):
    at = [pl.BlockSpec(memory_space=pltpu.SMEM if a.dtype == jnp.int32 else pltpu.VMEM) for a in args]
    return pl.pallas_call(
        kernel,
        out_shape=out_shape,
        in_specs=at,
        out_specs=jax.tree.map(lambda _: pl.BlockSpec(memory_space=pltpu.VMEM), out_shape),
        compiler_params=pltpu.CompilerParams(vmem_limit_bytes=VMEM_BYTES),
    )(*args)


def rows_kernel(quarter, where, x_rows, ids, router, out, ring_out):
    half = 2 * quarter
    values = x_rows[...].astype(F32)
    first, second = ids[:, 0:1], ids[:, 1:2]
    row, lane = grid(BLOCK, LANES)
    squashed, total = [], 0.0
    for e in range(EXPERTS):
        logit = jnp.sum(values * router[e : e + 1, :], axis=1, keepdims=True)
        kept = jnp.where((first == e) | (second == e), jax.nn.sigmoid(logit), 0.0)
        squashed.append(kept)
        total = total + kept
    tail = jnp.zeros((BLOCK, LANES), F32)
    for e in range(EXPERTS):
        share = squashed[e] / total
        high = share.astype(BF16).astype(F32)
        low = (share - high).astype(BF16).astype(F32)
        tail = jnp.where(lane == HIGH + e, high, jnp.where(lane == LOW + e, low, tail))
    expert = fifth(lane)
    named = (first == expert) | (second == expert)
    row, column = grid(BLOCK, BLOCK)
    rank = dot(ones(row > column).astype(BF16), ones(named).astype(BF16))
    marks = ones(named & (rank == fifth_rest(lane).astype(F32)))
    tail = jnp.where(lane < EXPERTS * CAP, marks, tail)
    for f in range(2):
        at = pl.ds(pl.multiple_of(f * half + where[0] * quarter, LANES), quarter)
        out[:, f * quarter : (f + 1) * quarter] = x_rows[:, at]
    out[:, half:] = tail.astype(BF16)
    at = pl.ds(pl.multiple_of(where[2] * half + where[0] * quarter, LANES), quarter)
    mine = x_rows[:, at]
    slot, lane = grid(PLANE * 2 * RING, LANES)
    pick = (fifth(lane) == slot >> 3) & (fifth_rest(lane) == PLAIN + ((slot >> 1) & 1))
    select = dot_t(ones(pick).astype(BF16), marks.astype(BF16))
    second_half = grid(PLANE * 2 * RING, BLOCK)[0] & 1
    ring_out[...] = (
        dot((select * ones(second_half == 0)).astype(BF16), mine[:, : quarter // 2])
        + dot((select * ones(second_half == 1)).astype(BF16), mine[:, quarter // 2 :])
    ).astype(BF16)


def ring_kernel(*refs):
    blocks, out = refs[:-1], refs[-1]
    width = blocks[0].shape[1]
    for k in range(ZALL):
        at = slice(k * width, (k + 1) * width)
        if k < 4:
            out[:, at] = blocks[k][...]
        elif k == 4:
            out[:, at] = jnp.concatenate([blocks[4][...], blocks[5][...]], axis=0)
        else:
            out[:, at] = blocks[k + 1][...]


def pack_kernel(quarter, *refs):
    blocks, (out, marks) = refs[:4], refs[4:]
    half = 2 * quarter
    eighth = quarter // 2
    rows = jnp.concatenate([b[:, :half] for b in blocks], axis=0)
    chosen = jnp.concatenate([b[:, half:] for b in blocks], axis=0)
    marks[...] = chosen
    lane = grid(ZLO * BLOCK, LANES)[1]
    chosen = jnp.where(lane < EXPERTS * CAP, chosen, jnp.zeros_like(chosen))
    chosen4 = jnp.concatenate([chosen] * 4, axis=0)
    rows4 = jnp.concatenate([rows[:, i * eighth : (i + 1) * eighth] for i in range(4)], axis=0)
    for j in range(PLAIN):
        slot, lane = grid(EXPERTS * BLOCK, LANES)
        number = 4 * j + (slot & 3)
        same = (fifth(lane) == slot >> 4) & (fifth_rest(lane) == number - PLAIN * third(number))
        slot, row = grid(EXPERTS * BLOCK, 4 * ZLO * BLOCK)
        number = 4 * j + (slot & 3)
        mask = ones(((slot >> 2) & 3 == row >> 6) & ((row >> 4) & 3 == third(number)))
        select = dot_t(ones(same).astype(BF16), chosen4) * mask
        part = dot(select.astype(BF16), rows4).astype(BF16).reshape(EXPERTS, BLOCK, eighth)
        for x in range(2):
            out[:, x, :, j * eighth : (j + 1) * eighth] = part


def experts_in(quarter, where, core, block, ring, w_gate, w_up):
    half, eighth = 2 * quarter, quarter // 2
    plain = dot(shuffle_table(False), block[...]).astype(BF16)
    new, old = grid(PLANE * 2 * RING, PLANE * 2 * RING)
    spot = (old & 1) * 2 * BLOCK + (old >> 1)
    split = ones(new == spot).astype(BF16)
    z_pos = where[2] * ZLO + where[1]
    gate, up = 0.0, 0.0
    for f in range(2):
        rows = []
        for j in range(PLAIN):
            at = slice(j * eighth, (j + 1) * eighth)
            pair = [plain[g * 64 : (g + 1) * 64, at] for g in (2 * f, 2 * f + 1)]
            rows.append(jnp.concatenate(pair, axis=1))
        for k in range(ZLO):
            near = ((z_pos + k) & (ZALL - 1)) >> 2 == f
            piece = jnp.where(
                near,
                ring[:, k * eighth : (k + 1) * eighth],
                ring[:, (k + ZLO) * eighth : (k + ZLO + 1) * eighth],
            )
            piece = dot(split, piece).astype(BF16)
            rows.append(jnp.concatenate([piece[: 2 * BLOCK], piece[2 * BLOCK :]], axis=1))
        rows = jnp.concatenate(rows, axis=0)
        at = pl.ds(pl.multiple_of(f * half + core * quarter, LANES), quarter)
        gate = gate + dot_t(rows, w_gate[:, at])
        up = up + dot_t(rows, w_up[:, at])
    return gate, up


def return_order(hidden):
    count = PLANE * (BLOCK + ZLO)
    new, old = grid(count, count)
    main = new < PLANE * BLOCK
    src = jnp.where(main, new >> 4, (new - PLANE * BLOCK) >> 2)
    slot = jnp.where(main, new & 15, 16 + (new & 3))
    k, s = fifth(slot), fifth_rest(slot)
    number = k * PLAIN + s
    plain = (number >> 2) * 64 + src * 4 + (number & 3)
    ring = PLAIN * 64 + k * 2 * BLOCK + src * 2 + s - PLAIN
    spot = jnp.where(s < PLAIN, plain, ring)
    return dot(ones(old == spot).astype(BF16), hidden).astype(BF16)


def experts_out(quarter, core, hidden, w_down):
    half, eighth = 2 * quarter, quarter // 2
    mains, rests = [], []
    for f in range(2):
        at = pl.ds(pl.multiple_of(f * half + core * quarter, LANES), quarter)
        y = dot(hidden, w_down[:, at])
        mains.append(y[: PLANE * BLOCK])
        tail = y[PLANE * BLOCK :]
        rests += [tail[:, :eighth], tail[:, eighth:]]
    return mains, jnp.concatenate(rests, axis=0)


def own_kernel(quarter, where, block, ring, w_gate, w_up, gate_out, up_out):
    gate, up = experts_in(quarter, where, where[0], block, ring, w_gate, w_up)
    gate_out[...] = gate
    up_out[...] = up


def other_kernel(
    quarter, where, block, ring, w_gate, w_up, w_down, gate_in, up_in, hidden_out, away
):
    half = 2 * quarter
    there = 1 - where[0]
    gate, up = experts_in(quarter, where, there, block, ring, w_gate, w_up)
    gate, up = gate + gate_in[...], up + up_in[...]
    hidden = return_order((gate * jax.nn.sigmoid(gate) * up).astype(BF16))
    hidden_out[...] = hidden
    mains, rest = experts_out(quarter, there, hidden, w_down)
    for f in range(2):
        away[:, f * quarter : (f + 1) * quarter] = mains[f].astype(BF16)
    away[:, half:] = dot(shuffle_table(True), rest.astype(BF16)).astype(BF16)


def sum_kernel(quarter, core, hidden, w_down, got, out):
    half = 2 * quarter
    mains, rest = experts_out(quarter, core[0], hidden[...], w_down)
    for f in range(2):
        at = slice(f * quarter, (f + 1) * quarter)
        out[:, at] = (mains[f] + got[:, at].astype(F32)).astype(BF16)
    high = rest.astype(BF16)
    low = (rest - high.astype(F32)).astype(BF16)
    unshuffle = shuffle_table(True)
    rest = dot(unshuffle, high) + dot(unshuffle, low)
    out[:, half:] = (rest + got[:, half:].astype(F32)).astype(BF16)


def combine_kernel(quarter, where, back, marks, out):
    half = 2 * quarter
    chosen = marks[...]
    lane, slot = grid(LANES, PLANE * BLOCK)
    expert = slot >> 5
    same = fifth(lane) == expert
    back_main = ones(same & (fifth_rest(lane) == fifth_rest(slot & 15))).astype(BF16)
    back_rest = ones(same & (fifth_rest(lane) == 1 + (slot & 3))).astype(BF16)
    wide_high = dot(chosen, ones(lane == HIGH + expert).astype(BF16))
    wide_low = dot(chosen, ones(lane == LOW + expert).astype(BF16))
    row, slot = grid(ZLO * BLOCK, PLANE * BLOCK)
    main = dot(chosen, back_main) * ones(fifth(slot & 15) == row >> 4)
    rest = dot(chosen, back_rest) * ones(row >> 4 == 3)
    total = dot((main * wide_high).astype(BF16), back[:, :half]) + dot(
        (main * wide_low).astype(BF16), back[:, :half]
    )
    tail = back[:, half:]
    pieces = []
    for i in range(4):
        mask = rest * ones((slot >> 2) & 3 == i)
        pieces.append(
            dot((mask * wide_high).astype(BF16), tail) + dot((mask * wide_low).astype(BF16), tail)
        )
    total = total + jnp.concatenate(pieces, axis=1)
    for k in range(ZLO):
        owner = (where[1] + (REACH[k] % ZLO)) & (ZLO - 1)
        for f in range(2):
            piece = total[k * BLOCK : (k + 1) * BLOCK, f * quarter : (f + 1) * quarter]
            out[owner * 2 + f] = piece.astype(BF16)


def attention_block(queries, cache, lengths):
    head_dim = cache.shape[2] // 2
    head_count = queries.shape[1] // head_dim
    requests = queries.shape[0]
    position_count = cache.shape[1]
    query_heads = queries.reshape(requests, head_count, head_dim)
    key_block = cache[:, :, :head_dim]
    value_block = cache[:, :, head_dim:]
    scores = jnp.einsum(
        "bhd,bpd->bhp", query_heads, key_block, preferred_element_type=F32
    ) / math.sqrt(head_dim)
    live = jnp.arange(position_count)[None, :] < lengths[:, None]
    scores = jnp.where(live[:, None, :], scores, -1e30)
    largest = jnp.max(scores, axis=2, keepdims=True)
    weights = jnp.where(live[:, None, :], jnp.exp(scores - largest), 0.0)
    denominator = jnp.sum(weights, axis=2, keepdims=True)
    mixed = jnp.einsum("bhp,bpd->bhd", weights.astype(BF16), value_block, preferred_element_type=F32)
    return (mixed / denominator).astype(BF16).reshape(requests, head_count * head_dim)


def shards(x_rows, route_ids, router, w_gate, w_up, w_down, queries, cache, lengths):
    model_width = x_rows.shape[1]
    hidden_count = w_gate.shape[1]
    w_gate, w_up = w_gate.T, w_up.T
    quarter = model_width // 4
    half, eighth = 2 * quarter, quarter // 2
    width = half + eighth
    where = jnp.stack([lax.axis_index(a) for a in ("c", "zl", "zh")]).astype(jnp.int32)
    payload, ring = call(
        functools.partial(rows_kernel, quarter),
        (
            jax.ShapeDtypeStruct((BLOCK, half + LANES), BF16),
            jax.ShapeDtypeStruct((PLANE * 2 * RING, eighth), BF16),
        ),
        where, x_rows, route_ids.astype(F32), router.T,
    )
    blocks = [payload] + [z_send(payload, -k) for k in REACH[1:]]
    ring = lax.all_to_all(
        ring.reshape(PLANE, 2 * RING, eighth), ("y", "xh", "xl"), 0, 0, tiled=True
    ).reshape(PLANE * 2 * RING, eighth)
    payload, queries = lax.optimization_barrier((payload, queries))
    attn_out = attention_block(queries, cache, lengths)
    blocks, ring, attn_out = lax.optimization_barrier((blocks, ring, attn_out))
    ups, downs = [ring], [ring]
    for _ in range(3):
        ups.append(z_send(ups[-1], -1))
        downs.append(z_send(downs[-1], 1))
    middle = PLANE * RING
    ring = call(
        ring_kernel,
        jax.ShapeDtypeStruct((PLANE * 2 * RING, ZALL * eighth), BF16),
        *ups, z_send(ups[-1][:middle], -1), z_send(downs[-1][middle:], 1), *downs[:0:-1],
    )
    ring_beside = lax.ppermute(ring, "c", SWAP)
    packed, marks = call(
        functools.partial(pack_kernel, quarter),
        (
            jax.ShapeDtypeStruct((EXPERTS, 2, BLOCK, PLAIN * eighth), BF16),
            jax.ShapeDtypeStruct((ZLO * BLOCK, LANES), BF16),
        ),
        *blocks,
    )
    arrived = lax.all_to_all(
        packed.reshape(PLANE, BLOCK, PLAIN * eighth), ("y", "xh", "xl"), 0, 0, tiled=True
    ).reshape(PLANE * BLOCK, PLAIN * eighth)
    beside = lax.ppermute(arrived, "c", SWAP)
    rows = PLANE * (BLOCK + ZLO)
    partial = jax.ShapeDtypeStruct((rows, hidden_count), F32)
    gate, up = call(
        functools.partial(own_kernel, quarter),
        (partial, partial),
        where, arrived, ring, w_gate, w_up,
    )
    pieces = jax.ShapeDtypeStruct((PLANE * BLOCK, width), BF16)
    hidden, away = call(
        functools.partial(other_kernel, quarter),
        (jax.ShapeDtypeStruct((rows, hidden_count), BF16), pieces),
        where, beside, ring_beside, w_gate, w_up, w_down, gate, up,
    )
    got = lax.ppermute(away, "c", SWAP)
    summed = call(
        functools.partial(sum_kernel, quarter),
        pieces,
        where, hidden, w_down, got,
    )
    returned = lax.all_to_all(
        summed.reshape(PLANE, BLOCK, width), ("y", "xh", "xl"), 0, 0, tiled=True
    ).reshape(PLANE * BLOCK, width)

    parts = call(
        functools.partial(combine_kernel, quarter),
        jax.ShapeDtypeStruct((ZALL, BLOCK, quarter), BF16),
        where, returned, marks,
    )
    parts = lax.all_to_all(parts, ("zl", "zh"), 0, 0, tiled=True)
    moe_out = jnp.sum(parts.astype(F32), axis=0)
    return (moe_out.astype(BF16), attn_out)


def solution(mesh):
    fine = Mesh(mesh.devices.reshape(4, 2, 2, 4, 2, 2), ("y", "xh", "xl", "zl", "zh", "c"))
    grp, tp = ("y", "xh", "xl", "zl"), ("zh", "c")
    every = grp + tp
    return jax.shard_map(
        shards,
        mesh=fine,
        in_specs=(
            P(grp, None),
            P(grp, None),
            P(),
            P(None, every),
            P(None, every),
            P(every, None),
            P(every, None),
            P(every, None, None),
            P(every),
        ),
        out_specs=(P(grp, tp), P(every, None)),
        check_vma=False,
    )
```

```python
import functools
import math

import jax
import jax.numpy as jnp
from jax import lax
from jax.experimental import pallas as pl
from jax.experimental.pallas import tpu as pltpu
from jax.sharding import Mesh
from jax.sharding import PartitionSpec as P

CAP = 5
ZLO = 4
ZALL = 8
EXPERTS = 8
BLOCK = 16
PLANE = 16
LANES = 128
REACH = (0, 1, 2, -1)
HIGH, LOW = 64, 72
BF16, F32 = jnp.bfloat16, jnp.float32
VMEM_BYTES = 40 * 1024 * 1024
ALL_VMEM_BYTES = 60 * 1024 * 1024


def place(z):
    return (z % ZLO) * 2 + z // ZLO


def z_pairs(step):
    return [(place(z), place((z + step) % ZALL)) for z in range(ZALL)]


SWAP = [(0, 1), (1, 0)]


def z_send(value, step):
    return lax.ppermute(value, ("zl", "zh"), z_pairs(step))


def grid(rows, columns):
    return (
        lax.broadcasted_iota(jnp.int32, (rows, columns), 0),
        lax.broadcasted_iota(jnp.int32, (rows, columns), 1),
    )


def fifth(value):
    return (value * 205) >> 10


def fifth_rest(value):
    return value - CAP * fifth(value)


def ones(condition):
    return jnp.where(condition, 1.0, 0.0)


def shuffle_table(back):
    new, old = grid(PLANE * BLOCK, PLANE * BLOCK)
    if back:
        new, old = old, new
    spot = ((old >> 2) & 3) * 64 + (old >> 4) * 4 + (old & 3)
    return ones(new == spot).astype(BF16)


def dot(a, b):
    return jnp.dot(a, b, preferred_element_type=F32)


def dot_t(a, b):
    return lax.dot_general(a, b, (((1,), (1,)), ((), ())), preferred_element_type=F32)


def scalars(array):
    return pl.BlockSpec(memory_space=pltpu.SMEM)


def call(kernel, out_shape, *args):
    at = [pl.BlockSpec(memory_space=pltpu.SMEM if a.dtype == jnp.int32 else pltpu.VMEM) for a in args]
    return pl.pallas_call(
        kernel,
        out_shape=out_shape,
        in_specs=at,
        out_specs=jax.tree.map(lambda _: pl.BlockSpec(memory_space=pltpu.VMEM), out_shape),
        compiler_params=pltpu.CompilerParams(vmem_limit_bytes=VMEM_BYTES),
    )(*args)


def rows_kernel(quarter, where, x_rows, ids, router, out):
    half = 2 * quarter
    values = x_rows[...].astype(F32)
    row, lane = grid(BLOCK, LANES)
    first, second = jnp.zeros_like(row), jnp.zeros_like(row)
    for r in range(BLOCK):
        first = jnp.where(row == r, ids[0, r], first)
        second = jnp.where(row == r, ids[1, r], second)
    squashed, total = [], 0.0
    for e in range(EXPERTS):
        logit = jnp.sum(values * router[e : e + 1, :], axis=1, keepdims=True)
        kept = jnp.where((first == e) | (second == e), jax.nn.sigmoid(logit), 0.0)
        squashed.append(kept)
        total = total + kept
    tail = jnp.zeros((BLOCK, LANES), F32)
    for e in range(EXPERTS):
        share = squashed[e] / total
        high = share.astype(BF16).astype(F32)
        low = (share - high).astype(BF16).astype(F32)
        tail = jnp.where(lane == HIGH + e, high, jnp.where(lane == LOW + e, low, tail))
    expert = fifth(lane)
    named = (first == expert) | (second == expert)
    row, column = grid(BLOCK, BLOCK)
    rank = dot(ones(row > column).astype(BF16), ones(named).astype(BF16))
    marks = ones(named & (rank == fifth_rest(lane).astype(F32)))
    tail = jnp.where(lane < EXPERTS * CAP, marks, tail)
    for f in range(2):
        at = pl.ds(pl.multiple_of(f * half + where[0] * quarter, LANES), quarter)
        out[:, f * quarter : (f + 1) * quarter] = x_rows[:, at]
    out[:, half:] = tail.astype(BF16)


def pack_kernel(quarter, *refs):
    blocks, (out, marks) = refs[:4], refs[4:]
    half = 2 * quarter
    eighth = quarter // 2
    rows = jnp.concatenate([b[:, :half] for b in blocks], axis=0)
    chosen = jnp.concatenate([b[:, half:] for b in blocks], axis=0)
    marks[...] = chosen
    lane = grid(ZLO * BLOCK, LANES)[1]
    chosen = jnp.where(lane < EXPERTS * CAP, chosen, jnp.zeros_like(chosen))
    slot, lane = grid(EXPERTS * BLOCK, LANES)
    same = fifth(lane) == slot >> 4
    pick_main = ones(same & (fifth_rest(lane) == fifth_rest(slot & 15))).astype(BF16)
    pick_rest = ones(same & (fifth_rest(lane) == 1 + (slot & 3))).astype(BF16)
    slot, row = grid(EXPERTS * BLOCK, ZLO * BLOCK)
    mask = ones(fifth(slot & 15) == row >> 4)
    main = dot((dot_t(pick_main, chosen) * mask).astype(BF16), rows)
    main = main.astype(BF16).reshape(EXPERTS, BLOCK, half)
    chosen4 = jnp.concatenate([chosen] * 4, axis=0)
    rows4 = jnp.concatenate([rows[:, i * eighth : (i + 1) * eighth] for i in range(4)], axis=0)
    slot, row = grid(EXPERTS * BLOCK, 4 * ZLO * BLOCK)
    mask = ones(((slot >> 2) & 3 == row >> 6) & ((row >> 4) & 3 == 3))
    rest = dot((dot_t(pick_rest, chosen4) * mask).astype(BF16), rows4)
    rest = rest.astype(BF16).reshape(EXPERTS, BLOCK, eighth)
    for x in range(2):
        out[:, x, :, :half] = main
        out[:, x, :, half:] = rest


def experts_in(quarter, core, block, w_gate, w_up):
    half = 2 * quarter
    rest = dot(shuffle_table(False), block[:, half:]).astype(BF16)
    gate, up = 0.0, 0.0
    for f in range(2):
        top = block[:, f * quarter : (f + 1) * quarter]
        tail = jnp.concatenate(
            [rest[(2 * f + i) * 64 : (2 * f + i + 1) * 64] for i in range(2)], axis=1
        )
        rows = jnp.concatenate([top, tail], axis=0)
        at = pl.ds(pl.multiple_of(f * half + core * quarter, LANES), quarter)
        gate = gate + dot_t(rows, w_gate[:, at])
        up = up + dot_t(rows, w_up[:, at])
    return gate, up


def columns(quarter, core, f):
    return pl.ds(pl.multiple_of(f * 2 * quarter + core * quarter, LANES), quarter)


def tails_out(quarter, core, hidden, w_down):
    tails = []
    for f in range(2):
        y = dot(hidden[PLANE * BLOCK :], w_down[:, columns(quarter, core, f)])
        tails += [y[:, : quarter // 2], y[:, quarter // 2 :]]
    return jnp.concatenate(tails, axis=0)


def own_kernel(quarter, core, block, w_gate, w_up, gate_out, up_out):
    gate, up = experts_in(quarter, core[0], block, w_gate, w_up)
    gate_out[...] = gate
    up_out[...] = up


def other_kernel(
    quarter, core, block, w_gate, w_up, w_down, gate_in, up_in, hidden_out, away
):
    there = 1 - core[0]
    gate, up = experts_in(quarter, there, block, w_gate, w_up)
    gate, up = gate + gate_in[...], up + up_in[...]
    hidden = (gate * jax.nn.sigmoid(gate) * up).astype(BF16)
    hidden_out[...] = hidden
    away[...] = dot(hidden[: PLANE * BLOCK], w_down[:, columns(quarter, there, 0)]).astype(BF16)


def away_kernel(quarter, where, hidden, w_down, away):
    there = 1 - where[0]
    main = dot(hidden[: PLANE * BLOCK, :], w_down[:, columns(quarter, there, 1)])
    away[:, :quarter] = main.astype(BF16)
    rest = tails_out(quarter, there, hidden[...], w_down).astype(BF16)
    away[:, quarter:] = dot(shuffle_table(True), rest).astype(BF16)


def sum_kernel(quarter, where, hidden, w_down, got_first, got_second, out):
    for f, got in enumerate((got_first, got_second)):
        main = dot(hidden[: PLANE * BLOCK, :], w_down[:, columns(quarter, where[0], f)])
        main = main + got[:, :quarter].astype(F32)
        out[:, f * quarter : (f + 1) * quarter] = main.astype(BF16)
    rest = tails_out(quarter, where[0], hidden[...], w_down)
    high = rest.astype(BF16)
    low = (rest - high.astype(F32)).astype(BF16)
    unshuffle = shuffle_table(True)
    rest = dot(unshuffle, high) + dot(unshuffle, low)
    out[:, 2 * quarter :] = (rest + got_second[:, quarter:].astype(F32)).astype(BF16)


def combine_kernel(quarter, where, back, marks, out):
    half = 2 * quarter
    chosen = marks[...]
    lane, slot = grid(LANES, PLANE * BLOCK)
    expert = slot >> 5
    same = fifth(lane) == expert
    back_main = ones(same & (fifth_rest(lane) == fifth_rest(slot & 15))).astype(BF16)
    back_rest = ones(same & (fifth_rest(lane) == 1 + (slot & 3))).astype(BF16)
    wide_high = dot(chosen, ones(lane == HIGH + expert).astype(BF16))
    wide_low = dot(chosen, ones(lane == LOW + expert).astype(BF16))
    row, slot = grid(ZLO * BLOCK, PLANE * BLOCK)
    main = dot(chosen, back_main) * ones(fifth(slot & 15) == row >> 4)
    rest = dot(chosen, back_rest) * ones(row >> 4 == 3)
    wides = (wide_high, wide_low)
    count = ZLO * BLOCK
    both = dot(jnp.concatenate([(main * w).astype(BF16) for w in wides], axis=0), back[:, :half])
    picked = [rest * ones((slot >> 2) & 3 == i) for i in range(4)]
    stack = jnp.concatenate([(p * w).astype(BF16) for p in picked for w in wides], axis=0)
    tails = dot(stack, back[:, half:])
    pieces = [
        tails[2 * i * count : (2 * i + 1) * count] + tails[(2 * i + 1) * count : (2 * i + 2) * count]
        for i in range(4)
    ]
    total = both[:count] + both[count:] + jnp.concatenate(pieces, axis=1)
    for k in range(ZLO):
        owner = (where[1] + (REACH[k] % ZLO)) & (ZLO - 1)
        for f in range(2):
            piece = total[k * BLOCK : (k + 1) * BLOCK, f * quarter : (f + 1) * quarter]
            out[owner * 2 + f] = piece.astype(BF16)


def attention_kernel(lengths, queries, cache, out):
    live_count = lengths[pl.program_id(0)]
    head_dim = queries.shape[2]
    scores = dot_t(queries[0], cache[0, :, :head_dim]) / math.sqrt(head_dim)
    live = lax.broadcasted_iota(jnp.int32, scores.shape, 1) < live_count
    scores = jnp.where(live, scores, -1e30)
    largest = jnp.max(scores, axis=1, keepdims=True)
    weights = jnp.where(live, jnp.exp(scores - largest), 0.0)
    denominator = jnp.sum(weights, axis=1, keepdims=True)
    mixed = dot(weights.astype(BF16), cache[0, :, head_dim:])
    out[0] = (mixed / denominator).astype(BF16)


def attention_block(queries, cache, lengths):
    requests, positions, both = cache.shape
    head_dim = both // 2
    heads = queries.shape[1] // head_dim
    rows = pl.BlockSpec((1, heads, head_dim), lambda i: (i, 0, 0))
    mixed = pl.pallas_call(
        attention_kernel,
        grid=(requests,),
        out_shape=jax.ShapeDtypeStruct((requests, heads, head_dim), BF16),
        in_specs=[
            scalars(lengths),
            rows,
            pl.BlockSpec((1, positions, both), lambda i: (i, 0, 0)),
        ],
        out_specs=rows,
        compiler_params=pltpu.CompilerParams(vmem_limit_bytes=ALL_VMEM_BYTES),
    )(lengths, queries.reshape(requests, heads, head_dim), cache)
    return mixed.reshape(queries.shape)


def shards(x_rows, route_ids, router, w_gate, w_up, w_down, queries, cache, lengths):
    model_width = x_rows.shape[1]
    hidden_count = w_gate.shape[1]
    w_gate, w_up = w_gate.T, w_up.T
    quarter = model_width // 4
    half, eighth = 2 * quarter, quarter // 2
    width = half + eighth
    where = jnp.stack([lax.axis_index("c"), lax.axis_index("zl")]).astype(jnp.int32)
    def whole(array):
        return pl.BlockSpec(array.shape, lambda i: (0, 0))

    payload = jax.ShapeDtypeStruct((BLOCK, half + LANES), BF16)
    payload = pl.pallas_call(
        functools.partial(rows_kernel, quarter),
        grid=(1,),
        out_shape=payload,
        in_specs=[scalars(where), whole(x_rows), scalars(route_ids), whole(router.T)],
        out_specs=whole(payload),
        compiler_params=pltpu.CompilerParams(vmem_limit_bytes=ALL_VMEM_BYTES),
    )(where, x_rows, route_ids.T, router.T)
    blocks = [payload] + [z_send(payload, -k) for k in REACH[1:]]

    payload, queries = lax.optimization_barrier((payload, queries))
    attn_out = attention_block(queries, cache, lengths)
    blocks, attn_out = lax.optimization_barrier((blocks, attn_out))
    packed, marks = call(
        functools.partial(pack_kernel, quarter),
        (
            jax.ShapeDtypeStruct((EXPERTS, 2, BLOCK, width), BF16),
            jax.ShapeDtypeStruct((ZLO * BLOCK, LANES), BF16),
        ),
        *blocks,
    )
    arrived = lax.all_to_all(
        packed.reshape(PLANE, BLOCK, width), ("y", "xh", "xl"), 0, 0, tiled=True
    ).reshape(PLANE * BLOCK, width)
    beside = lax.ppermute(arrived, "c", SWAP)
    rows = PLANE * (BLOCK + ZLO)
    partial = jax.ShapeDtypeStruct((rows, hidden_count), F32)
    gate, up = call(
        functools.partial(own_kernel, quarter),
        (partial, partial),
        where, arrived, w_gate, w_up,
    )
    main = PLANE * BLOCK
    hidden, away = call(
        functools.partial(other_kernel, quarter),
        (
            jax.ShapeDtypeStruct((rows, hidden_count), BF16),
            jax.ShapeDtypeStruct((main, quarter), BF16),
        ),
        where, beside, w_gate, w_up, w_down, gate, up,
    )
    got_first = lax.ppermute(away, "c", SWAP)
    away = call(
        functools.partial(away_kernel, quarter),
        jax.ShapeDtypeStruct((main, quarter + eighth), BF16),
        where, hidden, w_down,
    )
    got_second = lax.ppermute(away, "c", SWAP)
    summed = call(
        functools.partial(sum_kernel, quarter),
        jax.ShapeDtypeStruct((main, width), BF16),
        where, hidden, w_down, got_first, got_second,
    )
    returned = lax.all_to_all(
        summed.reshape(PLANE, BLOCK, width), ("y", "xh", "xl"), 0, 0, tiled=True
    ).reshape(PLANE * BLOCK, width)

    parts = call(
        functools.partial(combine_kernel, quarter),
        jax.ShapeDtypeStruct((ZALL, BLOCK, quarter), BF16),
        where, returned, marks,
    )
    parts = lax.all_to_all(parts, ("zl", "zh"), 0, 0, tiled=True)
    moe_out = jnp.sum(parts.astype(F32), axis=0)
    return (moe_out.astype(BF16), attn_out)


def solution(mesh):
    fine = Mesh(mesh.devices.reshape(4, 2, 2, 4, 2, 2), ("y", "xh", "xl", "zl", "zh", "c"))
    grp, tp = ("y", "xh", "xl", "zl"), ("zh", "c")
    every = grp + tp
    return jax.shard_map(
        shards,
        mesh=fine,
        in_specs=(
            P(grp, None),
            P(grp, None),
            P(),
            P(None, every),
            P(None, every),
            P(every, None),
            P(every, None),
            P(every, None, None),
            P(every),
        ),
        out_specs=(P(grp, tp), P(every, None)),
        check_vma=False,
    )
```

```python
import functools
import math

import jax
import jax.numpy as jnp
from jax import lax
from jax.experimental import pallas as pl
from jax.experimental.pallas import tpu as pltpu
from jax.sharding import Mesh
from jax.sharding import PartitionSpec as P

CAP = 5
ZLO = 4
ZALL = 8
EXPERTS = 8
BLOCK = 16
PLANE = 16
LANES = 128
REACH = (0, 1, 2, -1)
HIGH, LOW = 64, 72
BF16, F32 = jnp.bfloat16, jnp.float32
VMEM_BYTES = 40 * 1024 * 1024
ALL_VMEM_BYTES = 60 * 1024 * 1024


def place(z):
    return (z % ZLO) * 2 + z // ZLO


def z_pairs(step):
    return [(place(z), place((z + step) % ZALL)) for z in range(ZALL)]


SWAP = [(0, 1), (1, 0)]


def z_send(value, step):
    return lax.ppermute(value, ("zl", "zh"), z_pairs(step))


def grid(rows, columns):
    return (
        lax.broadcasted_iota(jnp.int32, (rows, columns), 0),
        lax.broadcasted_iota(jnp.int32, (rows, columns), 1),
    )


def fifth(value):
    return (value * 205) >> 10


def fifth_rest(value):
    return value - CAP * fifth(value)


def ones(condition):
    return jnp.where(condition, 1.0, 0.0)


def shuffle_table(back):
    new, old = grid(PLANE * BLOCK, PLANE * BLOCK)
    if back:
        new, old = old, new
    spot = ((old >> 2) & 3) * 64 + (old >> 4) * 4 + (old & 3)
    return ones(new == spot).astype(BF16)


def dot(a, b):
    return jnp.dot(a, b, preferred_element_type=F32)


def dot_t(a, b):
    return lax.dot_general(a, b, (((1,), (1,)), ((), ())), preferred_element_type=F32)


def scalars(array):
    return pl.BlockSpec(memory_space=pltpu.SMEM)


def call(kernel, out_shape, *args):
    return pl.pallas_call(
        kernel,
        out_shape=out_shape,
        in_specs=[pl.BlockSpec(memory_space=pltpu.VMEM)] * len(args),
        out_specs=jax.tree.map(lambda _: pl.BlockSpec(memory_space=pltpu.VMEM), out_shape),
        compiler_params=pltpu.CompilerParams(vmem_limit_bytes=VMEM_BYTES),
    )(*args)


def rows_kernel(quarter, x_rows, ids, router, out):
    half = 2 * quarter
    values = x_rows[...].astype(F32)
    row, lane = grid(BLOCK, LANES)
    first, second = jnp.zeros_like(row), jnp.zeros_like(row)
    for r in range(BLOCK):
        first = jnp.where(row == r, ids[0, r], first)
        second = jnp.where(row == r, ids[1, r], second)
    squashed, total = [], 0.0
    for e in range(EXPERTS):
        logit = jnp.sum(values * router[e : e + 1, :], axis=1, keepdims=True)
        kept = jnp.where((first == e) | (second == e), jax.nn.sigmoid(logit), 0.0)
        squashed.append(kept)
        total = total + kept
    tail = jnp.zeros((BLOCK, LANES), F32)
    for e in range(EXPERTS):
        share = squashed[e] / total
        high = share.astype(BF16).astype(F32)
        low = (share - high).astype(BF16).astype(F32)
        tail = jnp.where(lane == HIGH + e, high, jnp.where(lane == LOW + e, low, tail))
    expert = fifth(lane)
    named = (first == expert) | (second == expert)
    row, column = grid(BLOCK, BLOCK)
    rank = dot(ones(row > column).astype(BF16), ones(named).astype(BF16))
    marks = ones(named & (rank == fifth_rest(lane).astype(F32)))
    tail = jnp.where(lane < EXPERTS * CAP, marks, tail)
    for f in range(2):
        at = columns(quarter, lax.axis_index("c"), f)
        out[:, f * quarter : (f + 1) * quarter] = x_rows[:, at]
    out[:, half:] = tail.astype(BF16)


def pack_kernel(quarter, *refs):
    blocks, (out, marks) = refs[:4], refs[4:]
    half = 2 * quarter
    eighth = quarter // 2
    rows = jnp.concatenate([b[:, :half] for b in blocks], axis=0)
    chosen = jnp.concatenate([b[:, half:] for b in blocks], axis=0)
    marks[...] = chosen
    lane = grid(ZLO * BLOCK, LANES)[1]
    chosen = jnp.where(lane < EXPERTS * CAP, chosen, jnp.zeros_like(chosen))
    slot, lane = grid(EXPERTS * BLOCK, LANES)
    same = fifth(lane) == slot >> 4
    pick_main = ones(same & (fifth_rest(lane) == fifth_rest(slot & 15))).astype(BF16)
    pick_rest = ones(same & (fifth_rest(lane) == 1 + (slot & 3))).astype(BF16)
    slot, row = grid(EXPERTS * BLOCK, ZLO * BLOCK)
    mask = ones(fifth(slot & 15) == row >> 4)
    main = dot((dot_t(pick_main, chosen) * mask).astype(BF16), rows)
    main = main.astype(BF16).reshape(EXPERTS, BLOCK, half)
    chosen4 = jnp.concatenate([chosen] * 4, axis=0)
    rows4 = jnp.concatenate([rows[:, i * eighth : (i + 1) * eighth] for i in range(4)], axis=0)
    slot, row = grid(EXPERTS * BLOCK, 4 * ZLO * BLOCK)
    mask = ones(((slot >> 2) & 3 == row >> 6) & ((row >> 4) & 3 == 3))
    rest = dot((dot_t(pick_rest, chosen4) * mask).astype(BF16), rows4)
    rest = rest.astype(BF16).reshape(EXPERTS, BLOCK, eighth)
    for x in range(2):
        out[:, x, :, :half] = main
        out[:, x, :, half:] = rest


def experts_in(quarter, core, block, w_gate, w_up):
    half = 2 * quarter
    rest = dot(shuffle_table(False), block[:, half:]).astype(BF16)
    gate, up = 0.0, 0.0
    for f in range(2):
        top = block[:, f * quarter : (f + 1) * quarter]
        tail = jnp.concatenate(
            [rest[(2 * f + i) * 64 : (2 * f + i + 1) * 64] for i in range(2)], axis=1
        )
        rows = jnp.concatenate([top, tail], axis=0)
        at = pl.ds(pl.multiple_of(f * half + core * quarter, LANES), quarter)
        gate = gate + dot_t(rows, w_gate[:, at])
        up = up + dot_t(rows, w_up[:, at])
    return gate, up


def columns(quarter, core, f):
    return pl.ds(pl.multiple_of(f * 2 * quarter + core * quarter, LANES), quarter)


def tails_out(quarter, core, hidden, w_down):
    tails = []
    for f in range(2):
        y = dot(hidden[PLANE * BLOCK :], w_down[:, columns(quarter, core, f)])
        tails += [y[:, : quarter // 2], y[:, quarter // 2 :]]
    return jnp.concatenate(tails, axis=0)


def own_kernel(quarter, block, w_gate, w_up, gate_out, up_out):
    gate, up = experts_in(quarter, lax.axis_index("c"), block, w_gate, w_up)
    gate_out[...] = gate
    up_out[...] = up


def other_kernel(
    quarter, block, w_gate, w_up, w_down, gate_in, up_in, hidden_out, away
):
    there = 1 - lax.axis_index("c")
    gate, up = experts_in(quarter, there, block, w_gate, w_up)
    gate, up = gate + gate_in[...], up + up_in[...]
    hidden = (gate * jax.nn.sigmoid(gate) * up).astype(BF16)
    hidden_out[...] = hidden
    for f in range(2):
        main = dot(hidden[: PLANE * BLOCK], w_down[:, columns(quarter, there, f)])
        away[:, f * quarter : (f + 1) * quarter] = main.astype(BF16)
    rest = tails_out(quarter, there, hidden, w_down).astype(BF16)
    away[:, 2 * quarter :] = dot(shuffle_table(True), rest).astype(BF16)


def sum_kernel(quarter, hidden, w_down, got, out):
    core = lax.axis_index("c")
    for f in range(2):
        at = slice(f * quarter, (f + 1) * quarter)
        main = dot(hidden[: PLANE * BLOCK, :], w_down[:, columns(quarter, core, f)])
        out[:, at] = (main + got[:, at].astype(F32)).astype(BF16)
    rest = tails_out(quarter, core, hidden[...], w_down)
    high = rest.astype(BF16)
    low = (rest - high.astype(F32)).astype(BF16)
    unshuffle = shuffle_table(True)
    rest = dot(unshuffle, high) + dot(unshuffle, low)
    out[:, 2 * quarter :] = (rest + got[:, 2 * quarter :].astype(F32)).astype(BF16)


def combine_kernel(quarter, back, marks, out):
    half = 2 * quarter
    chosen = marks[...]
    lane, slot = grid(LANES, PLANE * BLOCK)
    expert = slot >> 5
    same = fifth(lane) == expert
    back_main = ones(same & (fifth_rest(lane) == fifth_rest(slot & 15))).astype(BF16)
    back_rest = ones(same & (fifth_rest(lane) == 1 + (slot & 3))).astype(BF16)
    wide_high = dot(chosen, ones(lane == HIGH + expert).astype(BF16))
    wide_low = dot(chosen, ones(lane == LOW + expert).astype(BF16))
    row, slot = grid(ZLO * BLOCK, PLANE * BLOCK)
    main = dot(chosen, back_main) * ones(fifth(slot & 15) == row >> 4)
    rest = dot(chosen, back_rest) * ones(row >> 4 == 3)
    wides = (wide_high, wide_low)
    count = ZLO * BLOCK
    both = dot(jnp.concatenate([(main * w).astype(BF16) for w in wides], axis=0), back[:, :half])
    picked = [rest * ones((slot >> 2) & 3 == i) for i in range(4)]
    stack = jnp.concatenate([(p * w).astype(BF16) for p in picked for w in wides], axis=0)
    tails = dot(stack, back[:, half:])
    pieces = [
        tails[2 * i * count : (2 * i + 1) * count] + tails[(2 * i + 1) * count : (2 * i + 2) * count]
        for i in range(4)
    ]
    total = both[:count] + both[count:] + jnp.concatenate(pieces, axis=1)
    for k in range(ZLO):
        owner = (lax.axis_index("zl") + (REACH[k] % ZLO)) & (ZLO - 1)
        for f in range(2):
            piece = total[k * BLOCK : (k + 1) * BLOCK, f * quarter : (f + 1) * quarter]
            out[owner * 2 + f] = piece.astype(BF16)


def attention_weights(queries, cache, lengths):
    head_dim = cache.shape[2] // 2
    heads = queries.shape[1] // head_dim
    query_heads = queries.reshape(queries.shape[0], heads, head_dim)
    scores = jnp.einsum(
        "bhd,bpd->bhp", query_heads, cache[:, :, :head_dim], preferred_element_type=F32
    ) / math.sqrt(head_dim)
    live = jnp.arange(cache.shape[1])[None, :] < lengths[:, None]
    scores = jnp.where(live[:, None, :], scores, -1e30)
    largest = jnp.max(scores, axis=2, keepdims=True)
    weights = jnp.where(live[:, None, :], jnp.exp(scores - largest), 0.0)
    return weights.astype(BF16), jnp.sum(weights, axis=2, keepdims=True)


def attention_mix(weights, denominator, cache):
    head_dim = cache.shape[2] // 2
    mixed = jnp.einsum(
        "bhp,bpd->bhd", weights, cache[:, :, head_dim:], preferred_element_type=F32
    )
    return (mixed / denominator).astype(BF16).reshape(cache.shape[0], -1)


def shards(x_rows, route_ids, router, w_gate, w_up, w_down, queries, cache, lengths):
    model_width = x_rows.shape[1]
    hidden_count = w_gate.shape[1]
    w_gate, w_up = w_gate.T, w_up.T
    quarter = model_width // 4
    half, eighth = 2 * quarter, quarter // 2
    width = half + eighth

    def whole(array):
        return pl.BlockSpec(array.shape, lambda i: (0, 0))

    payload = jax.ShapeDtypeStruct((BLOCK, half + LANES), BF16)
    payload = pl.pallas_call(
        functools.partial(rows_kernel, quarter),
        grid=(1,),
        out_shape=payload,
        in_specs=[whole(x_rows), scalars(route_ids), whole(router.T)],
        out_specs=whole(payload),
        compiler_params=pltpu.CompilerParams(vmem_limit_bytes=ALL_VMEM_BYTES),
    )(x_rows, route_ids.T, router.T)
    blocks = [payload] + [z_send(payload, -k) for k in REACH[1:]]

    payload, queries = lax.optimization_barrier((payload, queries))
    weights, denominator = attention_weights(queries, cache, lengths)
    blocks[0], weights, denominator = lax.optimization_barrier((payload, weights, denominator))
    packed, marks = call(
        functools.partial(pack_kernel, quarter),
        (
            jax.ShapeDtypeStruct((EXPERTS, 2, BLOCK, width), BF16),
            jax.ShapeDtypeStruct((ZLO * BLOCK, LANES), BF16),
        ),
        *blocks,
    )
    arrived = lax.all_to_all(
        packed.reshape(PLANE, BLOCK, width), ("y", "xh", "xl"), 0, 0, tiled=True
    ).reshape(PLANE * BLOCK, width)
    beside = lax.ppermute(arrived, "c", SWAP)
    rows = PLANE * (BLOCK + ZLO)
    partial = jax.ShapeDtypeStruct((rows, hidden_count), F32)
    gate, up = call(
        functools.partial(own_kernel, quarter),
        (partial, partial),
        arrived, w_gate, w_up,
    )
    pieces = jax.ShapeDtypeStruct((PLANE * BLOCK, width), BF16)
    hidden, away = call(
        functools.partial(other_kernel, quarter),
        (jax.ShapeDtypeStruct((rows, hidden_count), BF16), pieces),
        beside, w_gate, w_up, w_down, gate, up,
    )
    away, weights = lax.optimization_barrier((away, weights))
    attn_out = attention_mix(weights, denominator, cache)
    got = lax.ppermute(away, "c", SWAP)
    hidden, attn_out = lax.optimization_barrier((hidden, attn_out))
    summed = call(functools.partial(sum_kernel, quarter), pieces, hidden, w_down, got)
    returned = lax.all_to_all(
        summed.reshape(PLANE, BLOCK, width), ("y", "xh", "xl"), 0, 0, tiled=True
    ).reshape(PLANE * BLOCK, width)

    parts = call(
        functools.partial(combine_kernel, quarter),
        jax.ShapeDtypeStruct((ZALL, BLOCK, quarter), BF16),
        returned, marks,
    )
    parts = lax.all_to_all(parts, ("zl", "zh"), 0, 0, tiled=True)
    moe_out = jnp.sum(parts.astype(F32), axis=0)
    return (moe_out.astype(BF16), attn_out)


def solution(mesh):
    fine = Mesh(mesh.devices.reshape(4, 2, 2, 4, 2, 2), ("y", "xh", "xl", "zl", "zh", "c"))
    grp, tp = ("y", "xh", "xl", "zl"), ("zh", "c")
    every = grp + tp
    return jax.shard_map(
        shards,
        mesh=fine,
        in_specs=(
            P(grp, None),
            P(grp, None),
            P(),
            P(None, every),
            P(None, every),
            P(every, None),
            P(every, None),
            P(every, None, None),
            P(every),
        ),
        out_specs=(P(grp, tp), P(every, None)),
        check_vma=False,
    )
```

```python
import functools
import math

import jax
import jax.numpy as jnp
from jax import lax
from jax.experimental import pallas as pl
from jax.experimental.pallas import tpu as pltpu
from jax.sharding import Mesh
from jax.sharding import PartitionSpec as P

CAP = 5
ZLO = 4
ZALL = 8
EXPERTS = 8
BLOCK = 16
PLANE = 16
LANES = 128
REACH = (0, 1, 2, -1)
HIGH, LOW = 64, 72
BF16, F32 = jnp.bfloat16, jnp.float32
VMEM_BYTES = 40 * 1024 * 1024
ALL_VMEM_BYTES = 60 * 1024 * 1024


def place(z):
    return (z % ZLO) * 2 + z // ZLO


def z_pairs(step):
    return [(place(z), place((z + step) % ZALL)) for z in range(ZALL)]


SWAP = [(0, 1), (1, 0)]


def z_send(value, step):
    return lax.ppermute(value, ("zl", "zh"), z_pairs(step))


def z_send_apart(value, step):
    both = [[(2 * a + c, 2 * b + c) for a, b in z_pairs(way)] for c, way in enumerate((step, -step))]
    return lax.ppermute(value, ("zl", "zh", "c"), both[0] + both[1])


def grid(rows, columns):
    return (
        lax.broadcasted_iota(jnp.int32, (rows, columns), 0),
        lax.broadcasted_iota(jnp.int32, (rows, columns), 1),
    )


def fifth(value):
    return (value * 205) >> 10


def fifth_rest(value):
    return value - CAP * fifth(value)


def ones(condition):
    return jnp.where(condition, 1.0, 0.0)


def shuffle_table(back):
    new, old = grid(PLANE * BLOCK, PLANE * BLOCK)
    if back:
        new, old = old, new
    spot = ((old >> 2) & 3) * 64 + (old >> 4) * 4 + (old & 3)
    return ones(new == spot).astype(BF16)


def dot(a, b):
    return jnp.dot(a, b, preferred_element_type=F32)


def dot_t(a, b):
    return lax.dot_general(a, b, (((1,), (1,)), ((), ())), preferred_element_type=F32)


def call(kernel, out_shape, *args):
    return pl.pallas_call(
        kernel,
        out_shape=out_shape,
        in_specs=[pl.BlockSpec(memory_space=pltpu.VMEM)] * len(args),
        out_specs=jax.tree.map(lambda _: pl.BlockSpec(memory_space=pltpu.VMEM), out_shape),
        compiler_params=pltpu.CompilerParams(vmem_limit_bytes=VMEM_BYTES),
    )(*args)


def rows_kernel(quarter, x_far, ids_far, router_far, out, x_rows, ids, router, arrived):
    half = 2 * quarter
    loads = [
        pltpu.make_async_copy(source, target, arrived.at[i])
        for i, (source, target) in enumerate(
            ((x_far, x_rows), (router_far, router), (ids_far, ids))
        )
    ]
    for load in loads:
        load.start()
    for load in loads:
        load.wait()
    values = x_rows[...].astype(F32)
    row, lane = grid(BLOCK, LANES)
    first, second = jnp.zeros_like(row), jnp.zeros_like(row)
    for r in range(BLOCK):
        first = jnp.where(row == r, ids[0, r], first)
        second = jnp.where(row == r, ids[1, r], second)
    squashed, total = [], 0.0
    for e in range(EXPERTS):
        logit = jnp.sum(values * router[e : e + 1, :], axis=1, keepdims=True)
        kept = jnp.where((first == e) | (second == e), jax.nn.sigmoid(logit), 0.0)
        squashed.append(kept)
        total = total + kept
    tail = jnp.zeros((BLOCK, LANES), F32)
    for e in range(EXPERTS):
        share = squashed[e] / total
        high = share.astype(BF16).astype(F32)
        low = (share - high).astype(BF16).astype(F32)
        tail = jnp.where(lane == HIGH + e, high, jnp.where(lane == LOW + e, low, tail))
    expert = fifth(lane)
    named = (first == expert) | (second == expert)
    row, column = grid(BLOCK, BLOCK)
    rank = dot(ones(row > column).astype(BF16), ones(named).astype(BF16))
    marks = ones(named & (rank == fifth_rest(lane).astype(F32)))
    tail = jnp.where(lane < EXPERTS * CAP, marks, tail)
    for f in range(2):
        at = columns(quarter, lax.axis_index("c"), f)
        out[:, f * quarter : (f + 1) * quarter] = x_rows[:, at]
    out[:, half:] = tail.astype(BF16)


def pack_kernel(quarter, *refs):
    blocks, (out, marks) = refs[:4], refs[4:]
    half = 2 * quarter
    eighth = quarter // 2
    rows = jnp.concatenate([b[:, :half] for b in blocks], axis=0)
    chosen = jnp.concatenate([b[:, half:] for b in blocks], axis=0)
    marks[...] = chosen
    lane = grid(ZLO * BLOCK, LANES)[1]
    chosen = jnp.where(lane < EXPERTS * CAP, chosen, jnp.zeros_like(chosen))
    slot, lane = grid(EXPERTS * BLOCK, LANES)
    same = fifth(lane) == slot >> 4
    pick_main = ones(same & (fifth_rest(lane) == fifth_rest(slot & 15))).astype(BF16)
    pick_rest = ones(same & (fifth_rest(lane) == 1 + (slot & 3))).astype(BF16)
    slot, row = grid(EXPERTS * BLOCK, ZLO * BLOCK)
    mask = ones(fifth(slot & 15) == row >> 4)
    main = dot((dot_t(pick_main, chosen) * mask).astype(BF16), rows)
    main = main.astype(BF16).reshape(EXPERTS, BLOCK, half)
    chosen4 = jnp.concatenate([chosen] * 4, axis=0)
    rows4 = jnp.concatenate([rows[:, i * eighth : (i + 1) * eighth] for i in range(4)], axis=0)
    slot, row = grid(EXPERTS * BLOCK, 4 * ZLO * BLOCK)
    mask = ones(((slot >> 2) & 3 == row >> 6) & ((row >> 4) & 3 == 3))
    rest = dot((dot_t(pick_rest, chosen4) * mask).astype(BF16), rows4)
    rest = rest.astype(BF16).reshape(EXPERTS, BLOCK, eighth)
    for x in range(2):
        out[:, x, :, :half] = main
        out[:, x, :, half:] = rest


def experts_in(quarter, core, block, w_gate, w_up):
    half = 2 * quarter
    rest = dot(shuffle_table(False), block[:, half:]).astype(BF16)
    gate, up = 0.0, 0.0
    for f in range(2):
        top = block[:, f * quarter : (f + 1) * quarter]
        tail = jnp.concatenate(
            [rest[(2 * f + i) * 64 : (2 * f + i + 1) * 64] for i in range(2)], axis=1
        )
        rows = jnp.concatenate([top, tail], axis=0)
        at = pl.ds(pl.multiple_of(f * half + core * quarter, LANES), quarter)
        gate = gate + dot_t(rows, w_gate[:, at])
        up = up + dot_t(rows, w_up[:, at])
    return gate, up


def columns(quarter, core, f):
    return pl.ds(pl.multiple_of(f * 2 * quarter + core * quarter, LANES), quarter)


def tails_out(quarter, core, hidden, w_down):
    tails = []
    for f in range(2):
        y = dot(hidden[PLANE * BLOCK :], w_down[:, columns(quarter, core, f)])
        tails += [y[:, : quarter // 2], y[:, quarter // 2 :]]
    return jnp.concatenate(tails, axis=0)


def own_kernel(quarter, block, w_gate, w_up, gate_out, up_out):
    gate, up = experts_in(quarter, lax.axis_index("c"), block, w_gate, w_up)
    gate_out[...] = gate
    up_out[...] = up


def other_kernel(
    quarter, block, w_gate, w_up, w_down, gate_in, up_in, hidden_out, away
):
    there = 1 - lax.axis_index("c")
    gate, up = experts_in(quarter, there, block, w_gate, w_up)
    gate, up = gate + gate_in[...], up + up_in[...]
    hidden = (gate * jax.nn.sigmoid(gate) * up).astype(BF16)
    hidden_out[...] = hidden
    for f in range(2):
        main = dot(hidden[: PLANE * BLOCK], w_down[:, columns(quarter, there, f)])
        away[:, f * quarter : (f + 1) * quarter] = main.astype(BF16)
    rest = tails_out(quarter, there, hidden, w_down).astype(BF16)
    away[:, 2 * quarter :] = dot(shuffle_table(True), rest).astype(BF16)


def sum_kernel(quarter, hidden, w_down, got, out):
    core = lax.axis_index("c")
    for f in range(2):
        at = slice(f * quarter, (f + 1) * quarter)
        main = dot(hidden[: PLANE * BLOCK, :], w_down[:, columns(quarter, core, f)])
        out[:, at] = (main + got[:, at].astype(F32)).astype(BF16)
    rest = tails_out(quarter, core, hidden[...], w_down)
    high = rest.astype(BF16)
    low = (rest - high.astype(F32)).astype(BF16)
    unshuffle = shuffle_table(True)
    rest = dot(unshuffle, high) + dot(unshuffle, low)
    out[:, 2 * quarter :] = (rest + got[:, 2 * quarter :].astype(F32)).astype(BF16)


def combine_kernel(quarter, back, marks, out):
    half = 2 * quarter
    chosen = marks[...]
    lane, slot = grid(LANES, PLANE * BLOCK)
    expert = slot >> 5
    same = fifth(lane) == expert
    back_main = ones(same & (fifth_rest(lane) == fifth_rest(slot & 15))).astype(BF16)
    back_rest = ones(same & (fifth_rest(lane) == 1 + (slot & 3))).astype(BF16)
    wide_high = dot(chosen, ones(lane == HIGH + expert).astype(BF16))
    wide_low = dot(chosen, ones(lane == LOW + expert).astype(BF16))
    row, slot = grid(ZLO * BLOCK, PLANE * BLOCK)
    main = dot(chosen, back_main) * ones(fifth(slot & 15) == row >> 4)
    rest = dot(chosen, back_rest) * ones(row >> 4 == 3)
    wides = (wide_high, wide_low)
    count = ZLO * BLOCK
    both = dot(jnp.concatenate([(main * w).astype(BF16) for w in wides], axis=0), back[:, :half])
    picked = [rest * ones((slot >> 2) & 3 == i) for i in range(4)]
    stack = jnp.concatenate([(p * w).astype(BF16) for p in picked for w in wides], axis=0)
    tails = dot(stack, back[:, half:])
    pieces = [
        tails[2 * i * count : (2 * i + 1) * count] + tails[(2 * i + 1) * count : (2 * i + 2) * count]
        for i in range(4)
    ]
    total = both[:count] + both[count:] + jnp.concatenate(pieces, axis=1)
    for k in range(ZLO):
        owner = (lax.axis_index("zl") + (REACH[k] % ZLO)) & (ZLO - 1)
        for f in range(2):
            piece = total[k * BLOCK : (k + 1) * BLOCK, f * quarter : (f + 1) * quarter]
            out[owner * 2 + f] = piece.astype(BF16)


def attention_weights(queries, cache, lengths):
    head_dim = cache.shape[2] // 2
    heads = queries.shape[1] // head_dim
    query_heads = queries.reshape(queries.shape[0], heads, head_dim)
    scores = jnp.einsum(
        "bhd,bpd->bhp", query_heads, cache[:, :, :head_dim], preferred_element_type=F32
    ) / math.sqrt(head_dim)
    live = jnp.arange(cache.shape[1])[None, :] < lengths[:, None]
    scores = jnp.where(live[:, None, :], scores, -1e30)
    largest = jnp.max(scores, axis=2, keepdims=True)
    weights = jnp.where(live[:, None, :], jnp.exp(scores - largest), 0.0)
    return weights.astype(BF16), jnp.sum(weights, axis=2, keepdims=True)


def attention_mix(weights, denominator, cache):
    head_dim = cache.shape[2] // 2
    mixed = jnp.einsum(
        "bhp,bpd->bhd", weights, cache[:, :, head_dim:], preferred_element_type=F32
    )
    return (mixed / denominator).astype(BF16).reshape(cache.shape[0], -1)


def shards(x_rows, route_ids, router, w_gate, w_up, w_down, queries, cache, lengths):
    model_width = x_rows.shape[1]
    hidden_count = w_gate.shape[1]
    w_gate, w_up = w_gate.T, w_up.T
    quarter = model_width // 4
    half, eighth = 2 * quarter, quarter // 2
    width = half + eighth

    far = pl.BlockSpec(memory_space=pl.ANY)
    payload = pl.pallas_call(
        functools.partial(rows_kernel, quarter),
        out_shape=jax.ShapeDtypeStruct((BLOCK, half + LANES), BF16),
        in_specs=[far, far, far],
        out_specs=pl.BlockSpec(memory_space=pltpu.VMEM),
        scratch_shapes=[
            pltpu.VMEM(x_rows.shape, BF16),
            pltpu.SMEM(route_ids.T.shape, jnp.int32),
            pltpu.VMEM(router.T.shape, F32),
            pltpu.SemaphoreType.DMA((3,)),
        ],
        compiler_params=pltpu.CompilerParams(vmem_limit_bytes=ALL_VMEM_BYTES),
    )(x_rows, route_ids.T, router.T)
    blocks = [payload, z_send(payload, -1), z_send_apart(payload, -2), z_send(payload, 1)]

    payload, queries = lax.optimization_barrier((payload, queries))
    weights, denominator = attention_weights(queries, cache, lengths)
    blocks[0], weights, denominator = lax.optimization_barrier((payload, weights, denominator))
    packed, marks = call(
        functools.partial(pack_kernel, quarter),
        (
            jax.ShapeDtypeStruct((EXPERTS, 2, BLOCK, width), BF16),
            jax.ShapeDtypeStruct((ZLO * BLOCK, LANES), BF16),
        ),
        *blocks,
    )
    arrived = lax.all_to_all(
        packed.reshape(PLANE, BLOCK, width), ("y", "xh", "xl"), 0, 0, tiled=True
    ).reshape(PLANE * BLOCK, width)
    beside = lax.ppermute(arrived, "c", SWAP)
    rows = PLANE * (BLOCK + ZLO)
    partial = jax.ShapeDtypeStruct((rows, hidden_count), F32)
    gate, up = call(
        functools.partial(own_kernel, quarter),
        (partial, partial),
        arrived, w_gate, w_up,
    )
    pieces = jax.ShapeDtypeStruct((PLANE * BLOCK, width), BF16)
    hidden, away = call(
        functools.partial(other_kernel, quarter),
        (jax.ShapeDtypeStruct((rows, hidden_count), BF16), pieces),
        beside, w_gate, w_up, w_down, gate, up,
    )
    away, weights = lax.optimization_barrier((away, weights))
    attn_out = attention_mix(weights, denominator, cache)
    got = lax.ppermute(away, "c", SWAP)
    hidden, attn_out = lax.optimization_barrier((hidden, attn_out))
    summed = call(functools.partial(sum_kernel, quarter), pieces, hidden, w_down, got)
    returned = lax.all_to_all(
        summed.reshape(PLANE, BLOCK, width), ("y", "xh", "xl"), 0, 0, tiled=True
    ).reshape(PLANE * BLOCK, width)

    parts = call(
        functools.partial(combine_kernel, quarter),
        jax.ShapeDtypeStruct((ZALL, BLOCK, quarter), BF16),
        returned, marks,
    )
    parts = lax.all_to_all(parts, ("zl", "zh"), 0, 0, tiled=True)
    moe_out = jnp.sum(parts.astype(F32), axis=0)
    return (moe_out.astype(BF16), attn_out)


def solution(mesh):
    fine = Mesh(mesh.devices.reshape(4, 2, 2, 4, 2, 2), ("y", "xh", "xl", "zl", "zh", "c"))
    grp, tp = ("y", "xh", "xl", "zl"), ("zh", "c")
    every = grp + tp
    return jax.shard_map(
        shards,
        mesh=fine,
        in_specs=(
            P(grp, None),
            P(grp, None),
            P(),
            P(None, every),
            P(None, every),
            P(every, None),
            P(every, None),
            P(every, None, None),
            P(every),
        ),
        out_specs=(P(grp, tp), P(every, None)),
        check_vma=False,
    )
```

```python
import functools
import math

import jax
import jax.numpy as jnp
from jax import lax
from jax.experimental import pallas as pl
from jax.experimental.pallas import tpu as pltpu
from jax.sharding import Mesh
from jax.sharding import PartitionSpec as P

CAP = 5
ZLO = 4
ZALL = 8
EXPERTS = 8
BLOCK = 16
PLANE = 16
LANES = 128
REACH = (0, 1, 2, -1)
HIGH, LOW = 64, 72
BF16, F32 = jnp.bfloat16, jnp.float32
VMEM_BYTES = 24 * 1024 * 1024
ALL_VMEM_BYTES = 60 * 1024 * 1024


def place(z):
    return (z % ZLO) * 2 + z // ZLO


def z_pairs(step):
    return [(place(z), place((z + step) % ZALL)) for z in range(ZALL)]


SWAP = [(0, 1), (1, 0)]


def z_send(value, step):
    return lax.ppermute(value, ("zl", "zh"), z_pairs(step))


def z_send_apart(value, step):
    both = [[(2 * a + c, 2 * b + c) for a, b in z_pairs(way)] for c, way in enumerate((step, -step))]
    return lax.ppermute(value, ("zl", "zh", "c"), both[0] + both[1])


def grid(rows, columns):
    return (
        lax.broadcasted_iota(jnp.int32, (rows, columns), 0),
        lax.broadcasted_iota(jnp.int32, (rows, columns), 1),
    )


def fifth(value):
    return (value * 205) >> 10


def fifth_rest(value):
    return value - CAP * fifth(value)


def ones(condition):
    return jnp.where(condition, 1.0, 0.0)


def shuffle_table(back):
    new, old = grid(PLANE * BLOCK, PLANE * BLOCK)
    if back:
        new, old = old, new
    spot = ((old >> 2) & 3) * 64 + (old >> 4) * 4 + (old & 3)
    return ones(new == spot).astype(BF16)


def dot(a, b):
    return jnp.dot(a, b, preferred_element_type=F32)


def dot_t(a, b):
    return lax.dot_general(a, b, (((1,), (1,)), ((), ())), preferred_element_type=F32)


def call(kernel, out_shape, *args):
    return pl.pallas_call(
        kernel,
        out_shape=out_shape,
        in_specs=[pl.BlockSpec(memory_space=pltpu.VMEM)] * len(args),
        out_specs=jax.tree.map(lambda _: pl.BlockSpec(memory_space=pltpu.VMEM), out_shape),
        compiler_params=pltpu.CompilerParams(vmem_limit_bytes=VMEM_BYTES),
    )(*args)


def rows_kernel(quarter, x_far, ids_far, router_far, out, x_rows, ids, router, arrived):
    half = 2 * quarter
    loads = [
        pltpu.make_async_copy(source, target, arrived.at[i])
        for i, (source, target) in enumerate(
            ((x_far, x_rows), (router_far, router), (ids_far, ids))
        )
    ]
    for load in loads:
        load.start()
    for load in loads:
        load.wait()
    values = x_rows[...].astype(F32)
    row, lane = grid(BLOCK, LANES)
    first, second = jnp.zeros_like(row), jnp.zeros_like(row)
    for r in range(BLOCK):
        first = jnp.where(row == r, ids[0, r], first)
        second = jnp.where(row == r, ids[1, r], second)
    squashed, total = [], 0.0
    for e in range(EXPERTS):
        logit = jnp.sum(values * router[e : e + 1, :], axis=1, keepdims=True)
        kept = jnp.where((first == e) | (second == e), jax.nn.sigmoid(logit), 0.0)
        squashed.append(kept)
        total = total + kept
    tail = jnp.zeros((BLOCK, LANES), F32)
    for e in range(EXPERTS):
        share = squashed[e] / total
        high = share.astype(BF16).astype(F32)
        low = (share - high).astype(BF16).astype(F32)
        tail = jnp.where(lane == HIGH + e, high, jnp.where(lane == LOW + e, low, tail))
    expert = fifth(lane)
    named = (first == expert) | (second == expert)
    row, column = grid(BLOCK, BLOCK)
    rank = dot(ones(row > column).astype(BF16), ones(named).astype(BF16))
    marks = ones(named & (rank == fifth_rest(lane).astype(F32)))
    tail = jnp.where(lane < EXPERTS * CAP, marks, tail)
    for f in range(2):
        at = columns(quarter, lax.axis_index("c"), f)
        out[:, f * quarter : (f + 1) * quarter] = x_rows[:, at]
    out[:, half:] = tail.astype(BF16)


def pack_kernel(quarter, *refs):
    blocks, (out, marks) = refs[:4], refs[4:]
    half = 2 * quarter
    eighth = quarter // 2
    rows = jnp.concatenate([b[:, :half] for b in blocks], axis=0)
    chosen = jnp.concatenate([b[:, half:] for b in blocks], axis=0)
    marks[...] = chosen
    lane = grid(ZLO * BLOCK, LANES)[1]
    chosen = jnp.where(lane < EXPERTS * CAP, chosen, jnp.zeros_like(chosen))
    slot, lane = grid(EXPERTS * BLOCK, LANES)
    same = fifth(lane) == slot >> 4
    pick_main = ones(same & (fifth_rest(lane) == fifth_rest(slot & 15))).astype(BF16)
    pick_rest = ones(same & (fifth_rest(lane) == 1 + (slot & 3))).astype(BF16)
    slot, row = grid(EXPERTS * BLOCK, ZLO * BLOCK)
    mask = ones(fifth(slot & 15) == row >> 4)
    main = dot((dot_t(pick_main, chosen) * mask).astype(BF16), rows)
    main = main.astype(BF16).reshape(EXPERTS, BLOCK, half)
    chosen4 = jnp.concatenate([chosen] * 4, axis=0)
    rows4 = jnp.concatenate([rows[:, i * eighth : (i + 1) * eighth] for i in range(4)], axis=0)
    slot, row = grid(EXPERTS * BLOCK, 4 * ZLO * BLOCK)
    mask = ones(((slot >> 2) & 3 == row >> 6) & ((row >> 4) & 3 == 3))
    rest = dot((dot_t(pick_rest, chosen4) * mask).astype(BF16), rows4)
    rest = rest.astype(BF16).reshape(EXPERTS, BLOCK, eighth)
    for x in range(2):
        out[:, x, :, :half] = main
        out[:, x, :, half:] = rest


def columns(quarter, core, f):
    return pl.ds(pl.multiple_of(f * 2 * quarter + core * quarter, LANES), quarter)


def expert_rows(quarter, block, f):
    rest = dot(shuffle_table(False), block[:, 2 * quarter :]).astype(BF16)
    top = block[:, f * quarter : (f + 1) * quarter]
    tail = [rest[(2 * f + i) * 64 : (2 * f + i + 1) * 64] for i in range(2)]
    return jnp.concatenate([top, jnp.concatenate(tail, axis=1)], axis=0)


def inner_kernel(quarter, block, w_gate, w_up, other_gate, other_up, mine, theirs):
    core = lax.axis_index("c")
    rows = [expert_rows(quarter, block, f) for f in range(2)]
    for out, weights in ((theirs, (other_gate, other_up)), (mine, (w_gate, w_up))):
        for i, weight in enumerate(weights):
            out[i, :, LANES:] = jnp.zeros((out.shape[1], out.shape[2] - LANES), F32)
            out[i, :, : weight.shape[0]] = dot_t(
                rows[0], weight[:, columns(quarter, core, 0)]
            ) + dot_t(rows[1], weight[:, columns(quarter, core, 1)])


def hidden_kernel(mine, got, hidden):
    count = hidden.shape[1]
    gate, up = (mine[i, :, :count] + got[i, :, :count] for i in range(2))
    hidden[...] = (gate * jax.nn.sigmoid(gate) * up).astype(BF16)


def outer_kernel(quarter, hidden, other_hidden, w_down, other_down, out):
    core = lax.axis_index("c")
    main = PLANE * BLOCK
    tails = []
    for f in range(2):
        at = columns(quarter, core, f)
        y = dot(hidden[...], w_down[:, at]) + dot(other_hidden[...], other_down[:, at])
        y = y.astype(BF16)
        out[:, f * quarter : (f + 1) * quarter] = y[:main]
        tails += [y[main:, : quarter // 2], y[main:, quarter // 2 :]]
    tails = jnp.concatenate(tails, axis=0)
    out[:, 2 * quarter :] = dot(shuffle_table(True), tails).astype(BF16)


def combine_kernel(quarter, back, marks, out):
    half = 2 * quarter
    chosen = marks[...]
    lane, slot = grid(LANES, PLANE * BLOCK)
    expert = slot >> 5
    same = fifth(lane) == expert
    back_main = ones(same & (fifth_rest(lane) == fifth_rest(slot & 15))).astype(BF16)
    back_rest = ones(same & (fifth_rest(lane) == 1 + (slot & 3))).astype(BF16)
    wide_high = dot(chosen, ones(lane == HIGH + expert).astype(BF16))
    wide_low = dot(chosen, ones(lane == LOW + expert).astype(BF16))
    row, slot = grid(ZLO * BLOCK, PLANE * BLOCK)
    main = dot(chosen, back_main) * ones(fifth(slot & 15) == row >> 4)
    rest = dot(chosen, back_rest) * ones(row >> 4 == 3)
    wides = (wide_high, wide_low)
    count = ZLO * BLOCK
    both = dot(jnp.concatenate([(main * w).astype(BF16) for w in wides], axis=0), back[:, :half])
    picked = [rest * ones((slot >> 2) & 3 == i) for i in range(4)]
    stack = jnp.concatenate([(p * w).astype(BF16) for p in picked for w in wides], axis=0)
    tails = dot(stack, back[:, half:])
    pieces = [
        tails[2 * i * count : (2 * i + 1) * count] + tails[(2 * i + 1) * count : (2 * i + 2) * count]
        for i in range(4)
    ]
    total = both[:count] + both[count:] + jnp.concatenate(pieces, axis=1)
    for k in range(ZLO):
        owner = (lax.axis_index("zl") + (REACH[k] % ZLO)) & (ZLO - 1)
        for f in range(2):
            piece = total[k * BLOCK : (k + 1) * BLOCK, f * quarter : (f + 1) * quarter]
            out[owner * 2 + f] = piece.astype(BF16)


def attention_weights(queries, cache, lengths):
    head_dim = cache.shape[2] // 2
    heads = queries.shape[1] // head_dim
    query_heads = queries.reshape(queries.shape[0], heads, head_dim)
    scores = jnp.einsum(
        "bhd,bpd->bhp", query_heads, cache[:, :, :head_dim], preferred_element_type=F32
    ) / math.sqrt(head_dim)
    live = jnp.arange(cache.shape[1])[None, :] < lengths[:, None]
    scores = jnp.where(live[:, None, :], scores, -1e30)
    largest = jnp.max(scores, axis=2, keepdims=True)
    weights = jnp.where(live[:, None, :], jnp.exp(scores - largest), 0.0)
    return weights.astype(BF16), jnp.sum(weights, axis=2, keepdims=True)


def attention_mix(weights, denominator, cache):
    head_dim = cache.shape[2] // 2
    mixed = jnp.einsum(
        "bhp,bpd->bhd", weights, cache[:, :, head_dim:], preferred_element_type=F32
    )
    return (mixed / denominator).astype(BF16).reshape(cache.shape[0], -1)


def shards(x_rows, route_ids, router, w_gate, w_up, w_down, queries, cache, lengths):
    model_width = x_rows.shape[1]
    hidden_count = w_gate.shape[1]
    w_gate, w_up = w_gate.T, w_up.T
    other_gate, other_up, other_down = (lax.ppermute(w, "c", SWAP) for w in (w_gate, w_up, w_down))
    quarter = model_width // 4
    half, eighth = 2 * quarter, quarter // 2
    width = half + eighth

    far = pl.BlockSpec(memory_space=pl.ANY)
    payload = pl.pallas_call(
        functools.partial(rows_kernel, quarter),
        out_shape=jax.ShapeDtypeStruct((BLOCK, half + LANES), BF16),
        in_specs=[far, far, far],
        out_specs=pl.BlockSpec(memory_space=pltpu.VMEM),
        scratch_shapes=[
            pltpu.VMEM(x_rows.shape, BF16),
            pltpu.SMEM(route_ids.T.shape, jnp.int32),
            pltpu.VMEM(router.T.shape, F32),
            pltpu.SemaphoreType.DMA((3,)),
        ],
        compiler_params=pltpu.CompilerParams(vmem_limit_bytes=ALL_VMEM_BYTES),
    )(x_rows, route_ids.T, router.T)
    blocks = [payload, z_send(payload, -1), z_send_apart(payload, -2), z_send(payload, 1)]

    payload, queries = lax.optimization_barrier((payload, queries))
    weights, denominator = attention_weights(queries, cache, lengths)
    blocks[0], weights, denominator = lax.optimization_barrier((payload, weights, denominator))
    packed, marks = call(
        functools.partial(pack_kernel, quarter),
        (
            jax.ShapeDtypeStruct((EXPERTS, 2, BLOCK, width), BF16),
            jax.ShapeDtypeStruct((ZLO * BLOCK, LANES), BF16),
        ),
        *blocks,
    )
    arrived = lax.all_to_all(
        packed.reshape(PLANE, BLOCK, width), ("y", "xh", "xl"), 0, 0, tiled=True
    ).reshape(PLANE * BLOCK, width)
    rows = PLANE * (BLOCK + ZLO)
    wide = -(-hidden_count // (2 * LANES)) * 2 * LANES
    sums = jax.ShapeDtypeStruct((2, rows, wide), F32)
    mine, theirs = call(
        functools.partial(inner_kernel, quarter),
        (sums, sums),
        arrived, w_gate, w_up, other_gate, other_up,
    )
    theirs, weights = lax.optimization_barrier((theirs, weights))
    attn_out = attention_mix(weights, denominator, cache)
    got = lax.ppermute(theirs, "c", SWAP)
    mine, attn_out = lax.optimization_barrier((mine, attn_out))
    hidden = call(hidden_kernel, jax.ShapeDtypeStruct((rows, hidden_count), BF16), mine, got)
    summed = call(
        functools.partial(outer_kernel, quarter),
        jax.ShapeDtypeStruct((PLANE * BLOCK, width), BF16),
        hidden, lax.ppermute(hidden, "c", SWAP), w_down, other_down,
    )
    returned = lax.all_to_all(
        summed.reshape(PLANE, BLOCK, width), ("y", "xh", "xl"), 0, 0, tiled=True
    ).reshape(PLANE * BLOCK, width)

    parts = call(
        functools.partial(combine_kernel, quarter),
        jax.ShapeDtypeStruct((ZALL, BLOCK, quarter), BF16),
        returned, marks,
    )
    parts = lax.all_to_all(parts, ("zl", "zh"), 0, 0, tiled=True)
    moe_out = jnp.sum(parts.astype(F32), axis=0)
    return (moe_out.astype(BF16), attn_out)


def solution(mesh):
    fine = Mesh(mesh.devices.reshape(4, 2, 2, 4, 2, 2), ("y", "xh", "xl", "zl", "zh", "c"))
    grp, tp = ("y", "xh", "xl", "zl"), ("zh", "c")
    every = grp + tp
    return jax.shard_map(
        shards,
        mesh=fine,
        in_specs=(
            P(grp, None),
            P(grp, None),
            P(),
            P(None, every),
            P(None, every),
            P(every, None),
            P(every, None),
            P(every, None, None),
            P(every),
        ),
        out_specs=(P(grp, tp), P(every, None)),
        check_vma=False,
    )
```

```python
import functools
import math

import jax
import jax.numpy as jnp
from jax import lax
from jax.experimental import pallas as pl
from jax.experimental.pallas import tpu as pltpu
from jax.sharding import Mesh
from jax.sharding import PartitionSpec as P

CAP = 5
ZLO = 4
ZALL = 8
EXPERTS = 8
BLOCK = 16
PLANE = 16
LANES = 128
REACH = (0, 1, 2, -1)
HIGH, LOW = 64, 72
BF16, F32 = jnp.bfloat16, jnp.float32
VMEM_BYTES = 40 * 1024 * 1024
ALL_VMEM_BYTES = 60 * 1024 * 1024


def place(z):
    return (z % ZLO) * 2 + z // ZLO


def z_pairs(step):
    return [(place(z), place((z + step) % ZALL)) for z in range(ZALL)]


SWAP = [(0, 1), (1, 0)]


def z_send(value, step):
    return lax.ppermute(value, ("zl", "zh"), z_pairs(step))


def z_send_apart(value, step):
    both = [[(2 * a + c, 2 * b + c) for a, b in z_pairs(way)] for c, way in enumerate((step, -step))]
    return lax.ppermute(value, ("zl", "zh", "c"), both[0] + both[1])


def grid(rows, columns):
    return (
        lax.broadcasted_iota(jnp.int32, (rows, columns), 0),
        lax.broadcasted_iota(jnp.int32, (rows, columns), 1),
    )


def fifth(value):
    return (value * 205) >> 10


def fifth_rest(value):
    return value - CAP * fifth(value)


def ones(condition):
    return jnp.where(condition, 1.0, 0.0)


def shuffle_table(back):
    new, old = grid(PLANE * BLOCK, PLANE * BLOCK)
    if back:
        new, old = old, new
    spot = ((old >> 2) & 3) * 64 + (old >> 4) * 4 + (old & 3)
    return ones(new == spot).astype(BF16)


def dot(a, b):
    return jnp.dot(a, b, preferred_element_type=F32)


def dot_t(a, b):
    return lax.dot_general(a, b, (((1,), (1,)), ((), ())), preferred_element_type=F32)


def call(kernel, out_shape, *args):
    return pl.pallas_call(
        kernel,
        out_shape=out_shape,
        in_specs=[pl.BlockSpec(memory_space=pltpu.VMEM)] * len(args),
        out_specs=jax.tree.map(lambda _: pl.BlockSpec(memory_space=pltpu.VMEM), out_shape),
        compiler_params=pltpu.CompilerParams(vmem_limit_bytes=VMEM_BYTES),
    )(*args)


def rows_kernel(quarter, x_far, ids_far, router_far, out, x_rows, ids, router, arrived):
    half = 2 * quarter
    loads = [
        pltpu.make_async_copy(source, target, arrived.at[i])
        for i, (source, target) in enumerate(
            ((x_far, x_rows), (router_far, router), (ids_far, ids))
        )
    ]
    for load in loads:
        load.start()
    for load in loads:
        load.wait()
    values = x_rows[...].astype(F32)
    row, lane = grid(BLOCK, LANES)
    first, second = jnp.zeros_like(row), jnp.zeros_like(row)
    for r in range(BLOCK):
        first = jnp.where(row == r, ids[0, r], first)
        second = jnp.where(row == r, ids[1, r], second)
    squashed, total = [], 0.0
    for e in range(EXPERTS):
        logit = jnp.sum(values * router[e : e + 1, :], axis=1, keepdims=True)
        kept = jnp.where((first == e) | (second == e), jax.nn.sigmoid(logit), 0.0)
        squashed.append(kept)
        total = total + kept
    tail = jnp.zeros((BLOCK, LANES), F32)
    for e in range(EXPERTS):
        share = squashed[e] / total
        high = share.astype(BF16).astype(F32)
        low = (share - high).astype(BF16).astype(F32)
        tail = jnp.where(lane == HIGH + e, high, jnp.where(lane == LOW + e, low, tail))
    expert = fifth(lane)
    named = (first == expert) | (second == expert)
    row, column = grid(BLOCK, BLOCK)
    rank = dot(ones(row > column).astype(BF16), ones(named).astype(BF16))
    marks = ones(named & (rank == fifth_rest(lane).astype(F32)))
    tail = jnp.where(lane < EXPERTS * CAP, marks, tail)
    for f in range(2):
        at = columns(quarter, lax.axis_index("c"), f)
        out[:, f * quarter : (f + 1) * quarter] = x_rows[:, at]
    out[:, half:] = tail.astype(BF16)


def pack_kernel(quarter, *refs):
    blocks, (out, marks) = refs[:4], refs[4:]
    half = 2 * quarter
    eighth = quarter // 2
    rows = jnp.concatenate([b[:, :half] for b in blocks], axis=0)
    chosen = jnp.concatenate([b[:, half:] for b in blocks], axis=0)
    marks[...] = chosen
    lane = grid(ZLO * BLOCK, LANES)[1]
    chosen = jnp.where(lane < EXPERTS * CAP, chosen, jnp.zeros_like(chosen))
    slot, lane = grid(EXPERTS * BLOCK, LANES)
    same = fifth(lane) == slot >> 4
    pick_main = ones(same & (fifth_rest(lane) == fifth_rest(slot & 15))).astype(BF16)
    pick_rest = ones(same & (fifth_rest(lane) == 1 + (slot & 3))).astype(BF16)
    slot, row = grid(EXPERTS * BLOCK, ZLO * BLOCK)
    mask = ones(fifth(slot & 15) == row >> 4)
    main = dot((dot_t(pick_main, chosen) * mask).astype(BF16), rows)
    main = main.astype(BF16).reshape(EXPERTS, BLOCK, half)
    chosen4 = jnp.concatenate([chosen] * 4, axis=0)
    rows4 = jnp.concatenate([rows[:, i * eighth : (i + 1) * eighth] for i in range(4)], axis=0)
    slot, row = grid(EXPERTS * BLOCK, 4 * ZLO * BLOCK)
    mask = ones(((slot >> 2) & 3 == row >> 6) & ((row >> 4) & 3 == 3))
    rest = dot((dot_t(pick_rest, chosen4) * mask).astype(BF16), rows4)
    rest = rest.astype(BF16).reshape(EXPERTS, BLOCK, eighth)
    for x in range(2):
        out[:, x, :, :half] = main
        out[:, x, :, half:] = rest


def experts_in(quarter, core, block, w_gate, w_up):
    half = 2 * quarter
    rest = dot(shuffle_table(False), block[:, half:]).astype(BF16)
    gate, up = 0.0, 0.0
    for f in range(2):
        top = block[:, f * quarter : (f + 1) * quarter]
        tail = jnp.concatenate(
            [rest[(2 * f + i) * 64 : (2 * f + i + 1) * 64] for i in range(2)], axis=1
        )
        rows = jnp.concatenate([top, tail], axis=0)
        at = pl.ds(pl.multiple_of(f * half + core * quarter, LANES), quarter)
        gate = gate + dot_t(rows, w_gate[:, at])
        up = up + dot_t(rows, w_up[:, at])
    return gate, up


def columns(quarter, core, f):
    return pl.ds(pl.multiple_of(f * 2 * quarter + core * quarter, LANES), quarter)


def own_kernel(quarter, block, w_gate, w_up, gate_out, up_out):
    gate, up = experts_in(quarter, lax.axis_index("c"), block, w_gate, w_up)
    gate_out[...] = gate
    up_out[...] = up


def other_kernel(quarter, block, w_gate, w_up, gate_in, up_in, hidden):
    there = 1 - lax.axis_index("c")
    gate, up = experts_in(quarter, there, block, w_gate, w_up)
    gate, up = gate + gate_in[...], up + up_in[...]
    hidden[...] = (gate * jax.nn.sigmoid(gate) * up).astype(BF16)


def outer_kernel(quarter, hidden, other_hidden, w_down, other_down, out, weights, arrived):
    core = lax.axis_index("c")
    main = PLANE * BLOCK
    count = hidden.shape[1]
    loads = [
        pltpu.make_async_copy(
            source.at[:, columns(quarter, core, f)],
            weights.at[f, pl.ds(i * count, count)],
            arrived.at[f, i],
        )
        for f in range(2)
        for i, source in enumerate((w_down, other_down))
    ]
    for load in loads:
        load.start()
    both = jnp.concatenate([hidden[...], other_hidden[...]], axis=1)
    tails = []
    for f in range(2):
        loads[2 * f].wait()
        loads[2 * f + 1].wait()
        y = dot(both, weights[f]).astype(BF16)
        out[:, f * quarter : (f + 1) * quarter] = y[:main]
        tails += [y[main:, : quarter // 2], y[main:, quarter // 2 :]]
    tails = jnp.concatenate(tails, axis=0)
    out[:, 2 * quarter :] = dot(shuffle_table(True), tails).astype(BF16)


def combine_kernel(quarter, back, marks, out):
    half = 2 * quarter
    chosen = marks[...]
    lane, slot = grid(LANES, PLANE * BLOCK)
    expert = slot >> 5
    same = fifth(lane) == expert
    back_main = ones(same & (fifth_rest(lane) == fifth_rest(slot & 15))).astype(BF16)
    back_rest = ones(same & (fifth_rest(lane) == 1 + (slot & 3))).astype(BF16)
    wide_high = dot(chosen, ones(lane == HIGH + expert).astype(BF16))
    wide_low = dot(chosen, ones(lane == LOW + expert).astype(BF16))
    row, slot = grid(ZLO * BLOCK, PLANE * BLOCK)
    main = dot(chosen, back_main) * ones(fifth(slot & 15) == row >> 4)
    rest = dot(chosen, back_rest) * ones(row >> 4 == 3)
    wides = (wide_high, wide_low)
    count = ZLO * BLOCK
    both = dot(jnp.concatenate([(main * w).astype(BF16) for w in wides], axis=0), back[:, :half])
    picked = [rest * ones((slot >> 2) & 3 == i) for i in range(4)]
    stack = jnp.concatenate([(p * w).astype(BF16) for p in picked for w in wides], axis=0)
    tails = dot(stack, back[:, half:])
    pieces = [
        tails[2 * i * count : (2 * i + 1) * count] + tails[(2 * i + 1) * count : (2 * i + 2) * count]
        for i in range(4)
    ]
    total = both[:count] + both[count:] + jnp.concatenate(pieces, axis=1)
    for k in range(ZLO):
        owner = (lax.axis_index("zl") + (REACH[k] % ZLO)) & (ZLO - 1)
        for f in range(2):
            piece = total[k * BLOCK : (k + 1) * BLOCK, f * quarter : (f + 1) * quarter]
            out[owner * 2 + f] = piece.astype(BF16)


def attention_weights(queries, cache, lengths):
    head_dim = cache.shape[2] // 2
    heads = queries.shape[1] // head_dim
    query_heads = queries.reshape(queries.shape[0], heads, head_dim)
    scores = jnp.einsum(
        "bhd,bpd->bhp", query_heads, cache[:, :, :head_dim], preferred_element_type=F32
    ) / math.sqrt(head_dim)
    live = jnp.arange(cache.shape[1])[None, :] < lengths[:, None]
    scores = jnp.where(live[:, None, :], scores, -1e30)
    largest = jnp.max(scores, axis=2, keepdims=True)
    weights = jnp.where(live[:, None, :], jnp.exp(scores - largest), 0.0)
    return weights.astype(BF16), jnp.sum(weights, axis=2, keepdims=True)


def attention_mix(weights, denominator, cache):
    head_dim = cache.shape[2] // 2
    mixed = jnp.einsum(
        "bhp,bpd->bhd", weights, cache[:, :, head_dim:], preferred_element_type=F32
    )
    return (mixed / denominator).astype(BF16).reshape(cache.shape[0], -1)


def shards(x_rows, route_ids, router, w_gate, w_up, w_down, queries, cache, lengths):
    model_width = x_rows.shape[1]
    hidden_count = w_gate.shape[1]
    w_gate, w_up = w_gate.T, w_up.T
    quarter = model_width // 4
    half, eighth = 2 * quarter, quarter // 2
    width = half + eighth

    far = pl.BlockSpec(memory_space=pl.ANY)
    payload = pl.pallas_call(
        functools.partial(rows_kernel, quarter),
        out_shape=jax.ShapeDtypeStruct((BLOCK, half + LANES), BF16),
        in_specs=[far, far, far],
        out_specs=pl.BlockSpec(memory_space=pltpu.VMEM),
        scratch_shapes=[
            pltpu.VMEM(x_rows.shape, BF16),
            pltpu.SMEM(route_ids.T.shape, jnp.int32),
            pltpu.VMEM(router.T.shape, F32),
            pltpu.SemaphoreType.DMA((3,)),
        ],
        compiler_params=pltpu.CompilerParams(vmem_limit_bytes=ALL_VMEM_BYTES),
    )(x_rows, route_ids.T, router.T)
    blocks = [payload, z_send(payload, -1), z_send_apart(payload, -2), z_send(payload, 1)]

    payload, queries = lax.optimization_barrier((payload, queries))
    weights, denominator = attention_weights(queries, cache, lengths)
    other_down = lax.ppermute(w_down, "c", SWAP)
    blocks[0], weights, denominator, other_down = lax.optimization_barrier(
        (payload, weights, denominator, other_down)
    )
    packed, marks = call(
        functools.partial(pack_kernel, quarter),
        (
            jax.ShapeDtypeStruct((EXPERTS, 2, BLOCK, width), BF16),
            jax.ShapeDtypeStruct((ZLO * BLOCK, LANES), BF16),
        ),
        *blocks,
    )
    arrived = lax.all_to_all(
        packed.reshape(PLANE, BLOCK, width), ("y", "xh", "xl"), 0, 0, tiled=True
    ).reshape(PLANE * BLOCK, width)
    beside = lax.ppermute(arrived, "c", SWAP)
    rows = PLANE * (BLOCK + ZLO)
    partial = jax.ShapeDtypeStruct((rows, hidden_count), F32)
    gate, up = call(
        functools.partial(own_kernel, quarter),
        (partial, partial),
        arrived, w_gate, w_up,
    )
    gate, weights = lax.optimization_barrier((gate, weights))
    attn_out = attention_mix(weights, denominator, cache)
    gate, attn_out = lax.optimization_barrier((gate, attn_out))
    hidden = call(
        functools.partial(other_kernel, quarter),
        jax.ShapeDtypeStruct((rows, hidden_count), BF16),
        beside, w_gate, w_up, gate, up,
    )
    near = pl.BlockSpec(memory_space=pltpu.VMEM)
    summed = pl.pallas_call(
        functools.partial(outer_kernel, quarter),
        out_shape=jax.ShapeDtypeStruct((PLANE * BLOCK, width), BF16),
        in_specs=[near, near, far, far],
        out_specs=near,
        scratch_shapes=[
            pltpu.VMEM((2, 2 * hidden_count, quarter), BF16),
            pltpu.SemaphoreType.DMA((2, 2)),
        ],
        compiler_params=pltpu.CompilerParams(vmem_limit_bytes=VMEM_BYTES),
    )(hidden, lax.ppermute(hidden, "c", SWAP), w_down, other_down)
    returned = lax.all_to_all(
        summed.reshape(PLANE, BLOCK, width), ("y", "xh", "xl"), 0, 0, tiled=True
    ).reshape(PLANE * BLOCK, width)

    parts = call(
        functools.partial(combine_kernel, quarter),
        jax.ShapeDtypeStruct((ZALL, BLOCK, quarter), BF16),
        returned, marks,
    )
    parts = lax.all_to_all(parts, ("zl", "zh"), 0, 0, tiled=True)
    moe_out = jnp.sum(parts.astype(F32), axis=0)
    return (moe_out.astype(BF16), attn_out)


def solution(mesh):
    fine = Mesh(mesh.devices.reshape(4, 2, 2, 4, 2, 2), ("y", "xh", "xl", "zl", "zh", "c"))
    grp, tp = ("y", "xh", "xl", "zl"), ("zh", "c")
    every = grp + tp
    return jax.shard_map(
        shards,
        mesh=fine,
        in_specs=(
            P(grp, None),
            P(grp, None),
            P(),
            P(None, every),
            P(None, every),
            P(every, None),
            P(every, None),
            P(every, None, None),
            P(every),
        ),
        out_specs=(P(grp, tp), P(every, None)),
        check_vma=False,
    )
```

```python
import functools
import math

import jax
import jax.numpy as jnp
from jax import lax
from jax.experimental import pallas as pl
from jax.experimental.pallas import tpu as pltpu
from jax.sharding import Mesh
from jax.sharding import PartitionSpec as P

CAP = 5
ZLO = 4
ZALL = 8
EXPERTS = 8
BLOCK = 16
PLANE = 16
LANES = 128
REACH = (0, 1, 2, -1)
HIGH, LOW = 64, 72
BF16, F32 = jnp.bfloat16, jnp.float32
VMEM_BYTES = 40 * 1024 * 1024
ALL_VMEM_BYTES = 60 * 1024 * 1024


def place(z):
    return (z % ZLO) * 2 + z // ZLO


def z_pairs(step):
    return [(place(z), place((z + step) % ZALL)) for z in range(ZALL)]


SWAP = [(0, 1), (1, 0)]


def z_send(value, step):
    return lax.ppermute(value, ("zl", "zh"), z_pairs(step))


def z_send_apart(value, step):
    both = [[(2 * a + c, 2 * b + c) for a, b in z_pairs(way)] for c, way in enumerate((step, -step))]
    return lax.ppermute(value, ("zl", "zh", "c"), both[0] + both[1])


def grid(rows, columns):
    return (
        lax.broadcasted_iota(jnp.int32, (rows, columns), 0),
        lax.broadcasted_iota(jnp.int32, (rows, columns), 1),
    )


def fifth(value):
    return (value * 205) >> 10


def fifth_rest(value):
    return value - CAP * fifth(value)


def ones(condition):
    return jnp.where(condition, 1.0, 0.0)


def shuffle_table(back):
    new, old = grid(PLANE * BLOCK, PLANE * BLOCK)
    if back:
        new, old = old, new
    spot = ((old >> 2) & 3) * 64 + (old >> 4) * 4 + (old & 3)
    return ones(new == spot).astype(BF16)


def dot(a, b):
    return jnp.dot(a, b, preferred_element_type=F32)


def dot_t(a, b):
    return lax.dot_general(a, b, (((1,), (1,)), ((), ())), preferred_element_type=F32)


def call(kernel, out_shape, *args):
    return pl.pallas_call(
        kernel,
        out_shape=out_shape,
        in_specs=[pl.BlockSpec(memory_space=pltpu.VMEM)] * len(args),
        out_specs=jax.tree.map(lambda _: pl.BlockSpec(memory_space=pltpu.VMEM), out_shape),
        compiler_params=pltpu.CompilerParams(vmem_limit_bytes=VMEM_BYTES),
    )(*args)


def rows_kernel(quarter, x_far, ids_far, router_far, out, x_rows, ids, router, arrived):
    half = 2 * quarter
    loads = [
        pltpu.make_async_copy(source, target, arrived.at[i])
        for i, (source, target) in enumerate(
            ((x_far, x_rows), (router_far, router), (ids_far, ids))
        )
    ]
    for load in loads:
        load.start()
    for load in loads:
        load.wait()
    parts = [jnp.zeros((BLOCK, LANES), F32)] * EXPERTS
    for at in range(0, x_rows.shape[1], LANES):
        values = x_rows[:, at : at + LANES].astype(F32)
        for e in range(EXPERTS):
            parts[e] = parts[e] + values * router[e : e + 1, at : at + LANES]
    row, lane = grid(BLOCK, LANES)
    first, second = jnp.zeros_like(row), jnp.zeros_like(row)
    for r in range(BLOCK):
        first = jnp.where(row == r, ids[0, r], first)
        second = jnp.where(row == r, ids[1, r], second)
    squashed, total = [], 0.0
    for e in range(EXPERTS):
        logit = jnp.sum(parts[e], axis=1, keepdims=True)
        kept = jnp.where((first == e) | (second == e), jax.nn.sigmoid(logit), 0.0)
        squashed.append(kept)
        total = total + kept
    tail = jnp.zeros((BLOCK, LANES), F32)
    for e in range(EXPERTS):
        share = squashed[e] / total
        high = share.astype(BF16).astype(F32)
        low = (share - high).astype(BF16).astype(F32)
        tail = jnp.where(lane == HIGH + e, high, jnp.where(lane == LOW + e, low, tail))
    expert = fifth(lane)
    named = (first == expert) | (second == expert)
    row, column = grid(BLOCK, BLOCK)
    rank = dot(ones(row > column).astype(BF16), ones(named).astype(BF16))
    marks = ones(named & (rank == fifth_rest(lane).astype(F32)))
    tail = jnp.where(lane < EXPERTS * CAP, marks, tail)
    for f in range(2):
        at = columns(quarter, lax.axis_index("c"), f)
        out[:, f * quarter : (f + 1) * quarter] = x_rows[:, at]
    out[:, half:] = tail.astype(BF16)


def pack_kernel(quarter, *refs):
    blocks, (out, marks) = refs[:4], refs[4:]
    half = 2 * quarter
    eighth = quarter // 2
    rows = jnp.concatenate([b[:, :half] for b in blocks], axis=0)
    chosen = jnp.concatenate([b[:, half:] for b in blocks], axis=0)
    marks[...] = chosen
    lane = grid(ZLO * BLOCK, LANES)[1]
    chosen = jnp.where(lane < EXPERTS * CAP, chosen, jnp.zeros_like(chosen))
    slot, lane = grid(EXPERTS * BLOCK, LANES)
    same = fifth(lane) == slot >> 4
    pick_main = ones(same & (fifth_rest(lane) == fifth_rest(slot & 15))).astype(BF16)
    pick_rest = ones(same & (fifth_rest(lane) == 1 + (slot & 3))).astype(BF16)
    slot, row = grid(EXPERTS * BLOCK, ZLO * BLOCK)
    mask = ones(fifth(slot & 15) == row >> 4)
    main = dot((dot_t(pick_main, chosen) * mask).astype(BF16), rows)
    main = main.astype(BF16).reshape(EXPERTS, BLOCK, half)
    chosen4 = jnp.concatenate([chosen] * 4, axis=0)
    rows4 = jnp.concatenate([rows[:, i * eighth : (i + 1) * eighth] for i in range(4)], axis=0)
    slot, row = grid(EXPERTS * BLOCK, 4 * ZLO * BLOCK)
    mask = ones(((slot >> 2) & 3 == row >> 6) & ((row >> 4) & 3 == 3))
    rest = dot((dot_t(pick_rest, chosen4) * mask).astype(BF16), rows4)
    rest = rest.astype(BF16).reshape(EXPERTS, BLOCK, eighth)
    for x in range(2):
        out[:, x, :, :half] = main
        out[:, x, :, half:] = rest


def experts_in(quarter, core, block, w_gate, w_up):
    half = 2 * quarter
    rest = dot(shuffle_table(False), block[:, half:]).astype(BF16)
    gate, up = 0.0, 0.0
    for f in range(2):
        top = block[:, f * quarter : (f + 1) * quarter]
        tail = jnp.concatenate(
            [rest[(2 * f + i) * 64 : (2 * f + i + 1) * 64] for i in range(2)], axis=1
        )
        rows = jnp.concatenate([top, tail], axis=0)
        at = pl.ds(pl.multiple_of(f * half + core * quarter, LANES), quarter)
        gate = gate + dot_t(rows, w_gate[:, at])
        up = up + dot_t(rows, w_up[:, at])
    return gate, up


def columns(quarter, core, f):
    return pl.ds(pl.multiple_of(f * 2 * quarter + core * quarter, LANES), quarter)


def own_kernel(quarter, block, w_gate, w_up, gate_out, up_out):
    gate, up = experts_in(quarter, lax.axis_index("c"), block, w_gate, w_up)
    gate_out[...] = gate
    up_out[...] = up


def other_kernel(
    quarter, block, w_gate, w_up, gate_in, up_in, w_down, other_down, hidden, weights, arrived
):
    core = lax.axis_index("c")
    count = hidden.shape[1]
    loads = [
        pltpu.make_async_copy(
            source.at[:, columns(quarter, core, f)],
            weights.at[f, pl.ds(i * count, count)],
            arrived.at[f, i],
        )
        for f in range(2)
        for i, source in enumerate((w_down, other_down))
    ]
    for load in loads:
        load.start()
    gate, up = experts_in(quarter, 1 - core, block, w_gate, w_up)
    gate, up = gate + gate_in[...], up + up_in[...]
    hidden[...] = (gate * jax.nn.sigmoid(gate) * up).astype(BF16)
    for load in loads:
        load.wait()


def outer_kernel(quarter, hidden, other_hidden, weights, out):
    main = PLANE * BLOCK
    both = jnp.concatenate([hidden[...], other_hidden[...]], axis=1)
    tails = []
    for f in range(2):
        y = dot(both, weights[f]).astype(BF16)
        out[:, f * quarter : (f + 1) * quarter] = y[:main]
        tails += [y[main:, : quarter // 2], y[main:, quarter // 2 :]]
    tails = jnp.concatenate(tails, axis=0)
    out[:, 2 * quarter :] = dot(shuffle_table(True), tails).astype(BF16)


def combine_kernel(quarter, back, marks, out):
    half = 2 * quarter
    chosen = marks[...]
    lane, slot = grid(LANES, PLANE * BLOCK)
    expert = slot >> 5
    same = fifth(lane) == expert
    back_main = ones(same & (fifth_rest(lane) == fifth_rest(slot & 15))).astype(BF16)
    back_rest = ones(same & (fifth_rest(lane) == 1 + (slot & 3))).astype(BF16)
    wide_high = dot(chosen, ones(lane == HIGH + expert).astype(BF16))
    wide_low = dot(chosen, ones(lane == LOW + expert).astype(BF16))
    row, slot = grid(ZLO * BLOCK, PLANE * BLOCK)
    main = dot(chosen, back_main) * ones(fifth(slot & 15) == row >> 4)
    rest = dot(chosen, back_rest) * ones(row >> 4 == 3)
    wides = (wide_high, wide_low)
    count = ZLO * BLOCK
    both = dot(jnp.concatenate([(main * w).astype(BF16) for w in wides], axis=0), back[:, :half])
    picked = [rest * ones((slot >> 2) & 3 == i) for i in range(4)]
    stack = jnp.concatenate([(p * w).astype(BF16) for p in picked for w in wides], axis=0)
    tails = dot(stack, back[:, half:])
    pieces = [
        tails[2 * i * count : (2 * i + 1) * count] + tails[(2 * i + 1) * count : (2 * i + 2) * count]
        for i in range(4)
    ]
    total = both[:count] + both[count:] + jnp.concatenate(pieces, axis=1)
    for k in range(ZLO):
        owner = (lax.axis_index("zl") + (REACH[k] % ZLO)) & (ZLO - 1)
        for f in range(2):
            piece = total[k * BLOCK : (k + 1) * BLOCK, f * quarter : (f + 1) * quarter]
            out[owner * 2 + f] = piece.astype(BF16)


def attention_weights(queries, cache, lengths):
    head_dim = cache.shape[2] // 2
    heads = queries.shape[1] // head_dim
    query_heads = queries.reshape(queries.shape[0], heads, head_dim)
    scores = jnp.einsum(
        "bhd,bpd->bhp", query_heads, cache[:, :, :head_dim], preferred_element_type=F32
    ) / math.sqrt(head_dim)
    live = jnp.arange(cache.shape[1])[None, :] < lengths[:, None]
    scores = jnp.where(live[:, None, :], scores, -1e30)
    largest = jnp.max(scores, axis=2, keepdims=True)
    weights = jnp.where(live[:, None, :], jnp.exp(scores - largest), 0.0)
    return weights.astype(BF16), jnp.sum(weights, axis=2, keepdims=True)


def attention_mix(weights, denominator, cache):
    head_dim = cache.shape[2] // 2
    mixed = jnp.einsum(
        "bhp,bpd->bhd", weights, cache[:, :, head_dim:], preferred_element_type=F32
    )
    return (mixed / denominator).astype(BF16).reshape(cache.shape[0], -1)


def shards(x_rows, route_ids, router, w_gate, w_up, w_down, queries, cache, lengths):
    model_width = x_rows.shape[1]
    hidden_count = w_gate.shape[1]
    w_gate, w_up = w_gate.T, w_up.T
    quarter = model_width // 4
    half, eighth = 2 * quarter, quarter // 2
    width = half + eighth

    far = pl.BlockSpec(memory_space=pl.ANY)
    payload = pl.pallas_call(
        functools.partial(rows_kernel, quarter),
        out_shape=jax.ShapeDtypeStruct((BLOCK, half + LANES), BF16),
        in_specs=[far, far, far],
        out_specs=pl.BlockSpec(memory_space=pltpu.VMEM),
        scratch_shapes=[
            pltpu.VMEM(x_rows.shape, BF16),
            pltpu.SMEM(route_ids.T.shape, jnp.int32),
            pltpu.VMEM(router.T.shape, F32),
            pltpu.SemaphoreType.DMA((3,)),
        ],
        compiler_params=pltpu.CompilerParams(vmem_limit_bytes=ALL_VMEM_BYTES),
    )(x_rows, route_ids.T, router.T)
    blocks = [payload, z_send(payload, -1), z_send_apart(payload, -2), z_send(payload, 1)]

    payload, queries = lax.optimization_barrier((payload, queries))
    weights, denominator = attention_weights(queries, cache, lengths)
    other_down = lax.ppermute(lax.optimization_barrier((payload, w_down))[1], "c", SWAP)
    blocks[0], weights, denominator, other_down = lax.optimization_barrier(
        (payload, weights, denominator, other_down)
    )
    packed, marks = call(
        functools.partial(pack_kernel, quarter),
        (
            jax.ShapeDtypeStruct((EXPERTS, 2, BLOCK, width), BF16),
            jax.ShapeDtypeStruct((ZLO * BLOCK, LANES), BF16),
        ),
        *blocks,
    )
    arrived = lax.all_to_all(
        packed.reshape(PLANE, BLOCK, width), ("y", "xh", "xl"), 0, 0, tiled=True
    ).reshape(PLANE * BLOCK, width)
    beside = lax.ppermute(arrived, "c", SWAP)
    rows = PLANE * (BLOCK + ZLO)
    partial = jax.ShapeDtypeStruct((rows, hidden_count), F32)
    gate, up = call(
        functools.partial(own_kernel, quarter),
        (partial, partial),
        arrived, w_gate, w_up,
    )
    gate, weights = lax.optimization_barrier((gate, weights))
    attn_out = attention_mix(weights, denominator, cache)
    gate, attn_out = lax.optimization_barrier((gate, attn_out))
    near = pl.BlockSpec(memory_space=pltpu.VMEM)
    hidden, down = pl.pallas_call(
        functools.partial(other_kernel, quarter),
        out_shape=(
            jax.ShapeDtypeStruct((rows, hidden_count), BF16),
            jax.ShapeDtypeStruct((2, 2 * hidden_count, quarter), BF16),
        ),
        in_specs=[near] * 5 + [far] * 2,
        out_specs=(near, near),
        scratch_shapes=[pltpu.SemaphoreType.DMA((2, 2))],
        compiler_params=pltpu.CompilerParams(vmem_limit_bytes=VMEM_BYTES),
    )(beside, w_gate, w_up, gate, up, w_down, other_down)
    summed = call(
        functools.partial(outer_kernel, quarter),
        jax.ShapeDtypeStruct((PLANE * BLOCK, width), BF16),
        hidden, lax.ppermute(hidden, "c", SWAP), down,
    )
    returned = lax.all_to_all(
        summed.reshape(PLANE, BLOCK, width), ("y", "xh", "xl"), 0, 0, tiled=True
    ).reshape(PLANE * BLOCK, width)

    parts = call(
        functools.partial(combine_kernel, quarter),
        jax.ShapeDtypeStruct((ZALL, BLOCK, quarter), BF16),
        returned, marks,
    )
    parts = lax.all_to_all(parts, ("zl", "zh"), 0, 0, tiled=True)
    moe_out = jnp.sum(parts.astype(F32), axis=0)
    return (moe_out.astype(BF16), attn_out)


def solution(mesh):
    fine = Mesh(mesh.devices.reshape(4, 2, 2, 4, 2, 2), ("y", "xh", "xl", "zl", "zh", "c"))
    grp, tp = ("y", "xh", "xl", "zl"), ("zh", "c")
    every = grp + tp
    return jax.shard_map(
        shards,
        mesh=fine,
        in_specs=(
            P(grp, None),
            P(grp, None),
            P(),
            P(None, every),
            P(None, every),
            P(every, None),
            P(every, None),
            P(every, None, None),
            P(every),
        ),
        out_specs=(P(grp, tp), P(every, None)),
        check_vma=False,
    )
```

```python
import functools
import math

import jax
import jax.numpy as jnp
from jax import lax
from jax.experimental import pallas as pl
from jax.experimental.pallas import tpu as pltpu
from jax.sharding import Mesh
from jax.sharding import PartitionSpec as P

CAP = 5
ZLO = 4
ZALL = 8
EXPERTS = 8
BLOCK = 16
PLANE = 16
PLANE_AXES = ("y", "xl", "xh")
LANES = 128
REACH = (0, 1, 2, -1)
HIGH, LOW = 64, 72
BF16, F32 = jnp.bfloat16, jnp.float32
VMEM_BYTES = 40 * 1024 * 1024
ALL_VMEM_BYTES = 60 * 1024 * 1024


def place(z):
    return (z % ZLO) * 2 + z // ZLO


def z_pairs(step):
    return [(place(z), place((z + step) % ZALL)) for z in range(ZALL)]


SWAP = [(0, 1), (1, 0)]


def z_send(value, step):
    return lax.ppermute(value, ("zl", "zh"), z_pairs(step))


def z_send_apart(value, step):
    both = [[(2 * a + c, 2 * b + c) for a, b in z_pairs(way)] for c, way in enumerate((step, -step))]
    return lax.ppermute(value, ("zl", "zh", "c"), both[0] + both[1])


def grid(rows, columns):
    return (
        lax.broadcasted_iota(jnp.int32, (rows, columns), 0),
        lax.broadcasted_iota(jnp.int32, (rows, columns), 1),
    )


def fifth(value):
    return (value * 205) >> 10


def fifth_rest(value):
    return value - CAP * fifth(value)


def ones(condition):
    return jnp.where(condition, 1.0, 0.0)


def shuffle_table(back):
    new, old = grid(PLANE * BLOCK, PLANE * BLOCK)
    if back:
        new, old = old, new
    spot = ((old >> 2) & 3) * 64 + (old >> 4) * 4 + (old & 3)
    return ones(new == spot).astype(BF16)


def dot(a, b):
    return jnp.dot(a, b, preferred_element_type=F32)


def dot_t(a, b):
    return lax.dot_general(a, b, (((1,), (1,)), ((), ())), preferred_element_type=F32)


def call(kernel, out_shape, *args):
    return pl.pallas_call(
        kernel,
        out_shape=out_shape,
        in_specs=[pl.BlockSpec(memory_space=pltpu.VMEM)] * len(args),
        out_specs=jax.tree.map(lambda _: pl.BlockSpec(memory_space=pltpu.VMEM), out_shape),
        compiler_params=pltpu.CompilerParams(vmem_limit_bytes=VMEM_BYTES),
    )(*args)


def rows_kernel(quarter, x_far, ids_far, router_far, out, x_rows, ids, router, arrived):
    half = 2 * quarter
    loads = [
        pltpu.make_async_copy(source, target, arrived.at[i])
        for i, (source, target) in enumerate(
            ((x_far, x_rows), (router_far, router), (ids_far, ids))
        )
    ]
    for load in loads:
        load.start()
    for load in loads:
        load.wait()
    parts = [jnp.zeros((BLOCK, LANES), F32)] * EXPERTS
    for at in range(0, x_rows.shape[1], LANES):
        values = x_rows[:, at : at + LANES].astype(F32)
        for e in range(EXPERTS):
            parts[e] = parts[e] + values * router[e : e + 1, at : at + LANES]
    row, lane = grid(BLOCK, LANES)
    first, second = jnp.zeros_like(row), jnp.zeros_like(row)
    for r in range(BLOCK):
        first = jnp.where(row == r, ids[0, r], first)
        second = jnp.where(row == r, ids[1, r], second)
    squashed, total = [], 0.0
    for e in range(EXPERTS):
        logit = jnp.sum(parts[e], axis=1, keepdims=True)
        kept = jnp.where((first == e) | (second == e), jax.nn.sigmoid(logit), 0.0)
        squashed.append(kept)
        total = total + kept
    tail = jnp.zeros((BLOCK, LANES), F32)
    for e in range(EXPERTS):
        share = squashed[e] / total
        high = share.astype(BF16).astype(F32)
        low = (share - high).astype(BF16).astype(F32)
        tail = jnp.where(lane == HIGH + e, high, jnp.where(lane == LOW + e, low, tail))
    expert = fifth(lane)
    named = (first == expert) | (second == expert)
    row, column = grid(BLOCK, BLOCK)
    rank = dot(ones(row > column).astype(BF16), ones(named).astype(BF16))
    marks = ones(named & (rank == fifth_rest(lane).astype(F32)))
    tail = jnp.where(lane < EXPERTS * CAP, marks, tail)
    for f in range(2):
        at = columns(quarter, lax.axis_index("c"), f)
        out[:, f * quarter : (f + 1) * quarter] = x_rows[:, at]
    out[:, half:] = tail.astype(BF16)


def pack_kernel(quarter, *refs):
    blocks, (out, marks) = refs[:4], refs[4:]
    half = 2 * quarter
    eighth = quarter // 2
    rows = jnp.concatenate([b[:, :half] for b in blocks], axis=0)
    chosen = jnp.concatenate([b[:, half:] for b in blocks], axis=0)
    marks[...] = chosen
    lane = grid(ZLO * BLOCK, LANES)[1]
    chosen = jnp.where(lane < EXPERTS * CAP, chosen, jnp.zeros_like(chosen))
    slot, lane = grid(EXPERTS * BLOCK, LANES)
    same = fifth(lane) == slot >> 4
    pick_main = ones(same & (fifth_rest(lane) == fifth_rest(slot & 15))).astype(BF16)
    pick_rest = ones(same & (fifth_rest(lane) == 1 + (slot & 3))).astype(BF16)
    slot, row = grid(EXPERTS * BLOCK, ZLO * BLOCK)
    mask = ones(fifth(slot & 15) == row >> 4)
    main = dot((dot_t(pick_main, chosen) * mask).astype(BF16), rows)
    main = main.astype(BF16).reshape(EXPERTS // 2, 2, BLOCK, half)
    chosen4 = jnp.concatenate([chosen] * 4, axis=0)
    rows4 = jnp.concatenate([rows[:, i * eighth : (i + 1) * eighth] for i in range(4)], axis=0)
    slot, row = grid(EXPERTS * BLOCK, 4 * ZLO * BLOCK)
    mask = ones(((slot >> 2) & 3 == row >> 6) & ((row >> 4) & 3 == 3))
    rest = dot((dot_t(pick_rest, chosen4) * mask).astype(BF16), rows4)
    rest = rest.astype(BF16).reshape(EXPERTS // 2, 2, BLOCK, eighth)
    for x in range(2):
        out[:, x, :, :, :half] = main
        out[:, x, :, :, half:] = rest


def experts_in(quarter, core, block, w_gate, w_up):
    half = 2 * quarter
    rest = dot(shuffle_table(False), block[:, half:]).astype(BF16)
    gate, up = 0.0, 0.0
    for f in range(2):
        top = block[:, f * quarter : (f + 1) * quarter]
        tail = jnp.concatenate(
            [rest[(2 * f + i) * 64 : (2 * f + i + 1) * 64] for i in range(2)], axis=1
        )
        rows = jnp.concatenate([top, tail], axis=0)
        at = pl.ds(pl.multiple_of(f * half + core * quarter, LANES), quarter)
        gate = gate + dot_t(rows, w_gate[:, at])
        up = up + dot_t(rows, w_up[:, at])
    return gate, up


def columns(quarter, core, f):
    return pl.ds(pl.multiple_of(f * 2 * quarter + core * quarter, LANES), quarter)


def own_kernel(quarter, block, w_gate, w_up, gate_out, up_out):
    gate, up = experts_in(quarter, lax.axis_index("c"), block, w_gate, w_up)
    gate_out[...] = gate
    up_out[...] = up


def other_kernel(
    quarter, block, w_gate, w_up, gate_in, up_in, w_down, other_down, hidden, weights, arrived
):
    core = lax.axis_index("c")
    count = hidden.shape[1]
    loads = [
        pltpu.make_async_copy(
            source.at[:, columns(quarter, core, f)],
            weights.at[f, pl.ds(i * count, count)],
            arrived.at[f, i],
        )
        for f in range(2)
        for i, source in enumerate((w_down, other_down))
    ]
    for load in loads:
        load.start()
    gate, up = experts_in(quarter, 1 - core, block, w_gate, w_up)
    gate, up = gate + gate_in[...], up + up_in[...]
    hidden[...] = (gate * jax.nn.sigmoid(gate) * up).astype(BF16)
    for load in loads:
        load.wait()


def outer_kernel(quarter, hidden, other_hidden, weights, out):
    main = PLANE * BLOCK
    both = jnp.concatenate([hidden[...], other_hidden[...]], axis=1)
    tails = []
    for f in range(2):
        y = dot(both, weights[f]).astype(BF16)
        out[:, f * quarter : (f + 1) * quarter] = y[:main]
        tails += [y[main:, : quarter // 2], y[main:, quarter // 2 :]]
    tails = jnp.concatenate(tails, axis=0)
    out[:, 2 * quarter :] = dot(shuffle_table(True), tails).astype(BF16)


def combine_kernel(quarter, back, marks, out):
    half = 2 * quarter
    chosen = marks[...]
    lane, slot = grid(LANES, PLANE * BLOCK)
    expert = ((slot >> 6) << 1) + ((slot >> 4) & 1)
    same = fifth(lane) == expert
    back_main = ones(same & (fifth_rest(lane) == fifth_rest(slot & 15))).astype(BF16)
    back_rest = ones(same & (fifth_rest(lane) == 1 + (slot & 3))).astype(BF16)
    wide_high = dot(chosen, ones(lane == HIGH + expert).astype(BF16))
    wide_low = dot(chosen, ones(lane == LOW + expert).astype(BF16))
    row, slot = grid(ZLO * BLOCK, PLANE * BLOCK)
    main = dot(chosen, back_main) * ones(fifth(slot & 15) == row >> 4)
    rest = dot(chosen, back_rest) * ones(row >> 4 == 3)
    wides = (wide_high, wide_low)
    count = ZLO * BLOCK
    both = dot(jnp.concatenate([(main * w).astype(BF16) for w in wides], axis=0), back[:, :half])
    picked = [rest * ones((slot >> 2) & 3 == i) for i in range(4)]
    stack = jnp.concatenate([(p * w).astype(BF16) for p in picked for w in wides], axis=0)
    tails = dot(stack, back[:, half:])
    pieces = [
        tails[2 * i * count : (2 * i + 1) * count] + tails[(2 * i + 1) * count : (2 * i + 2) * count]
        for i in range(4)
    ]
    total = both[:count] + both[count:] + jnp.concatenate(pieces, axis=1)
    for k in range(ZLO):
        owner = (lax.axis_index("zl") + (REACH[k] % ZLO)) & (ZLO - 1)
        for f in range(2):
            piece = total[k * BLOCK : (k + 1) * BLOCK, f * quarter : (f + 1) * quarter]
            out[f * ZLO + owner] = piece.astype(BF16)


def attention_weights(queries, cache, lengths):
    head_dim = cache.shape[2] // 2
    heads = queries.shape[1] // head_dim
    query_heads = queries.reshape(queries.shape[0], heads, head_dim)
    scores = jnp.einsum(
        "bhd,bpd->bhp", query_heads, cache[:, :, :head_dim], preferred_element_type=F32
    ) / math.sqrt(head_dim)
    live = jnp.arange(cache.shape[1])[None, :] < lengths[:, None]
    scores = jnp.where(live[:, None, :], scores, -1e30)
    largest = jnp.max(scores, axis=2, keepdims=True)
    weights = jnp.where(live[:, None, :], jnp.exp(scores - largest), 0.0)
    return weights.astype(BF16), jnp.sum(weights, axis=2, keepdims=True)


def attention_mix(weights, denominator, cache):
    head_dim = cache.shape[2] // 2
    mixed = jnp.einsum(
        "bhp,bpd->bhd", weights, cache[:, :, head_dim:], preferred_element_type=F32
    )
    return (mixed / denominator).astype(BF16).reshape(cache.shape[0], -1)


def shards(x_rows, route_ids, router, w_gate, w_up, w_down, queries, cache, lengths):
    model_width = x_rows.shape[1]
    hidden_count = w_gate.shape[1]
    w_gate, w_up = w_gate.T, w_up.T
    quarter = model_width // 4
    half, eighth = 2 * quarter, quarter // 2
    width = half + eighth

    far = pl.BlockSpec(memory_space=pl.ANY)
    payload = pl.pallas_call(
        functools.partial(rows_kernel, quarter),
        out_shape=jax.ShapeDtypeStruct((BLOCK, half + LANES), BF16),
        in_specs=[far, far, far],
        out_specs=pl.BlockSpec(memory_space=pltpu.VMEM),
        scratch_shapes=[
            pltpu.VMEM(x_rows.shape, BF16),
            pltpu.SMEM(route_ids.T.shape, jnp.int32),
            pltpu.VMEM(router.T.shape, F32),
            pltpu.SemaphoreType.DMA((3,)),
        ],
        compiler_params=pltpu.CompilerParams(vmem_limit_bytes=ALL_VMEM_BYTES),
    )(x_rows, route_ids.T, router.T)
    blocks = [payload, z_send(payload, -1), z_send_apart(payload, -2), z_send(payload, 1)]

    payload, queries = lax.optimization_barrier((payload, queries))
    weights, denominator = attention_weights(queries, cache, lengths)
    other_down = lax.ppermute(lax.optimization_barrier((payload, w_down))[1], "c", SWAP)
    blocks[0], weights, denominator, other_down = lax.optimization_barrier(
        (payload, weights, denominator, other_down)
    )
    packed, marks = call(
        functools.partial(pack_kernel, quarter),
        (
            jax.ShapeDtypeStruct((EXPERTS // 2, 2, 2, BLOCK, width), BF16),
            jax.ShapeDtypeStruct((ZLO * BLOCK, LANES), BF16),
        ),
        *blocks,
    )
    arrived = lax.all_to_all(
        packed.reshape(PLANE, BLOCK, width), PLANE_AXES, 0, 0, tiled=True
    ).reshape(PLANE * BLOCK, width)
    beside = lax.ppermute(arrived, "c", SWAP)
    rows = PLANE * (BLOCK + ZLO)
    partial = jax.ShapeDtypeStruct((rows, hidden_count), F32)
    gate, up = call(
        functools.partial(own_kernel, quarter),
        (partial, partial),
        arrived, w_gate, w_up,
    )
    gate, weights = lax.optimization_barrier((gate, weights))
    attn_out = attention_mix(weights, denominator, cache)
    gate, attn_out = lax.optimization_barrier((gate, attn_out))
    near = pl.BlockSpec(memory_space=pltpu.VMEM)
    hidden, down = pl.pallas_call(
        functools.partial(other_kernel, quarter),
        out_shape=(
            jax.ShapeDtypeStruct((rows, hidden_count), BF16),
            jax.ShapeDtypeStruct((2, 2 * hidden_count, quarter), BF16),
        ),
        in_specs=[near] * 5 + [far] * 2,
        out_specs=(near, near),
        scratch_shapes=[pltpu.SemaphoreType.DMA((2, 2))],
        compiler_params=pltpu.CompilerParams(vmem_limit_bytes=VMEM_BYTES),
    )(beside, w_gate, w_up, gate, up, w_down, other_down)
    summed = call(
        functools.partial(outer_kernel, quarter),
        jax.ShapeDtypeStruct((PLANE * BLOCK, width), BF16),
        hidden, lax.ppermute(hidden, "c", SWAP), down,
    )
    returned = lax.all_to_all(
        summed.reshape(PLANE, BLOCK, width), PLANE_AXES, 0, 0, tiled=True
    ).reshape(PLANE * BLOCK, width)

    parts = call(
        functools.partial(combine_kernel, quarter),
        jax.ShapeDtypeStruct((ZALL, BLOCK, quarter), BF16),
        returned, marks,
    )
    parts = lax.all_to_all(parts, ("zh", "zl"), 0, 0, tiled=True)
    moe_out = jnp.sum(parts.astype(F32), axis=0)
    return (moe_out.astype(BF16), attn_out)


def solution(mesh):
    fine = Mesh(mesh.devices.reshape(4, 2, 2, 4, 2, 2), ("y", "xh", "xl", "zl", "zh", "c"))
    grp, tp = ("y", "xh", "xl", "zl"), ("zh", "c")
    every = grp + tp
    return jax.shard_map(
        shards,
        mesh=fine,
        in_specs=(
            P(grp, None),
            P(grp, None),
            P(),
            P(None, every),
            P(None, every),
            P(every, None),
            P(every, None),
            P(every, None, None),
            P(every),
        ),
        out_specs=(P(grp, tp), P(every, None)),
        check_vma=False,
    )
```

```python
import functools
import math

import jax
import jax.numpy as jnp
from jax import lax
from jax.experimental import pallas as pl
from jax.experimental.pallas import tpu as pltpu
from jax.sharding import Mesh
from jax.sharding import PartitionSpec as P

CAP = 5
ZLO = 4
ZALL = 8
EXPERTS = 8
BLOCK = 16
PLANE = 16
PLANE_AXES = ("y", "xl", "xh")
LANES = 128
REACH = (0, 1, 2, -1)
HIGH, LOW = 64, 72
BF16, F32 = jnp.bfloat16, jnp.float32
VMEM_BYTES = 40 * 1024 * 1024
ALL_VMEM_BYTES = 60 * 1024 * 1024


def place(z):
    return (z % ZLO) * 2 + z // ZLO


def z_pairs(step):
    return [(place(z), place((z + step) % ZALL)) for z in range(ZALL)]


SWAP = [(0, 1), (1, 0)]


def z_send(value, step):
    return lax.ppermute(value, ("zl", "zh"), z_pairs(step))


def z_send_apart(value, step):
    both = [[(2 * a + c, 2 * b + c) for a, b in z_pairs(way)] for c, way in enumerate((step, -step))]
    return lax.ppermute(value, ("zl", "zh", "c"), both[0] + both[1])


def grid(rows, columns):
    return (
        lax.broadcasted_iota(jnp.int32, (rows, columns), 0),
        lax.broadcasted_iota(jnp.int32, (rows, columns), 1),
    )


def fifth(value):
    return (value * 205) >> 10


def fifth_rest(value):
    return value - CAP * fifth(value)


def ones(condition):
    return jnp.where(condition, 1.0, 0.0)


def shuffle_table(back):
    new, old = grid(PLANE * BLOCK, PLANE * BLOCK)
    if back:
        new, old = old, new
    spot = ((old >> 2) & 3) * 64 + (old >> 4) * 4 + (old & 3)
    return ones(new == spot).astype(BF16)


def dot(a, b):
    return jnp.dot(a, b, preferred_element_type=F32)


def dot_t(a, b):
    return lax.dot_general(a, b, (((1,), (1,)), ((), ())), preferred_element_type=F32)


def call(kernel, out_shape, *args):
    return pl.pallas_call(
        kernel,
        out_shape=out_shape,
        in_specs=[pl.BlockSpec(memory_space=pltpu.VMEM)] * len(args),
        out_specs=jax.tree.map(lambda _: pl.BlockSpec(memory_space=pltpu.VMEM), out_shape),
        compiler_params=pltpu.CompilerParams(vmem_limit_bytes=VMEM_BYTES),
    )(*args)


def rows_kernel(quarter, x_far, ids_far, router_far, out, x_rows, ids, router, arrived):
    half = 2 * quarter
    loads = [
        pltpu.make_async_copy(source, target, arrived.at[i])
        for i, (source, target) in enumerate(
            ((x_far, x_rows), (router_far, router), (ids_far, ids))
        )
    ]
    for load in loads:
        load.start()
    for load in loads:
        load.wait()
    parts = [jnp.zeros((BLOCK, LANES), F32)] * EXPERTS
    for at in range(0, x_rows.shape[1], LANES):
        values = x_rows[:, at : at + LANES].astype(F32)
        for e in range(EXPERTS):
            parts[e] = parts[e] + values * router[e : e + 1, at : at + LANES]
    row, lane = grid(BLOCK, LANES)
    first, second = jnp.zeros_like(row), jnp.zeros_like(row)
    for r in range(BLOCK):
        first = jnp.where(row == r, ids[0, r], first)
        second = jnp.where(row == r, ids[1, r], second)
    squashed, total = [], 0.0
    for e in range(EXPERTS):
        logit = jnp.sum(parts[e], axis=1, keepdims=True)
        kept = jnp.where((first == e) | (second == e), jax.nn.sigmoid(logit), 0.0)
        squashed.append(kept)
        total = total + kept
    tail = jnp.zeros((BLOCK, LANES), F32)
    for e in range(EXPERTS):
        share = squashed[e] / total
        high = share.astype(BF16).astype(F32)
        low = (share - high).astype(BF16).astype(F32)
        tail = jnp.where(lane == HIGH + e, high, jnp.where(lane == LOW + e, low, tail))
    expert = fifth(lane)
    named = (first == expert) | (second == expert)
    row, column = grid(BLOCK, BLOCK)
    rank = dot(ones(row > column).astype(BF16), ones(named).astype(BF16))
    marks = ones(named & (rank == fifth_rest(lane).astype(F32)))
    tail = jnp.where(lane < EXPERTS * CAP, marks, tail)
    for f in range(2):
        at = columns(quarter, lax.axis_index("c"), f)
        out[:, f * quarter : (f + 1) * quarter] = x_rows[:, at]
    out[:, half:] = tail.astype(BF16)


def pack_kernel(quarter, *refs):
    blocks, (out, marks) = refs[:4], refs[4:]
    half = 2 * quarter
    eighth = quarter // 2
    rows = jnp.concatenate([b[:, :half] for b in blocks], axis=0)
    chosen = jnp.concatenate([b[:, half:] for b in blocks], axis=0)
    marks[...] = chosen
    lane = grid(ZLO * BLOCK, LANES)[1]
    chosen = jnp.where(lane < EXPERTS * CAP, chosen, jnp.zeros_like(chosen))
    slot, lane = grid(EXPERTS * BLOCK, LANES)
    same = fifth(lane) == slot >> 4
    pick_main = ones(same & (fifth_rest(lane) == fifth_rest(slot & 15))).astype(BF16)
    pick_rest = ones(same & (fifth_rest(lane) == 1 + (slot & 3))).astype(BF16)
    slot, row = grid(EXPERTS * BLOCK, ZLO * BLOCK)
    mask = ones(fifth(slot & 15) == row >> 4)
    main = dot((dot_t(pick_main, chosen) * mask).astype(BF16), rows)
    main = main.astype(BF16).reshape(EXPERTS // 2, 2, BLOCK, half)
    chosen4 = jnp.concatenate([chosen] * 4, axis=0)
    rows4 = jnp.concatenate([rows[:, i * eighth : (i + 1) * eighth] for i in range(4)], axis=0)
    slot, row = grid(EXPERTS * BLOCK, 4 * ZLO * BLOCK)
    mask = ones(((slot >> 2) & 3 == row >> 6) & ((row >> 4) & 3 == 3))
    rest = dot((dot_t(pick_rest, chosen4) * mask).astype(BF16), rows4)
    rest = rest.astype(BF16).reshape(EXPERTS // 2, 2, BLOCK, eighth)
    for x in range(2):
        out[:, x, :, :, :half] = main
        out[:, x, :, :, half:] = rest


def experts_in(quarter, core, block, w_gate, w_up):
    half = 2 * quarter
    rest = dot(shuffle_table(False), block[:, half:]).astype(BF16)
    gate, up = 0.0, 0.0
    for f in range(2):
        top = block[:, f * quarter : (f + 1) * quarter]
        tail = jnp.concatenate(
            [rest[(2 * f + i) * 64 : (2 * f + i + 1) * 64] for i in range(2)], axis=1
        )
        rows = jnp.concatenate([top, tail], axis=0)
        at = pl.ds(pl.multiple_of(f * half + core * quarter, LANES), quarter)
        gate = gate + dot_t(rows, w_gate[:, at])
        up = up + dot_t(rows, w_up[:, at])
    return gate, up


def columns(quarter, core, f):
    return pl.ds(pl.multiple_of(f * 2 * quarter + core * quarter, LANES), quarter)


def own_kernel(quarter, block, w_gate, w_up, gate_out, up_out):
    gate, up = experts_in(quarter, lax.axis_index("c"), block, w_gate, w_up)
    gate_out[...] = gate
    up_out[...] = up


def other_kernel(
    quarter, block, w_gate, w_up, gate_in, up_in, w_down, other_down, hidden, weights, arrived
):
    core = lax.axis_index("c")
    count = hidden.shape[1]
    loads = [
        pltpu.make_async_copy(
            source.at[:, columns(quarter, core, f)],
            weights.at[f, pl.ds(i * count, count)],
            arrived.at[f, i],
        )
        for f in range(2)
        for i, source in enumerate((w_down, other_down))
    ]
    for load in loads:
        load.start()
    gate, up = experts_in(quarter, 1 - core, block, w_gate, w_up)
    gate, up = gate + gate_in[...], up + up_in[...]
    hidden[...] = (gate * jax.nn.sigmoid(gate) * up).astype(BF16)
    for load in loads:
        load.wait()


def outer_kernel(quarter, hidden, other_hidden, weights, out):
    main = PLANE * BLOCK
    both = jnp.concatenate([hidden[...], other_hidden[...]], axis=1)
    tails = []
    for f in range(2):
        y = dot(both, weights[f]).astype(BF16)
        out[:, f * quarter : (f + 1) * quarter] = y[:main]
        tails += [y[main:, : quarter // 2], y[main:, quarter // 2 :]]
    tails = jnp.concatenate(tails, axis=0)
    out[:, 2 * quarter :] = dot(shuffle_table(True), tails).astype(BF16)


def combine_kernel(quarter, back, marks, out):
    half = 2 * quarter
    chosen = marks[...]
    lane, slot = grid(LANES, PLANE * BLOCK)
    expert = ((slot >> 6) << 1) + ((slot >> 4) & 1)
    same = fifth(lane) == expert
    back_main = ones(same & (fifth_rest(lane) == fifth_rest(slot & 15))).astype(BF16)
    back_rest = ones(same & (fifth_rest(lane) == 1 + (slot & 3))).astype(BF16)
    wide_high = dot(chosen, ones(lane == HIGH + expert).astype(BF16))
    wide_low = dot(chosen, ones(lane == LOW + expert).astype(BF16))
    row, slot = grid(ZLO * BLOCK, PLANE * BLOCK)
    main = dot(chosen, back_main) * ones(fifth(slot & 15) == row >> 4)
    rest = dot(chosen, back_rest) * ones(row >> 4 == 3)
    wides = (wide_high, wide_low)
    count = ZLO * BLOCK
    both = dot(jnp.concatenate([(main * w).astype(BF16) for w in wides], axis=0), back[:, :half])
    picked = [rest * ones((slot >> 2) & 3 == i) for i in range(4)]
    stack = jnp.concatenate([(p * w).astype(BF16) for p in picked for w in wides], axis=0)
    tails = dot(stack, back[:, half:])
    pieces = [
        tails[2 * i * count : (2 * i + 1) * count] + tails[(2 * i + 1) * count : (2 * i + 2) * count]
        for i in range(4)
    ]
    total = both[:count] + both[count:] + jnp.concatenate(pieces, axis=1)
    for k in range(ZLO):
        owner = (lax.axis_index("zl") + (REACH[k] % ZLO)) & (ZLO - 1)
        for f in range(2):
            piece = total[k * BLOCK : (k + 1) * BLOCK, f * quarter : (f + 1) * quarter]
            out[f * ZLO + owner] = piece.astype(BF16)


def attention_weights(queries, cache, lengths):
    head_dim = cache.shape[2] // 2
    heads = queries.shape[1] // head_dim
    query_heads = queries.reshape(queries.shape[0], heads, head_dim)
    scores = jnp.einsum(
        "bhd,bpd->bhp", query_heads, cache[:, :, :head_dim], preferred_element_type=F32
    ) / math.sqrt(head_dim)
    live = jnp.arange(cache.shape[1])[None, :] < lengths[:, None]
    scores = jnp.where(live[:, None, :], scores, -1e30)
    largest = jnp.max(scores, axis=2, keepdims=True)
    weights = jnp.where(live[:, None, :], jnp.exp(scores - largest), 0.0)
    return weights.astype(BF16), jnp.sum(weights, axis=2, keepdims=True)


def attention_mix(weights, denominator, cache):
    head_dim = cache.shape[2] // 2
    mixed = jnp.einsum(
        "bhp,bpd->bhd", weights, cache[:, :, head_dim:], preferred_element_type=F32
    )
    return (mixed / denominator).astype(BF16).reshape(cache.shape[0], -1)


def shards(x_rows, route_ids, router, w_gate, w_up, w_down, queries, cache, lengths):
    model_width = x_rows.shape[1]
    hidden_count = w_gate.shape[1]
    w_gate, w_up = w_gate.T, w_up.T
    quarter = model_width // 4
    half, eighth = 2 * quarter, quarter // 2
    width = half + eighth

    far = pl.BlockSpec(memory_space=pl.ANY)
    payload = pl.pallas_call(
        functools.partial(rows_kernel, quarter),
        out_shape=jax.ShapeDtypeStruct((BLOCK, half + LANES), BF16),
        in_specs=[far, far, far],
        out_specs=pl.BlockSpec(memory_space=pltpu.VMEM),
        scratch_shapes=[
            pltpu.VMEM(x_rows.shape, BF16),
            pltpu.SMEM(route_ids.T.shape, jnp.int32),
            pltpu.VMEM(router.T.shape, F32),
            pltpu.SemaphoreType.DMA((3,)),
        ],
        compiler_params=pltpu.CompilerParams(vmem_limit_bytes=ALL_VMEM_BYTES),
    )(x_rows, route_ids.T, router.T)
    blocks = [payload, z_send(payload, -1), z_send_apart(payload, -2), z_send(payload, 1)]

    payload, queries = lax.optimization_barrier((payload, queries))
    weights, denominator = attention_weights(queries, cache, lengths)
    other_down = lax.ppermute(w_down, "c", SWAP)
    blocks[0], weights, denominator, other_down = lax.optimization_barrier(
        (payload, weights, denominator, other_down)
    )
    packed, marks = call(
        functools.partial(pack_kernel, quarter),
        (
            jax.ShapeDtypeStruct((EXPERTS // 2, 2, 2, BLOCK, width), BF16),
            jax.ShapeDtypeStruct((ZLO * BLOCK, LANES), BF16),
        ),
        *blocks,
    )
    arrived = lax.all_to_all(
        packed.reshape(PLANE, BLOCK, width), PLANE_AXES, 0, 0, tiled=True
    ).reshape(PLANE * BLOCK, width)
    beside = lax.ppermute(arrived, "c", SWAP)
    rows = PLANE * (BLOCK + ZLO)
    partial = jax.ShapeDtypeStruct((rows, hidden_count), F32)
    gate, up = call(
        functools.partial(own_kernel, quarter),
        (partial, partial),
        arrived, w_gate, w_up,
    )
    gate, weights = lax.optimization_barrier((gate, weights))
    attn_out = attention_mix(weights, denominator, cache)
    gate, attn_out = lax.optimization_barrier((gate, attn_out))
    near = pl.BlockSpec(memory_space=pltpu.VMEM)
    hidden, down = pl.pallas_call(
        functools.partial(other_kernel, quarter),
        out_shape=(
            jax.ShapeDtypeStruct((rows, hidden_count), BF16),
            jax.ShapeDtypeStruct((2, 2 * hidden_count, quarter), BF16),
        ),
        in_specs=[near] * 5 + [far] * 2,
        out_specs=(near, near),
        scratch_shapes=[pltpu.SemaphoreType.DMA((2, 2))],
        compiler_params=pltpu.CompilerParams(vmem_limit_bytes=VMEM_BYTES),
    )(beside, w_gate, w_up, gate, up, w_down, other_down)
    summed = call(
        functools.partial(outer_kernel, quarter),
        jax.ShapeDtypeStruct((PLANE * BLOCK, width), BF16),
        hidden, lax.ppermute(hidden, "c", SWAP), down,
    )
    returned = lax.all_to_all(
        summed.reshape(PLANE, BLOCK, width), PLANE_AXES, 0, 0, tiled=True
    ).reshape(PLANE * BLOCK, width)

    parts = call(
        functools.partial(combine_kernel, quarter),
        jax.ShapeDtypeStruct((ZALL, BLOCK, quarter), BF16),
        returned, marks,
    )
    parts = lax.all_to_all(parts, ("zh", "zl"), 0, 0, tiled=True)
    moe_out = jnp.sum(parts.astype(F32), axis=0)
    return (moe_out.astype(BF16), attn_out)


def solution(mesh):
    fine = Mesh(mesh.devices.reshape(4, 2, 2, 4, 2, 2), ("y", "xh", "xl", "zl", "zh", "c"))
    grp, tp = ("y", "xh", "xl", "zl"), ("zh", "c")
    every = grp + tp
    return jax.shard_map(
        shards,
        mesh=fine,
        in_specs=(
            P(grp, None),
            P(grp, None),
            P(),
            P(None, every),
            P(None, every),
            P(every, None),
            P(every, None),
            P(every, None, None),
            P(every),
        ),
        out_specs=(P(grp, tp), P(every, None)),
        check_vma=False,
    )
```
